128 devices in a mesh: context: 16 (over x_hi, z, core), expert: 8 (over y, x_lo).
Axes of the slice: x: 4 (x_hi: 2, x_lo: 2; x = x_hi * 2 + x_lo), y: 4, z: 4, core: 2. Of those that a mesh axis runs over, the one named last changes fastest.
Arguments:
- tokens: bfloat16 [8, 2048, 768], P('expert', 'context'), may hold values from -6 to 6
- gain_one: float32 [768], replicated, may hold values from 0.5 to 1.5
- w_query: bfloat16 [768, 768], replicated, may hold values from -0.21875 to 0.21875
- w_key: bfloat16 [768, 768], replicated, may hold values from -0.21875 to 0.21875
- w_value: bfloat16 [768, 768], replicated, may hold values from -0.21875 to 0.21875
- w_out: bfloat16 [768, 768], replicated, may hold values from -1.75 to 1.75
- rel_table: float32 [12, 32], replicated, may hold values from -4 to 4
- gain_two: float32 [768], replicated, may hold values from 0.5 to 1.5
- w_router: bfloat16 [768, 8], replicated, may hold values from -0.15625 to 0.15625
- expert_in: bfloat16 [8, 768, 3072], P('expert', None, 'context'), may hold values from -0.21875 to 0.21875
- expert_out: bfloat16 [8, 768, 3072], P('expert', None, 'context'), may hold values from -0.109375 to 0.109375
- routes: int32 [8, 2048, 2], P('expert', 'context'), may hold values from 0 to 7, all different within a row; in each aligned block of 128 rows (0 to 127, 128 to 255, ..., all dimensions but the last counted through in order) at most 48 rows name the same one
- cotangent: bfloat16 [8, 2048, 768], P('expert', 'context'), may hold values from -6 to 6
Outputs:
- block_out: bfloat16 [8, 2048, 768], P('expert', 'context')
- grad_tokens: float32 [8, 2048, 768], P('expert', 'context')
- grad_gain_one: float32 [768], replicated
- grad_query: float32 [768, 768], replicated
- grad_key: float32 [768, 768], replicated
- grad_value: float32 [768, 768], replicated
- grad_w_out: float32 [768, 768], replicated
- grad_rel_table: float32 [12, 32], replicated
- grad_gain_two: float32 [768], replicated
- grad_router: float32 [768, 8], replicated
- grad_expert_in: float32 [8, 768, 3072], P('expert', None, 'context')
- grad_expert_out: float32 [8, 768, 3072], P('expert', None, 'context')
The draws below stay inside these ranges and needn't reach their ends.
Inputs may be any that keep to these rules, and one draw needn't show every extreme that they name: `routes`: A token's two experts differ. Within the rows of one device (aligned blocks of 128 rows of the flattened sequences and positions) no expert is named by more than 48 tokens, and in every draw some block has an expert named exactly 48 times.
All inputs are finite; a program needn't handle non-finite values.
Results may differ from the reference program's by a relative error of at most 0.022.
Values may be sent and summed in bfloat16 or wider, within the bound.
No kernel may reach another device: no remote copies, remote signals or barrier semaphores. Data moves between devices by JAX's collectives and lax.ppermute only.
A program may use at most 128 MiB of HBM per device.

```python
import math
import jax
import jax.numpy as jnp
import numpy as np
from jax import lax

D = 768
HEADS = 12
HEAD_DIM = 64
FF = 3072
BUCKETS = 32
MAX_DIST = 128
TOK_DEV = 128
EXPERTS = 8
SEQS = 8
LEN = 2048
CAP = 48
N_CONTEXT = 16


def steps_of(key, extent, split, least, top_value):
    def one(dim, parts):
        heights = jax.random.uniform(jax.random.fold_in(jax.random.fold_in(key, 6), dim), (parts,), jnp.float32, least / len(split), top_value / len(split))
        return jnp.repeat(jnp.exp(heights), extent[dim] // parts).reshape((-1,) + (1,) * (len(extent) - dim - 1))

    level = one(*split[0])
    for cut in split[1:]:
        level = level * one(*cut)
    return level


def routed_block(own_key, own, number, rows, count, top, reach, slope):
    order = jax.random.permutation(own_key, count)
    packed, usual = portions_of(count, rows * top, reach, slope, True), portions_of(count, rows * top, reach, slope, False)
    places = jnp.arange(count)

    def named(sizes, offset_by):
        used = int((sizes > 0).sum())
        fixed = max(1, used // 4)
        moved = fixed + (places - fixed + offset_by * (used - fixed)) % max(1, count - fixed)
        return jnp.zeros((count,), jnp.int32).at[order[jnp.where(places < fixed, places, moved)]].set(jnp.asarray(sizes, jnp.int32))

    sizes = jnp.where(number % 4 == 0, named(packed, number // 4), named(usual, number - number // 4 - 1))
    mixed = jax.random.permutation(jax.random.fold_in(own, 3), count)
    giver, receiver = mixed[0:count // 2 * 2:2], mixed[1:count // 2 * 2:2]
    slack = jnp.minimum(sizes[giver] - 1, reach - sizes[receiver]) // 2
    slack = jnp.where((giver == order[0]) | (receiver == order[0]) | (sizes[receiver] == 0), 0, jnp.maximum(slack, 0))
    moved = jax.random.randint(jax.random.fold_in(own, 4), (count // 2,), 0, 1 << 20) % (slack + 1)
    sizes = sizes.at[giver].add(-moved).at[receiver].add(moved)
    members = jnp.searchsorted(jnp.cumsum(sizes), jnp.arange(rows * top), side="right").astype(jnp.int32)
    grid = members.reshape(top, rows).T
    grid = grid[jax.random.permutation(jax.random.fold_in(own, 1), rows)]
    offset_by = jax.random.randint(jax.random.fold_in(own, 2), (rows, 1), 0, top)
    return jnp.take_along_axis(grid, (jnp.arange(top)[None, :] + offset_by) % top, axis=1)


def portions_of(count, total, bound, lean, full):
    loads = [(1 << 20) // math.isqrt(grade ** lean) + 1 for grade in range(1, count + 1)]
    largest = bound if full else min(bound, max(-(-total // count), total * loads[0] // sum(loads)))
    least = 1 if total - largest >= count - 1 else 0
    counts, rest = [largest] + [least] * (count - 1), total - largest - least * (count - 1)
    while rest > 0:
        free = [i for i in range(1, count) if counts[i] < largest] or [i for i in range(1, count) if counts[i] < bound]
        mass, budget = sum([loads[i] for i in free]), rest
        for i in free:
            addition = min(bound - counts[i], max(1, budget * loads[i] // mass), rest)
            counts[i] = counts[i] + addition
            rest = rest - addition
    return np.array(counts)


def bell_draw(own_key, dims, spread, most, cuts=(), held_as=jnp.bfloat16):
    array = spread * jax.random.normal(own_key, dims, jnp.float32)
    if cuts:
        array = array * steps_of(own_key, dims, cuts, -0.22, 0.18)
    return jnp.clip(array, -most, most).astype(held_as)


def setup_inputs(seed: int = 0) -> dict:
    splits = jax.random.split(jax.random.key(seed), 14)
    tokens = bell_draw(splits[0], (SEQS, LEN, D), 1.0, 6.0, ((0, 8), (1, 16)))
    gain_one = jnp.clip(1.0 + 0.1 * jax.random.normal(splits[1], (D,), jnp.float32), 0.5, 1.5)
    w_query = bell_draw(splits[2], (D, D), D ** -0.5, 0.21875)
    w_key = bell_draw(splits[3], (D, D), D ** -0.5, 0.21875)
    w_value = bell_draw(splits[4], (D, D), D ** -0.5, 0.21875)
    w_out = bell_draw(splits[5], (D, D), (D // 64) ** -0.5, 1.75)
    rel_table = bell_draw(splits[6], (HEADS, BUCKETS), 1.0, 4.0, (), jnp.float32)
    gain_two = jnp.clip(1.0 + 0.1 * jax.random.normal(splits[7], (D,), jnp.float32), 0.5, 1.5)
    w_router = bell_draw(splits[8], (D, EXPERTS), (2 * D) ** -0.5, 0.15625)
    expert_in = bell_draw(splits[9], (EXPERTS, D, FF), D ** -0.5, 0.21875, ((0, 8), (2, 16)))
    expert_out = bell_draw(splits[10], (EXPERTS, D, FF), FF ** -0.5, 0.109375, ((0, 8), (2, 16)))
    routes_keys = jax.random.split(jax.random.fold_in(splits[11], 1), SEQS * LEN // TOK_DEV)
    routes_turns = jax.random.permutation(jax.random.fold_in(splits[11], 3), SEQS * LEN // TOK_DEV)
    routes = jax.vmap(lambda own, number: routed_block(jax.random.fold_in(splits[11], 2), own, number, TOK_DEV, EXPERTS, 2, CAP, 2))(routes_keys, routes_turns).reshape((SEQS, LEN, 2))
    cotangent = bell_draw(splits[12], (SEQS, LEN, D), 1.0, 6.0, ((0, 8), (1, 16)))
    return dict(tokens=tokens, gain_one=gain_one, w_query=w_query, w_key=w_key, w_value=w_value, w_out=w_out, rel_table=rel_table, gain_two=gain_two, w_router=w_router, expert_in=expert_in, expert_out=expert_out, routes=routes, cotangent=cotangent)


@jax.custom_vjp
def low(v):
    return lax.optimization_barrier(v.astype(jnp.bfloat16)).astype(jnp.float32)

@jax.custom_vjp
def low_back(v):
    return v

def low_keep(v):
    return (low(v), None)

def low_pass(kept, grad):
    return (grad,)

def back_keep(v):
    return (v, None)

def back_low(kept, grad):
    return (low(grad),)
low.defvjp(low_keep, low_pass)
low_back.defvjp(back_keep, back_low)
EPSILON = 1e-06
HIGHEST = lax.Precision.HIGHEST
NEG_LARGE = -1e+30

def gelu_tanh(values):
    return 0.5 * values * (1.0 + jnp.tanh(0.7978845608 * (values + 0.044715 * values * values * values)))

def relative_bucket(distance, buckets, far_reach):
    exact_span = buckets // 2
    near_dist = jnp.maximum(distance, 0)
    result = jnp.full(near_dist.shape, exact_span, jnp.int32)
    for level_step in range(1, buckets - exact_span):
        threshold = int(math.ceil(exact_span * (far_reach / exact_span) ** (level_step / (buckets - exact_span))))
        result = result + (near_dist >= threshold).astype(jnp.int32)
    return jnp.where(near_dist < exact_span, near_dist, result).astype(jnp.int32)

def rms_scale(values):
    return lax.rsqrt(lax.optimization_barrier(jnp.mean(values * values, axis=-1, keepdims=True)) + EPSILON)

def slot_numbers(route_block, experts_count):
    pair_expert = route_block.reshape(-1).astype(jnp.int32)
    onehot = (pair_expert[:, None] == jnp.arange(experts_count, dtype=jnp.int32)[None, :]).astype(jnp.int32)
    ranks = (jnp.cumsum(onehot, axis=0) - onehot).astype(jnp.int32)
    return (pair_expert, lax.optimization_barrier(jnp.sum(ranks * onehot, axis=1)).astype(jnp.int32))

def attend_block(query_blk, key_seq, value_seq, bias_table, first_row):
    score_scale = HEAD_DIM ** (-0.5)
    raw_scores = jnp.einsum('qhd,khd->hqk', query_blk, key_seq, precision=HIGHEST) * score_scale
    query_pos = first_row + jnp.arange(query_blk.shape[0], dtype=jnp.int32)
    key_pos = jnp.arange(key_seq.shape[0], dtype=jnp.int32)
    distance = query_pos[:, None] - key_pos[None, :]
    bias_terms = jnp.take(bias_table, relative_bucket(distance, BUCKETS, MAX_DIST), axis=1)
    scores = low_back(raw_scores + bias_terms)
    scores = jnp.where(distance[None] >= 0, scores, NEG_LARGE)
    top_score = lax.optimization_barrier(jnp.max(scores, axis=2, keepdims=True))
    expos = jnp.exp(scores - top_score)
    probabilities = low(expos / lax.optimization_barrier(jnp.sum(expos, axis=2, keepdims=True)))
    return jnp.einsum('hqk,khd->qhd', probabilities, value_seq, precision=HIGHEST)

def attend_sequence(query_seq, key_seq, value_seq, bias_table):
    block_rows = min(512, LEN)
    block_count = LEN // block_rows
    query_blocks = query_seq.reshape(block_count, block_rows, HEADS, HEAD_DIM)
    starts = jnp.arange(block_count, dtype=jnp.int32) * block_rows

    def one_block(block_item):
        return attend_block(block_item[0], key_seq, value_seq, bias_table, block_item[1])
    outputs = lax.map(jax.checkpoint(one_block), (query_blocks, starts))
    return outputs.reshape(LEN, D)

def expert_rows(block_item):
    weight_in, weight_out, slot_rows = block_item
    pre_act = low_back(jnp.dot(slot_rows, weight_in, precision=HIGHEST))
    act_low = low(gelu_tanh(pre_act))
    produced = jnp.dot(act_low, weight_out.T, precision=HIGHEST)
    return low_back(low(produced))

def reference(tokens, gain_one, w_query, w_key, w_value, w_out, rel_table, gain_two, w_router, expert_in, expert_out, routes, cotangent):
    block_total = SEQS * N_CONTEXT
    pair_total = 2 * SEQS * LEN
    route_blocks = routes.reshape(block_total, TOK_DEV, 2)
    pair_expert, slots = jax.vmap(lambda block_item: slot_numbers(block_item, EXPERTS))(route_blocks)
    block_index = jnp.arange(block_total, dtype=jnp.int32)[:, None]
    destination = (pair_expert * (block_total * CAP) + block_index * CAP + slots).reshape(-1).astype(jnp.int32)
    source_pair = jnp.full((EXPERTS * block_total * CAP,), pair_total, jnp.int32).at[destination].set(jnp.arange(pair_total, dtype=jnp.int32))
    source_token = (source_pair // 2).astype(jnp.int32)
    routes_flat = routes.reshape(-1, 2).astype(jnp.int32)

    def layer_forward(inputs, gain_a, query_w, key_w, value_w, out_w, bias_table, gain_b, router_w, first_w, second_w):
        flat_tokens = inputs.reshape(SEQS * LEN, D)
        normed = low(flat_tokens * rms_scale(flat_tokens) * gain_a)

        def project(weight):
            return low_back(low(jnp.dot(normed, weight, precision=HIGHEST))).reshape(SEQS, LEN, HEADS, HEAD_DIM)
        queries = project(query_w)
        keys = project(key_w)
        values = project(value_w)
        attended = lax.map(lambda block_item: attend_sequence(block_item[0], block_item[1], block_item[2], bias_table), (queries, keys, values))
        attended = low_back(low(attended.reshape(SEQS * LEN, D)))
        mixed_sum = flat_tokens + low_back(jnp.dot(attended, out_w, precision=HIGHEST))
        second = low(mixed_sum * rms_scale(mixed_sum) * gain_b)
        logits = jnp.dot(second, router_w, precision=HIGHEST)
        chosen = jnp.take_along_axis(logits, routes_flat, axis=1)
        chosen_top = lax.optimization_barrier(jnp.max(chosen, axis=1, keepdims=True))
        chosen_exp = jnp.exp(chosen - chosen_top)
        gate_probs = chosen_exp / lax.optimization_barrier(jnp.sum(chosen_exp, axis=1, keepdims=True))
        padded = jnp.concatenate([second, jnp.zeros((1, D), second.dtype)], axis=0)
        slot_rows = low_back(padded[source_token]).reshape(EXPERTS, block_total * CAP, D)
        produced = lax.map(jax.checkpoint(expert_rows), (first_w, second_w, slot_rows))
        produced = produced.reshape(EXPERTS * block_total * CAP, D)
        picked = produced[destination].reshape(SEQS * LEN, 2, D)
        result = mixed_sum + lax.optimization_barrier(jnp.sum(gate_probs[:, :, None] * picked, axis=1))
        return result.reshape(SEQS, LEN, D)
    floats = (tokens, gain_one, w_query, w_key, w_value, w_out, rel_table, gain_two, w_router, expert_in, expert_out)
    floats = tuple((entry.astype(jnp.float32) for entry in floats))
    primal, pullback = jax.vjp(layer_forward, *floats)
    gradients = pullback(cotangent.astype(jnp.float32))
    return (primal.astype(jnp.bfloat16), gradients[0], gradients[1], gradients[2], gradients[3], gradients[4], gradients[5], gradients[6], gradients[7], gradients[8], gradients[9], gradients[10])
```

```python
import math

import jax
import jax.numpy as jnp
from jax import lax
from jax.experimental import pallas as pl
from jax.experimental.pallas import tpu as pltpu
from jax.sharding import PartitionSpec as P

MAX_DIST = 128
EPSILON = 1e-06
NEG_LARGE = -1e30
BLK = 256
HEAD_SLOTS = 16

F32 = jnp.float32
BF16 = jnp.bfloat16
HIGHEST = lax.Precision.HIGHEST

NN = (((1,), (0,)), ((), ()))
NT = (((1,), (1,)), ((), ()))
TN = (((0,), (0,)), ((), ()))


def dot(a, b, dims=NN, precision=None):
    return lax.dot_general(a, b, dims, precision=precision, preferred_element_type=F32)


def bucket_starts(buckets, far_reach):
    span = buckets // 2
    rest = [
        int(math.ceil(span * (far_reach / span) ** (step / (buckets - span))))
        for step in range(1, buckets - span)
    ]
    return list(range(span + 1)) + rest


def rms_scale(values):
    return lax.rsqrt(jnp.mean(values * values, axis=-1, keepdims=True) + EPSILON)


def norm_back(values, inv_root, gain_vec, grad_normed):
    weighted = grad_normed * gain_vec
    cubed = inv_root * inv_root * inv_root
    return inv_root * weighted - values * cubed * jnp.mean(
        weighted * values, axis=-1, keepdims=True
    )


def whole(vmem_mib=56):
    return pltpu.CompilerParams(vmem_limit_bytes=vmem_mib * 2**20)


def vspec():
    return pl.BlockSpec(memory_space=pltpu.VMEM)


def sspec():
    return pl.BlockSpec(memory_space=pltpu.SMEM)


def project_kernel(tok_ref, gain_ref, wq_ref, wk_ref, wv_ref, normed_ref, out_ref):
    inputs = tok_ref[...].astype(F32)
    normed = (inputs * rms_scale(inputs) * gain_ref[...]).astype(BF16)
    normed_ref[...] = normed
    half = normed.shape[0] // 2
    queries = (dot(normed, wq_ref[...]).astype(BF16).astype(F32) * 0.125).astype(BF16)
    keys = dot(normed, wk_ref[...]).astype(BF16)
    values = dot(normed, wv_ref[...]).astype(BF16)
    heads = queries.shape[1] // 64
    for h in range(heads):
        cols = slice(64 * h, 64 * h + 64)
        out_ref[h, : 2 * half, :] = jnp.concatenate([queries[:, cols], keys[:, cols]], axis=1)
        out_ref[h, 2 * half :, :] = jnp.concatenate(
            [values[:half, cols], values[half:, cols]], axis=1
        )
    for h in range(heads, HEAD_SLOTS):
        out_ref[h] = jnp.zeros_like(out_ref[h])


def project(tokens, gain_one, w_query, w_key, w_value):
    rows, width = tokens.shape
    return pl.pallas_call(
        project_kernel,
        name="project",
        out_shape=(
            jax.ShapeDtypeStruct((rows, width), BF16),
            jax.ShapeDtypeStruct((HEAD_SLOTS, rows + rows // 2, 128), BF16),
        ),
        in_specs=[vspec()] * 5,
        out_specs=(vspec(), vspec()),
        compiler_params=whole(),
    )(tokens, gain_one.reshape(1, width), w_query, w_key, w_value)


def bias_tile(table_ref, head, buckets, rows_first, shape, key_dim):
    sign = [1, -1] if key_dim == 1 else [-1, 1]
    dist = (
        rows_first
        + sign[0] * lax.broadcasted_iota(jnp.int32, shape, 0)
        + sign[1] * lax.broadcasted_iota(jnp.int32, shape, 1)
    )
    far = table_ref[head, buckets - 1]
    tile = jnp.full(shape, NEG_LARGE, F32)
    for b, start in enumerate(bucket_starts(buckets, MAX_DIST)):
        tile = jnp.where(dist >= start, table_ref[head, b] - far, tile)
    return tile


def unpack_qkv(qkv_ref, q_s, k_s, v_s, ones_lane):
    count = qkv_ref.shape[0]
    lane = lax.broadcasted_iota(jnp.int32, (64, 64), 1)
    one = jnp.where(lane == 0, 1.0, 0.0).astype(BF16)
    for c in range(count):
        pair = qkv_ref[c, :128, :]
        q_s[128 * c : 128 * c + 128, :] = pair[:, :64]
        k_s[128 * c : 128 * c + 128, :] = pair[:, 64:]
        two = qkv_ref[c, 128:192, :]
        top, bottom = two[:, :64], two[:, 64:]
        if ones_lane:
            top = jnp.concatenate([top, one], axis=1)
            bottom = jnp.concatenate([bottom, one], axis=1)
        v_s[128 * c : 128 * c + 64, :] = top
        v_s[128 * c + 64 : 128 * c + 128, :] = bottom


def attend_kernel(buckets, head_ref, table_ref, qkv_ref, out_ref, keep_ref, lse_ref, q_s, k_s, v_s, bias_s, s_s):
    head = head_ref[0]
    unpack_qkv(qkv_ref, q_s, k_s, v_s, True)
    bias_s[0] = bias_tile(table_ref, head, buckets, BLK, (BLK, BLK), 1)
    bias_s[1] = bias_tile(table_ref, head, buckets, 0, (BLK, BLK), 1)
    blocks = q_s.shape[0] // BLK

    def fold(scores):
        return jnp.maximum(scores[:, :128], scores[:, 128:])

    def one_query(qb, unused):
        rows = pl.ds(pl.multiple_of(qb * BLK, BLK), BLK)
        query = q_s[rows, :]

        def score(kb):
            return dot(query, k_s[pl.ds(pl.multiple_of(kb * BLK, BLK), BLK), :], NT)

        def far(kb, top):
            scores = score(kb)
            s_s[kb] = scores
            return jnp.maximum(top, fold(scores))

        top = lax.fori_loop(0, qb - 1, far, jnp.full((BLK, 128), NEG_LARGE, F32))
        before = jnp.maximum(qb - 1, 0)
        scores = jnp.where(qb > 0, score(before) + bias_s[0], NEG_LARGE)
        s_s[before] = scores
        top = jnp.maximum(top, fold(scores))
        scores = score(qb) + bias_s[1]
        s_s[qb] = scores
        top = jnp.max(jnp.maximum(top, fold(scores)), axis=1, keepdims=True)

        def weigh(kb, total):
            weights = jnp.exp(s_s[kb] - top).astype(BF16)
            return total + dot(weights, v_s[pl.ds(pl.multiple_of(kb * BLK, BLK), BLK), :])

        total = lax.fori_loop(0, qb + 1, weigh, jnp.zeros((BLK, 128), F32))
        norm = total[:, 64:65]
        out = total[:, :64] / norm
        log_total = top + jnp.log(norm)
        spread = jnp.broadcast_to(log_total, (BLK, 128)).T
        lse_ref[qb] = spread[:8, :]
        for part in range(BLK // 128):
            two = jnp.concatenate(
                [out[128 * part : 128 * part + 64], out[128 * part + 64 : 128 * part + 128]], axis=1
            )
            place = qb * (BLK // 128) + part
            out_ref[place] = two.astype(BF16)
            keep_ref[place] = two
        return unused

    lax.fori_loop(0, blocks, one_query, 0)


def attend(head, rel_table, qkv):
    count = qkv.shape[0]
    length = 128 * count
    blocks = length // BLK
    return pl.pallas_call(
        lambda *refs: attend_kernel(rel_table.shape[1], *refs),
        name="attend",
        out_shape=(
            jax.ShapeDtypeStruct((count, 64, 128), BF16),
            jax.ShapeDtypeStruct((count, 64, 128), F32),
            jax.ShapeDtypeStruct((blocks, 8, BLK), F32),
        ),
        in_specs=[sspec(), sspec(), vspec()],
        out_specs=(vspec(), vspec(), vspec()),
        scratch_shapes=[
            pltpu.VMEM((length, 64), BF16),
            pltpu.VMEM((length, 64), BF16),
            pltpu.VMEM((length, 128), BF16),
            pltpu.VMEM((2, BLK, BLK), F32),
            pltpu.VMEM((blocks, BLK, BLK), F32),
        ],
        compiler_params=whole(),
    )(head, rel_table, qkv)


def attend_back_kernel(
    buckets,
    head_ref,
    table_ref,
    qkv_ref,
    go_ref,
    keep_ref,
    lse_ref,
    normed_ref,
    dqkv_ref,
    dw_ref,
    q_s,
    k_s,
    v_s,
    kt_s,
    go_s,
    delta_s,
    dq_s,
    dk_s,
    dv_s,
    bias_s,
    acc_s,
    low_s,
):
    head = head_ref[0]
    length = q_s.shape[0]
    count = qkv_ref.shape[0]
    blocks = length // BLK
    unpack_qkv(qkv_ref, q_s, k_s, v_s, False)
    ones = jnp.ones((8, 64), F32)
    for c in range(count):
        kt_s[:, 128 * c : 128 * c + 128] = k_s[128 * c : 128 * c + 128, :].T
        two, kept = go_ref[c], keep_ref[c]
        go_s[128 * c : 128 * c + 64, :] = two[:, :64]
        go_s[128 * c + 64 : 128 * c + 128, :] = two[:, 64:]
        both = two.astype(F32) * kept
        prod = jnp.concatenate([both[:, :64], both[:, 64:]], axis=0)
        delta_s[:, 128 * c : 128 * c + 128] = dot(ones, prod, NT, HIGHEST)
    bias_s[0] = bias_tile(table_ref, head, buckets, BLK, (BLK, BLK), 0)
    bias_s[1] = bias_tile(table_ref, head, buckets, 0, (BLK, BLK), 0)
    acc_s[...] = jnp.zeros_like(acc_s)
    dk_s[...] = jnp.zeros_like(dk_s)
    dv_s[...] = jnp.zeros_like(dv_s)

    def one_query(qb, far_sum):
        rows = pl.ds(pl.multiple_of(qb * BLK, BLK), BLK)
        query, grad = q_s[rows, :], go_s[rows, :]
        lse = lse_ref[qb][:1, :]
        delta = delta_s[:1, rows]

        def block(kb, near, grad_query, far_sum):
            cols = pl.ds(pl.multiple_of(kb * BLK, BLK), BLK)
            scores = dot(k_s[cols, :], query, NT)
            if near is not None:
                scores = scores + bias_s[near]
            probs = jnp.exp(scores - lse)
            grad_probs = dot(v_s[cols, :], grad, NT)
            grad_scores = (probs * (grad_probs - delta)).astype(BF16)
            dv_s[cols, :] += dot(probs.astype(BF16), grad)
            dk_s[cols, :] += dot(grad_scores, query)
            grad_query = grad_query + dot(kt_s[:, cols], grad_scores)
            wide = grad_scores.astype(F32)
            if near is None:
                far_sum = far_sum + jnp.sum(wide.reshape(BLK // 8, 8, BLK), axis=0)
            else:
                acc_s[near] += wide
            return grad_query, far_sum

        start = (jnp.zeros((64, BLK), F32), far_sum)
        grad_query, far_sum = lax.fori_loop(
            0, qb - 1, lambda kb, state: block(kb, None, *state), start
        )
        dq_s[:, rows] = grad_query

        @pl.when(qb > 0)
        def _():
            more, unused = block(qb - 1, 0, jnp.zeros((64, BLK), F32), None)
            dq_s[:, rows] += more

        more, unused = block(qb, 1, jnp.zeros((64, BLK), F32), None)
        dq_s[:, rows] += more
        return far_sum

    far_sum = lax.fori_loop(0, blocks, one_query, jnp.zeros((8, BLK), F32))

    for c in range(count):
        here = slice(128 * c, 128 * c + 128)
        dq_t = (dq_s[:, here] * 0.125).astype(BF16)
        dk = dk_s[here, :].astype(BF16)
        dv = dv_s[here, :].astype(BF16)
        pair = jnp.concatenate([dq_t.T, dk], axis=1)
        dqkv_ref[c, :128, :] = pair
        dqkv_ref[c, 128:192, :] = jnp.concatenate([dv[:64], dv[64:]], axis=1)
        low_s[:128, here] = pair.T
        low_s[128:192, here] = dv.T

    width = normed_ref.shape[1]
    grads = dot(low_s[...], normed_ref[...])
    pair, third = grads[:128].T, grads[128:192].T
    shares = dw_ref.shape[0]
    each = width // shares
    lane = lax.broadcasted_iota(jnp.int32, (16, 128), 1)
    dist0 = (
        BLK
        - lax.broadcasted_iota(jnp.int32, (BLK, BLK), 0)
        + lax.broadcasted_iota(jnp.int32, (BLK, BLK), 1)
    )
    dist1 = dist0 - BLK

    def total(values):
        return jnp.sum(jnp.sum(values, axis=1, keepdims=True), axis=0, keepdims=True)

    starts = bucket_starts(buckets, MAX_DIST)
    row = jnp.zeros((16, 128), F32)
    above = None
    for b in reversed(range(buckets)):
        reach = total(
            jnp.where(dist0 >= starts[b], acc_s[0], 0.0)
            + jnp.where(dist1 >= starts[b], acc_s[1], 0.0)
        )
        mine = reach + total(far_sum) if b == buckets - 1 else reach - above
        above = reach
        row = jnp.where(lane == b, mine, row)
    row = row.astype(BF16)
    for s in range(shares):
        mine = slice(each * s, each * s + each)
        dw_ref[s, :each, :] = pair[mine].astype(BF16)
        last = third[mine].astype(BF16)
        dw_ref[s, each : each + each // 2, :] = jnp.concatenate(
            [last[: each // 2], last[each // 2 :]], axis=1
        )
        dw_ref[s, each + each // 2 :, :] = row


def attend_back(head, rel_table, qkv, grad_heads, keep, lse, normed_all, shares):
    count = qkv.shape[0]
    length = 128 * count
    width = normed_all.shape[1]
    each = width // shares
    return pl.pallas_call(
        lambda *refs: attend_back_kernel(rel_table.shape[1], *refs),
        name="attend_back",
        out_shape=(
            jax.ShapeDtypeStruct(qkv.shape, BF16),
            jax.ShapeDtypeStruct((shares, each + each // 2 + 16, 128), BF16),
        ),
        in_specs=[sspec(), sspec()] + [vspec()] * 5,
        out_specs=(vspec(), vspec()),
        scratch_shapes=[
            pltpu.VMEM((length, 64), BF16),
            pltpu.VMEM((length, 64), BF16),
            pltpu.VMEM((length, 64), BF16),
            pltpu.VMEM((64, length), BF16),
            pltpu.VMEM((length, 64), BF16),
            pltpu.VMEM((8, length), F32),
            pltpu.VMEM((64, length), F32),
            pltpu.VMEM((length, 64), F32),
            pltpu.VMEM((length, 64), F32),
            pltpu.VMEM((2, BLK, BLK), F32),
            pltpu.VMEM((2, BLK, BLK), F32),
            pltpu.VMEM((192, length), BF16),
        ],
        compiler_params=whole(),
    )(head, rel_table, qkv, grad_heads, keep, lse, normed_all)


def heads_to_rows(ref, scratch):
    for j in range(scratch.shape[1] // 128):
        one, two = ref[2 * j], ref[2 * j + 1]
        scratch[:64, 128 * j : 128 * j + 128] = jnp.concatenate([one[:, :64], two[:, :64]], axis=1)
        scratch[64:, 128 * j : 128 * j + 128] = jnp.concatenate([one[:, 64:], two[:, 64:]], axis=1)


def dispatch_kernel(
    experts,
    capacity,
    tok_ref,
    cot_ref,
    heads_ref,
    wo_ref,
    gain_ref,
    wr_ref,
    routes_ref,
    send_ref,
    att_ref,
    mixed_ref,
    second_ref,
    pick_ref,
    gates_ref,
):
    rows = tok_ref.shape[0]
    heads_to_rows(heads_ref, att_ref)
    mixed = tok_ref[...].astype(F32) + dot(att_ref[...], wo_ref[...])
    mixed_ref[...] = mixed
    second = (mixed * rms_scale(mixed) * gain_ref[...]).astype(BF16)
    second_ref[...] = second
    logits = dot(second, wr_ref[...])
    ids = lax.broadcasted_iota(jnp.int32, (rows, experts), 1)
    routes = routes_ref[...]
    marks = [(routes[:, k : k + 1] == ids).astype(F32) for k in range(2)]
    earlier = (
        lax.broadcasted_iota(jnp.int32, (rows, rows), 0)
        > lax.broadcasted_iota(jnp.int32, (rows, rows), 1)
    ).astype(F32)
    ranks = dot(earlier.astype(BF16), (marks[0] + marks[1]).astype(BF16))
    chosen = [jnp.sum(m * logits, axis=1, keepdims=True) for m in marks]
    top = jnp.maximum(chosen[0], chosen[1])
    exps = [jnp.exp(c - top) for c in chosen]
    gates = [e / (exps[0] + exps[1]) for e in exps]
    slot_ids = lax.broadcasted_iota(jnp.int32, (rows, experts * capacity), 1)
    grad_out = cot_ref[...].astype(F32)
    picks = []
    for k in range(2):
        slot = jnp.sum(marks[k] * ranks, axis=1, keepdims=True).astype(jnp.int32)
        place = routes[:, k : k + 1] * capacity + slot
        picks.append((place == slot_ids).astype(F32).astype(BF16))
        pick_ref[k] = picks[k]
    send_rows = dot(picks[0] + picks[1], second, TN).astype(BF16)
    send_grads = dot(picks[0], (gates[0] * grad_out).astype(BF16), TN) + dot(
        picks[1], (gates[1] * grad_out).astype(BF16), TN
    )
    send_grads = send_grads.astype(BF16)
    for e in range(experts):
        here = slice(capacity * e, capacity * e + capacity)
        send_ref[e, :capacity, :] = send_rows[here]
        send_ref[e, capacity:, :] = send_grads[here]
    lane = lax.broadcasted_iota(jnp.int32, (rows, 128), 1)
    gates_ref[...] = jnp.where(lane == 0, gates[0], gates[1])


def dispatch(tokens, cotangent, heads, w_out, gain_two, w_router, routes, experts):
    rows, width = tokens.shape
    capacity = 3 * rows // experts
    return pl.pallas_call(
        lambda *refs: dispatch_kernel(experts, capacity, *refs),
        name="dispatch",
        out_shape=(
            jax.ShapeDtypeStruct((experts, 2 * capacity, width), BF16),
            jax.ShapeDtypeStruct((rows, width), BF16),
            jax.ShapeDtypeStruct((rows, width), F32),
            jax.ShapeDtypeStruct((rows, width), BF16),
            jax.ShapeDtypeStruct((2, rows, experts * capacity), BF16),
            jax.ShapeDtypeStruct((rows, 128), F32),
        ),
        in_specs=[vspec()] * 7,
        out_specs=(vspec(),) * 6,
        compiler_params=whole(),
    )(tokens, cotangent, heads, w_out, gain_two.reshape(1, width), w_router, routes)


def expert_kernel(rows_ref, w_ref, back_ref, dw_ref, x_s, g_s, y_s, dx_s):
    step = pl.program_id(0)
    sources, both, width = rows_ref.shape
    capacity = both // 2

    @pl.when(step == 0)
    def _():
        for s in range(sources):
            x_s[capacity * s : capacity * s + capacity, :] = rows_ref[s, :capacity, :]
            g_s[capacity * s : capacity * s + capacity, :] = rows_ref[s, capacity:, :]
        y_s[...] = jnp.zeros_like(y_s)
        dx_s[...] = jnp.zeros_like(dx_s)

    w_in, w_back = w_ref[:, :width], w_ref[:, width:]
    pre = dot(x_s[...], w_in, NT)
    square = pre * pre
    curve = jnp.tanh(0.7978845608 * (pre + 0.044715 * square * pre))
    act = (0.5 * pre * (1.0 + curve)).astype(BF16)
    slope = 0.5 * (1.0 + curve) + 0.5 * pre * (1.0 - curve * curve) * (
        0.7978845608 * (1.0 + 3.0 * 0.044715 * square)
    )
    grad_pre = (dot(g_s[...], w_back, NT) * slope).astype(BF16)
    y_s[...] += dot(act, w_back)
    dx_s[...] += dot(grad_pre, w_in)
    dw_ref[:, :width] = dot(grad_pre, x_s[...], TN).astype(BF16)
    dw_ref[:, width:] = dot(act, g_s[...], TN).astype(BF16)

    @pl.when(step == pl.num_programs(0) - 1)
    def _():
        for s in range(sources):
            here = slice(capacity * s, capacity * s + capacity)
            back_ref[s, :capacity, :] = y_s[here, :].astype(BF16)
            back_ref[s, capacity:, :] = dx_s[here, :].astype(BF16)


def expert_both(rows, weights):
    sources, both, width = rows.shape
    hidden = weights.shape[0]
    chunk = 512
    held = sources * both // 2
    return pl.pallas_call(
        expert_kernel,
        name="expert_both",
        grid=(hidden // chunk,),
        out_shape=(
            jax.ShapeDtypeStruct(rows.shape, BF16),
            jax.ShapeDtypeStruct(weights.shape, BF16),
        ),
        in_specs=[
            pl.BlockSpec(rows.shape, lambda i: (0, 0, 0)),
            pl.BlockSpec((chunk, 2 * width), lambda i: (i, 0)),
        ],
        out_specs=(
            pl.BlockSpec(rows.shape, lambda i: (0, 0, 0)),
            pl.BlockSpec((chunk, 2 * width), lambda i: (i, 0)),
        ),
        scratch_shapes=[
            pltpu.VMEM((held, width), BF16),
            pltpu.VMEM((held, width), BF16),
            pltpu.VMEM((held, width), F32),
            pltpu.VMEM((held, width), F32),
        ],
        compiler_params=whole(),
    )(rows, weights)


def combine_kernel(
    cot_ref,
    back_ref,
    pick_ref,
    gates_ref,
    mixed_ref,
    second_ref,
    att_ref,
    routes_ref,
    gain_ref,
    wr_ref,
    wo_ref,
    out_ref,
    grad_mixed_ref,
    heads_ref,
    sums_ref,
    y_s,
    dx_s,
):
    experts, both, width = back_ref.shape
    capacity = both // 2
    rows = cot_ref.shape[0]
    for s in range(experts):
        here = slice(capacity * s, capacity * s + capacity)
        y_s[here, :] = back_ref[s, :capacity, :]
        dx_s[here, :] = back_ref[s, capacity:, :]
    grad_out = cot_ref[...].astype(F32)
    mixed = mixed_ref[...]
    gates = [gates_ref[:, k : k + 1] for k in range(2)]
    picked = [dot(pick_ref[k], y_s[...]) for k in range(2)]
    out_ref[...] = (mixed + (gates[0] * picked[0] + gates[1] * picked[1])).astype(BF16)
    grad_gates = [jnp.sum(p * grad_out, axis=1, keepdims=True) for p in picked]
    mean = gates[0] * grad_gates[0] + gates[1] * grad_gates[1]
    grad_chosen = [gates[k] * (grad_gates[k] - mean) for k in range(2)]
    ids = lax.broadcasted_iota(jnp.int32, (rows, experts), 1)
    routes = routes_ref[...]
    grad_logits = jnp.where(routes[:, :1] == ids, grad_chosen[0], 0.0) + jnp.where(
        routes[:, 1:2] == ids, grad_chosen[1], 0.0
    )
    grad_second = dot(pick_ref[0], dx_s[...]) + dot(pick_ref[1], dx_s[...])
    grad_second = grad_second + dot(grad_logits, wr_ref[...].astype(F32), NT, HIGHEST)
    second = second_ref[...]
    grad_router = dot(grad_logits, second.astype(F32), TN, HIGHEST)
    scale = rms_scale(mixed)
    grad_gain = jnp.sum(grad_second * mixed * scale, axis=0, keepdims=True)
    grad_mixed = grad_out + norm_back(mixed, scale, gain_ref[...], grad_second)
    grad_mixed_ref[...] = grad_mixed
    grad_branch = grad_mixed.astype(BF16)
    grad_att = dot(grad_branch, wo_ref[...], NT).astype(BF16)
    heads = width // 64
    for h in range(heads):
        cols = slice(64 * h, 64 * h + 64)
        heads_ref[h] = jnp.concatenate([grad_att[:64, cols], grad_att[64:, cols]], axis=1)
    for h in range(heads, HEAD_SLOTS):
        heads_ref[h] = jnp.zeros_like(heads_ref[h])
    grad_wo = dot(att_ref[...], grad_branch, TN).astype(BF16)
    slots, each, unused = sums_ref.shape
    used = width // each
    for c in range(used):
        sums_ref[c] = grad_wo[each * c : each * c + each]
    small = jnp.concatenate([grad_router, jnp.broadcast_to(grad_gain, (8, width))], axis=0)
    for c in range(used, slots):
        sums_ref[c] = jnp.zeros_like(sums_ref[c])
    sums_ref[used, :16, :] = small.astype(BF16)


def combine(cotangent, back, picks, gates, mixed, second, attended, routes, gain_two, w_router, w_out):
    rows, width = cotangent.shape
    experts, both, unused = back.shape
    held = experts * both // 2
    return pl.pallas_call(
        combine_kernel,
        name="combine",
        out_shape=(
            jax.ShapeDtypeStruct((rows, width), BF16),
            jax.ShapeDtypeStruct((rows, width), F32),
            jax.ShapeDtypeStruct((HEAD_SLOTS, rows // 2, 128), BF16),
            jax.ShapeDtypeStruct((HEAD_SLOTS, 64, width), BF16),
        ),
        in_specs=[vspec()] * 11,
        out_specs=(vspec(),) * 4,
        scratch_shapes=[pltpu.VMEM((held, width), BF16), pltpu.VMEM((held, width), BF16)],
        compiler_params=whole(),
    )(
        cotangent,
        back,
        picks,
        gates,
        mixed,
        second,
        attended,
        routes,
        gain_two.reshape(1, width),
        w_router,
        w_out,
    )


def input_grad_kernel(tok_ref, gain_ref, grads_ref, wq_ref, wk_ref, wv_ref, mixed_ref, out_ref, dq_s, dk_s, dv_s):
    for j in range(dq_s.shape[1] // 128):
        cols = slice(128 * j, 128 * j + 128)
        one, two = grads_ref[2 * j], grads_ref[2 * j + 1]
        dq_s[:, cols] = jnp.concatenate([one[:128, :64], two[:128, :64]], axis=1)
        dk_s[:, cols] = jnp.concatenate([one[:128, 64:], two[:128, 64:]], axis=1)
        dv_s[:64, cols] = jnp.concatenate([one[128:, :64], two[128:, :64]], axis=1)
        dv_s[64:, cols] = jnp.concatenate([one[128:, 64:], two[128:, 64:]], axis=1)
    grad_normed = dot(dq_s[...], wq_ref[...], NT)
    grad_normed = grad_normed + dot(dk_s[...], wk_ref[...], NT)
    grad_normed = grad_normed + dot(dv_s[...], wv_ref[...], NT)
    inputs = tok_ref[...].astype(F32)
    out_ref[...] = mixed_ref[...] + norm_back(inputs, rms_scale(inputs), gain_ref[...], grad_normed)


def input_grad(tokens, gain_one, grads, w_query, w_key, w_value, grad_mixed):
    rows, width = tokens.shape
    return pl.pallas_call(
        input_grad_kernel,
        name="input_grad",
        out_shape=jax.ShapeDtypeStruct((rows, width), F32),
        in_specs=[vspec()] * 7,
        out_specs=vspec(),
        scratch_shapes=[pltpu.VMEM((rows, width), BF16)] * 3,
        compiler_params=whole(),
    )(tokens, gain_one.reshape(1, width), grads, w_query, w_key, w_value, grad_mixed)


def coordinates(index):
    context, expert = index // 8, index % 8
    return (context // 8 * 2 + expert % 2, expert // 2, context // 2 % 4, context % 2)


def device_at(x, y, z, core):
    return ((x // 2 * 4 + z) * 2 + core) * 8 + y * 2 + x % 2


def shifted(dim, by):
    pairs = []
    for index in range(128):
        place = list(coordinates(index))
        place[dim] = (place[dim] + by) % (2 if dim == 3 else 4)
        pairs.append((index, device_at(*place)))
    return pairs


def ring_gather(block, dim):
    axes = ("context", "expert")
    ahead = lax.ppermute(block, axes, shifted(dim, -1))
    behind = lax.ppermute(block, axes, shifted(dim, 1))
    half = block.shape[0] // 2
    across = jnp.concatenate(
        [
            lax.ppermute(ahead[:half], axes, shifted(dim, -1)),
            lax.ppermute(behind[half:], axes, shifted(dim, 1)),
        ],
        axis=0,
    )
    return jnp.stack([block, ahead, across, behind])


def gather_all(piece):
    filled = ring_gather(piece, 2)
    filled = ring_gather(filled, 1)
    filled = ring_gather(filled, 0)
    other = lax.ppermute(filled, ("context", "expert"), shifted(3, 1))
    return jnp.stack([filled, other])


def unpack_kernel(
    buckets,
    place_ref,
    piece_ref,
    late_ref,
    gain_ref,
    wq_ref,
    wk_ref,
    wv_ref,
    dwq_ref,
    dwk_ref,
    dwv_ref,
    dwo_ref,
    bias_ref,
    small_ref,
    gain_grad_ref,
):
    expert = pl.program_id(0)
    my_x, my_y, my_z, my_core = (place_ref[i] for i in range(4))
    each = dwq_ref.shape[0]
    half = each // 2
    width = dwq_ref.shape[1]
    y = expert // 2
    rel_y = lax.rem(y - my_y + 4, 4)

    def rel(context):
        x = context // 8 * 2 + lax.rem(expert, 2)
        return (
            jnp.where(my_core == context % 2, 0, 1),
            lax.rem(x - my_x + 4, 4),
            rel_y,
            lax.rem(context // 2 % 4 - my_z + 4, 4),
        )

    bias = []
    for j in range(width // 128):
        cols = slice(128 * j, 128 * j + 128)
        one, two = piece_ref[rel(2 * j)].astype(F32), piece_ref[rel(2 * j + 1)].astype(F32)
        dwq_ref[:, cols] = jnp.concatenate([one[:each, :64], two[:each, :64]], axis=1)
        dwk_ref[:, cols] = jnp.concatenate([one[:each, 64:], two[:each, 64:]], axis=1)
        dwv_ref[:half, cols] = jnp.concatenate(
            [one[each : each + half, :64], two[each : each + half, :64]], axis=1
        )
        dwv_ref[half:, cols] = jnp.concatenate(
            [one[each : each + half, 64:], two[each : each + half, 64:]], axis=1
        )
        bias += [one[each + half : each + half + 1], two[each + half : each + half + 1]]
    bias_ref[...] = jnp.concatenate(bias, axis=0)[:, :buckets]
    for c in range(width // 64):
        dwo_ref[c] = late_ref[rel(c)].astype(F32)
    small_ref[0] = late_ref[rel(width // 64)].astype(F32)
    summed = jnp.sum(
        dwq_ref[...] * wq_ref[...].astype(F32)
        + dwk_ref[...] * wk_ref[...].astype(F32)
        + dwv_ref[...] * wv_ref[...].astype(F32),
        axis=1,
        keepdims=True,
    )
    gain_grad_ref[...] = summed / gain_ref[...]


def unpack(place, pieces, late, gain_one, w_query, w_key, w_value, heads, buckets, experts):
    width = w_query.shape[0]
    each = width // experts
    rows = pl.BlockSpec((each, width), lambda i: (i, 0))
    return pl.pallas_call(
        lambda *refs: unpack_kernel(buckets, *refs),
        name="unpack",
        grid=(experts,),
        out_shape=(
            jax.ShapeDtypeStruct((width, width), F32),
            jax.ShapeDtypeStruct((width, width), F32),
            jax.ShapeDtypeStruct((width, width), F32),
            jax.ShapeDtypeStruct((heads, experts, 8, width), F32),
            jax.ShapeDtypeStruct((heads, buckets), F32),
            jax.ShapeDtypeStruct((experts, 8, width), F32),
            jax.ShapeDtypeStruct((width, 1), F32),
        ),
        in_specs=[
            sspec(),
            vspec(),
            vspec(),
            pl.BlockSpec((each, 1), lambda i: (i, 0)),
            rows,
            rows,
            rows,
        ],
        out_specs=(
            rows,
            rows,
            rows,
            pl.BlockSpec((heads, None, 8, width), lambda i: (0, i, 0, 0)),
            pl.BlockSpec((heads, buckets), lambda i: (0, 0)),
            pl.BlockSpec((1, 8, width), lambda i: (i, 0, 0)),
            pl.BlockSpec((each, 1), lambda i: (i, 0)),
        ),
        compiler_params=whole(),
    )(place, pieces, late, gain_one.reshape(width, 1), w_query, w_key, w_value)


def add_up(received):
    return jnp.sum(received.astype(F32), axis=0)


def shards(
    tokens,
    gain_one,
    w_query,
    w_key,
    w_value,
    w_out,
    rel_table,
    gain_two,
    w_router,
    expert_in,
    expert_out,
    routes,
    cotangent,
):
    width = tokens.shape[2]
    heads, buckets = rel_table.shape
    experts = lax.axis_size("expert")
    inputs, grad_out, routes_here = tokens[0], cotangent[0], routes[0]
    context = lax.axis_index("context")
    head = jnp.minimum(context, heads - 1).astype(jnp.int32).reshape(1)

    normed, packed = project(inputs, gain_one, w_query, w_key, w_value)
    qkv = lax.all_to_all(packed, "context", split_axis=0, concat_axis=0, tiled=True)
    own_weights = jnp.concatenate([expert_in[0].T, expert_out[0].T], axis=1)
    weights = lax.all_gather(own_weights, "context", axis=0, tiled=True)
    normed_all = lax.all_gather(normed, "context", axis=0, tiled=True)

    out_heads, keep, lse = attend(head, rel_table, qkv)
    out_rows = lax.all_to_all(out_heads, "context", split_axis=0, concat_axis=0, tiled=True)
    send, attended, mixed, second, picks, gates = dispatch(
        inputs, grad_out, out_rows, w_out, gain_two, w_router, routes_here, experts
    )
    received = lax.all_to_all(send, "expert", split_axis=0, concat_axis=0, tiled=True)
    back, weight_grads = expert_both(received, weights)
    returned = lax.all_to_all(back, "expert", split_axis=0, concat_axis=0, tiled=True)
    own_grads = lax.psum_scatter(weight_grads, "context", scatter_dimension=0, tiled=True)
    block_out, grad_mixed, grad_heads, sums = combine(
        grad_out, returned, picks, gates, mixed, second, attended, routes_here, gain_two, w_router, w_out
    )
    grad_here = lax.all_to_all(grad_heads, "context", split_axis=0, concat_axis=0, tiled=True)
    sums = lax.all_to_all(sums, "context", split_axis=0, concat_axis=0, tiled=True)
    sums = add_up(sums).astype(BF16).reshape(experts, 8, width)
    sums = lax.all_to_all(sums, "expert", split_axis=0, concat_axis=0, tiled=True)
    late = gather_all(add_up(sums).astype(BF16))

    dqkv, dw = attend_back(head, rel_table, qkv, grad_here, keep, lse, normed_all, experts)
    dw = lax.all_to_all(dw, "expert", split_axis=0, concat_axis=0, tiled=True)
    pieces = gather_all(add_up(dw).astype(BF16))
    grads = lax.all_to_all(dqkv, "context", split_axis=0, concat_axis=0, tiled=True)
    grad_tokens = input_grad(inputs, gain_one, grads, w_query, w_key, w_value, grad_mixed)

    expert = lax.axis_index("expert")
    place = jnp.stack(coordinates(context * experts + expert)).astype(jnp.int32)
    dwq, dwk, dwv, dwo, bias, small, gain_grad = unpack(
        place, pieces, late, gain_one, w_query, w_key, w_value, heads, buckets, experts
    )
    own_grads = own_grads.astype(F32)
    return (
        block_out[None],
        grad_tokens[None],
        gain_grad.reshape(width),
        dwq,
        dwk,
        dwv,
        dwo.reshape(width, width),
        bias,
        small[1, 0],
        small[0].T,
        own_grads[:, :width].T[None],
        own_grads[:, width:].T[None],
    )


def solution(mesh):
    return jax.shard_map(
        shards,
        mesh=mesh,
        in_specs=(
            P("expert", "context", None),
            P(),
            P(),
            P(),
            P(),
            P(),
            P(),
            P(),
            P(),
            P("expert", None, "context"),
            P("expert", None, "context"),
            P("expert", "context", None),
            P("expert", "context", None),
        ),
        out_specs=(
            P("expert", "context", None),
            P("expert", "context", None),
            P(),
            P(),
            P(),
            P(),
            P(),
            P(),
            P(),
            P(),
            P("expert", None, "context"),
            P("expert", None, "context"),
        ),
        check_vma=False,
    )
```

```python
import math

import jax
import jax.numpy as jnp
from jax import lax
from jax.experimental import pallas as pl
from jax.experimental.pallas import tpu as pltpu
from jax.sharding import PartitionSpec as P

MAX_DIST = 128
EPSILON = 1e-06
NEG_LARGE = -1e30
BLK = 256
HEAD_SLOTS = 16

F32 = jnp.float32
BF16 = jnp.bfloat16
HIGHEST = lax.Precision.HIGHEST

NN = (((1,), (0,)), ((), ()))
NT = (((1,), (1,)), ((), ()))
TN = (((0,), (0,)), ((), ()))


def dot(a, b, dims=NN, precision=None):
    return lax.dot_general(a, b, dims, precision=precision, preferred_element_type=F32)


def bucket_starts(buckets, far_reach):
    span = buckets // 2
    rest = [
        int(math.ceil(span * (far_reach / span) ** (step / (buckets - span))))
        for step in range(1, buckets - span)
    ]
    return list(range(span + 1)) + rest


def rms_scale(values):
    return lax.rsqrt(jnp.mean(values * values, axis=-1, keepdims=True) + EPSILON)


def norm_back(values, inv_root, gain_vec, grad_normed):
    weighted = grad_normed * gain_vec
    cubed = inv_root * inv_root * inv_root
    return inv_root * weighted - values * cubed * jnp.mean(
        weighted * values, axis=-1, keepdims=True
    )


def whole(vmem_mib=56):
    return pltpu.CompilerParams(vmem_limit_bytes=vmem_mib * 2**20)


def vspec():
    return pl.BlockSpec(memory_space=pltpu.VMEM)


def sspec():
    return pl.BlockSpec(memory_space=pltpu.SMEM)


def project_kernel(tok_ref, gain_ref, wq_ref, wk_ref, wv_ref, win_ref, wback_ref, share_ref, out_ref):
    inputs = tok_ref[...].astype(F32)
    normed = (inputs * rms_scale(inputs) * gain_ref[...][None, :]).astype(BF16)
    rows, width = normed.shape
    half = rows // 2
    hidden = win_ref.shape[2]
    share_ref[:hidden, :width] = win_ref[0].T
    share_ref[:hidden, width:] = wback_ref[0].T
    share_ref[hidden:, :width] = normed[:half]
    share_ref[hidden:, width:] = normed[half:]
    queries = (dot(normed, wq_ref[...]).astype(BF16).astype(F32) * 0.125).astype(BF16)
    keys = dot(normed, wk_ref[...]).astype(BF16)
    values = dot(normed, wv_ref[...]).astype(BF16)
    heads = width // 64
    for h in range(heads):
        cols = slice(64 * h, 64 * h + 64)
        out_ref[h, :rows, :] = jnp.concatenate([queries[:, cols], keys[:, cols]], axis=1)
        out_ref[h, rows:, :] = jnp.concatenate([values[:half, cols], values[half:, cols]], axis=1)
    for h in range(heads, HEAD_SLOTS):
        out_ref[h] = jnp.zeros_like(out_ref[h])


def project(tokens, gain_one, w_query, w_key, w_value, expert_in, expert_out):
    rows, width = tokens.shape
    hidden = expert_in.shape[2]
    return pl.pallas_call(
        project_kernel,
        name="project",
        out_shape=(
            jax.ShapeDtypeStruct((hidden + rows // 2, 2 * width), BF16),
            jax.ShapeDtypeStruct((HEAD_SLOTS, rows + rows // 2, 128), BF16),
        ),
        in_specs=[vspec()] * 7,
        out_specs=(vspec(), vspec()),
        compiler_params=whole(),
    )(tokens, gain_one, w_query, w_key, w_value, expert_in, expert_out)


def bias_tile(table_ref, head, buckets, rows_first, shape, key_dim):
    sign = [1, -1] if key_dim == 1 else [-1, 1]
    dist = (
        rows_first
        + sign[0] * lax.broadcasted_iota(jnp.int32, shape, 0)
        + sign[1] * lax.broadcasted_iota(jnp.int32, shape, 1)
    )
    far = table_ref[head, buckets - 1]
    tile = jnp.full(shape, NEG_LARGE, F32)
    for b, start in enumerate(bucket_starts(buckets, MAX_DIST)):
        tile = jnp.where(dist >= start, table_ref[head, b] - far, tile)
    return tile


def unpack_qkv(qkv_ref, q_s, k_s, v_s, ones_lane):
    count = qkv_ref.shape[0]
    lane = lax.broadcasted_iota(jnp.int32, (64, 64), 1)
    one = jnp.where(lane == 0, 1.0, 0.0).astype(BF16)
    for c in range(count):
        pair = qkv_ref[c, :128, :]
        q_s[128 * c : 128 * c + 128, :] = pair[:, :64]
        k_s[128 * c : 128 * c + 128, :] = pair[:, 64:]
        two = qkv_ref[c, 128:192, :]
        top, bottom = two[:, :64], two[:, 64:]
        if ones_lane:
            top = jnp.concatenate([top, one], axis=1)
            bottom = jnp.concatenate([bottom, one], axis=1)
        v_s[128 * c : 128 * c + 64, :] = top
        v_s[128 * c + 64 : 128 * c + 128, :] = bottom


def attend_kernel(buckets, head_ref, table_ref, qkv_ref, out_ref, keep_ref, lse_ref, q_s, k_s, v_s, bias_s):
    head = head_ref[0]
    unpack_qkv(qkv_ref, q_s, k_s, v_s, True)
    bias_s[0] = bias_tile(table_ref, head, buckets, BLK, (BLK, BLK), 1)
    bias_s[1] = bias_tile(table_ref, head, buckets, 0, (BLK, BLK), 1)
    blocks = q_s.shape[0] // BLK

    for qb in range(blocks):
        query = q_s[BLK * qb : BLK * qb + BLK, :]
        near = max(qb - 1, 0) * BLK
        parts = []
        if near:
            parts.append((0, dot(query, k_s[:near, :], NT)))
        if qb:
            parts.append((near, dot(query, k_s[near : near + BLK, :], NT) + bias_s[0]))
        parts.append((BLK * qb, dot(query, k_s[BLK * qb : BLK * qb + BLK, :], NT) + bias_s[1]))
        top = parts[-1][1]
        top = jnp.maximum(top[:, :128], top[:, 128:])
        for unused, scores in parts[:-1]:
            for j in range(scores.shape[1] // 128):
                top = jnp.maximum(top, scores[:, 128 * j : 128 * j + 128])
        top = jnp.max(top, axis=1, keepdims=True)
        total = jnp.zeros((BLK, 128), F32)
        for first, scores in parts:
            weights = jnp.exp(scores - top).astype(BF16)
            total = total + dot(weights, v_s[first : first + scores.shape[1], :])
        norm = total[:, 64:65]
        out = total[:, :64] / norm
        log_total = top + jnp.log(norm)
        spread = jnp.broadcast_to(log_total, (BLK, 128)).T
        lse_ref[qb] = spread[:8, :]
        for part in range(BLK // 128):
            two = jnp.concatenate(
                [out[128 * part : 128 * part + 64], out[128 * part + 64 : 128 * part + 128]], axis=1
            )
            place = qb * (BLK // 128) + part
            out_ref[place] = two.astype(BF16)
            keep_ref[place] = two


def attend(head, rel_table, qkv):
    count = qkv.shape[0]
    length = 128 * count
    blocks = length // BLK
    return pl.pallas_call(
        lambda *refs: attend_kernel(rel_table.shape[1], *refs),
        name="attend",
        out_shape=(
            jax.ShapeDtypeStruct((count, 64, 128), BF16),
            jax.ShapeDtypeStruct((count, 64, 128), F32),
            jax.ShapeDtypeStruct((blocks, 8, BLK), F32),
        ),
        in_specs=[sspec(), sspec(), vspec()],
        out_specs=(vspec(), vspec(), vspec()),
        scratch_shapes=[
            pltpu.VMEM((length, 64), BF16),
            pltpu.VMEM((length, 64), BF16),
            pltpu.VMEM((length, 128), BF16),
            pltpu.VMEM((2, BLK, BLK), F32),
        ],
        compiler_params=whole(),
    )(head, rel_table, qkv)


def attend_back_kernel(
    buckets,
    head_ref,
    table_ref,
    qkv_ref,
    go_ref,
    keep_ref,
    lse_ref,
    dqkv_ref,
    bias_ref,
    q_s,
    k_s,
    v_s,
    kt_s,
    go_s,
    delta_s,
    dq_s,
    dk_s,
    dv_s,
    bias_s,
    acc_s,
):
    head = head_ref[0]
    length = q_s.shape[0]
    count = qkv_ref.shape[0]
    blocks = length // BLK
    unpack_qkv(qkv_ref, q_s, k_s, v_s, False)
    ones = jnp.ones((8, 64), F32)
    for c in range(count):
        kt_s[:, 128 * c : 128 * c + 128] = k_s[128 * c : 128 * c + 128, :].T
        two, kept = go_ref[c], keep_ref[c]
        go_s[128 * c : 128 * c + 64, :] = two[:, :64]
        go_s[128 * c + 64 : 128 * c + 128, :] = two[:, 64:]
        both = two.astype(F32) * kept
        prod = jnp.concatenate([both[:, :64], both[:, 64:]], axis=0)
        delta_s[:, 128 * c : 128 * c + 128] = dot(ones, prod, NT, HIGHEST)
    bias_s[0] = bias_tile(table_ref, head, buckets, BLK, (BLK, BLK), 0)
    bias_s[1] = bias_tile(table_ref, head, buckets, 0, (BLK, BLK), 0)
    acc_s[...] = jnp.zeros_like(acc_s)
    dk_s[...] = jnp.zeros_like(dk_s)
    dv_s[...] = jnp.zeros_like(dv_s)

    far_sum = jnp.zeros((8, BLK), F32)
    for qb in range(blocks):
        rows = slice(BLK * qb, BLK * qb + BLK)
        query, grad = q_s[rows, :], go_s[rows, :]
        lse = lse_ref[qb][:1, :]
        delta = delta_s[:1, rows]
        grad_query = jnp.zeros((64, BLK), F32)
        for kb in range(qb + 1):
            cols = slice(BLK * kb, BLK * kb + BLK)
            near = kb - qb + 1
            scores = dot(k_s[cols, :], query, NT)
            if near >= 0:
                scores = scores + bias_s[near]
            probs = jnp.exp(scores - lse)
            grad_probs = dot(v_s[cols, :], grad, NT)
            grad_scores = (probs * (grad_probs - delta)).astype(BF16)
            dv_s[cols, :] += dot(probs.astype(BF16), grad)
            dk_s[cols, :] += dot(grad_scores, query)
            grad_query = grad_query + dot(kt_s[:, cols], grad_scores)
            wide = grad_scores.astype(F32)
            if near < 0:
                far_sum = far_sum + jnp.sum(wide.reshape(BLK // 8, 8, BLK), axis=0)
            else:
                acc_s[near] += wide
        dq_s[:, rows] = grad_query

    for c in range(count):
        here = slice(128 * c, 128 * c + 128)
        dq_t = (dq_s[:, here] * 0.125).astype(BF16)
        dk = dk_s[here, :].astype(BF16)
        dv = dv_s[here, :].astype(BF16)
        dqkv_ref[c, :128, :] = jnp.concatenate([dq_t.T, dk], axis=1)
        dqkv_ref[c, 128:192, :] = jnp.concatenate([dv[:64], dv[64:]], axis=1)

    lane = lax.broadcasted_iota(jnp.int32, (16, 128), 1)
    dist0 = (
        BLK
        - lax.broadcasted_iota(jnp.int32, (BLK, BLK), 0)
        + lax.broadcasted_iota(jnp.int32, (BLK, BLK), 1)
    )
    dist1 = dist0 - BLK

    def total(values):
        return jnp.sum(jnp.sum(values, axis=1, keepdims=True), axis=0, keepdims=True)

    starts = bucket_starts(buckets, MAX_DIST)
    row = jnp.zeros((16, 128), F32)
    above = None
    for b in reversed(range(buckets)):
        reach = total(
            jnp.where(dist0 >= starts[b], acc_s[0], 0.0)
            + jnp.where(dist1 >= starts[b], acc_s[1], 0.0)
        )
        mine = reach + total(far_sum) if b == buckets - 1 else reach - above
        above = reach
        row = jnp.where(lane == b, mine, row)
    bias_ref[...] = row


def attend_back(head, rel_table, qkv, grad_heads, keep, lse):
    count = qkv.shape[0]
    length = 128 * count
    return pl.pallas_call(
        lambda *refs: attend_back_kernel(rel_table.shape[1], *refs),
        name="attend_back",
        out_shape=(
            jax.ShapeDtypeStruct(qkv.shape, BF16),
            jax.ShapeDtypeStruct((16, 128), F32),
        ),
        in_specs=[sspec(), sspec()] + [vspec()] * 4,
        out_specs=(vspec(), vspec()),
        scratch_shapes=[
            pltpu.VMEM((length, 64), BF16),
            pltpu.VMEM((length, 64), BF16),
            pltpu.VMEM((length, 64), BF16),
            pltpu.VMEM((64, length), BF16),
            pltpu.VMEM((length, 64), BF16),
            pltpu.VMEM((8, length), F32),
            pltpu.VMEM((64, length), F32),
            pltpu.VMEM((length, 64), F32),
            pltpu.VMEM((length, 64), F32),
            pltpu.VMEM((2, BLK, BLK), F32),
            pltpu.VMEM((2, BLK, BLK), F32),
        ],
        compiler_params=whole(),
    )(head, rel_table, qkv, grad_heads, keep, lse)


def head_grads_kernel(dqkv_ref, normed_ref, bias_ref, sums_ref, out_ref):
    count = dqkv_ref.shape[0]
    width = normed_ref.shape[2] // 2
    tokens = count * 64
    first = normed_ref[:, :, :width].reshape(tokens, width)
    second = normed_ref[:, :, width:].reshape(tokens, width)
    pairs = dot(dqkv_ref[:, :64, :].reshape(tokens, 128), first, TN) + dot(
        dqkv_ref[:, 64:128, :].reshape(tokens, 128), second, TN
    )
    two = dqkv_ref[:, 128:192, :].reshape(tokens, 128)
    third = dot(two, first, TN)[:64] + dot(two, second, TN)[64:]
    pairs, third = pairs.T, third.T
    total = sums_ref[0].astype(F32)
    for c in range(1, count):
        total = total + sums_ref[c].astype(F32)
    shares = out_ref.shape[0]
    each = width // shares
    row = bias_ref[...].astype(BF16)
    for s in range(shares):
        mine = slice(each * s, each * s + each)
        out_ref[s, :each, :] = pairs[mine].astype(BF16)
        last = third[mine].astype(BF16)
        out_ref[s, each : each + each // 2, :] = jnp.concatenate(
            [last[: each // 2], last[each // 2 :]], axis=1
        )
        at = each + each // 2
        out_ref[s, at : at + 16, :] = row
        part = total[8 * s : 8 * s + 8]
        out_ref[s, at + 16 :, :] = jnp.concatenate(
            [part[:, 128 * j : 128 * j + 128] for j in range(width // 128)], axis=0
        ).astype(BF16)


def head_grads(dqkv, shared, bias, sums, shares):
    count, rows, wide = shared.shape
    width = wide // 2
    each = width // shares
    held = each + each // 2 + 16 + width // 16
    return pl.pallas_call(
        head_grads_kernel,
        name="head_grads",
        grid=(1,),
        out_shape=jax.ShapeDtypeStruct((shares, held, 128), BF16),
        in_specs=[
            vspec(),
            pl.BlockSpec((count, 64, wide), lambda i: (0, rows // 64 - 1, 0)),
            vspec(),
            vspec(),
        ],
        out_specs=vspec(),
        compiler_params=whole(),
    )(dqkv, shared, bias, sums)


def heads_to_rows(ref, scratch):
    for j in range(scratch.shape[1] // 128):
        one, two = ref[2 * j], ref[2 * j + 1]
        scratch[:64, 128 * j : 128 * j + 128] = jnp.concatenate([one[:, :64], two[:, :64]], axis=1)
        scratch[64:, 128 * j : 128 * j + 128] = jnp.concatenate([one[:, 64:], two[:, 64:]], axis=1)


def dispatch_kernel(
    experts,
    capacity,
    tok_ref,
    cot_ref,
    heads_ref,
    wo_ref,
    gain_ref,
    wr_ref,
    routes_ref,
    send_ref,
    att_ref,
    mixed_ref,
    second_ref,
    pick_ref,
    gates_ref,
):
    rows = tok_ref.shape[0]
    heads_to_rows(heads_ref, att_ref)
    mixed = tok_ref[...].astype(F32) + dot(att_ref[...], wo_ref[...])
    mixed_ref[...] = mixed
    second = (mixed * rms_scale(mixed) * gain_ref[...][None, :]).astype(BF16)
    second_ref[...] = second
    logits = dot(second, wr_ref[...])
    ids = lax.broadcasted_iota(jnp.int32, (rows, experts), 1)
    routes = routes_ref[...]
    marks = [(routes[:, k : k + 1] == ids).astype(F32) for k in range(2)]
    earlier = (
        lax.broadcasted_iota(jnp.int32, (rows, rows), 0)
        > lax.broadcasted_iota(jnp.int32, (rows, rows), 1)
    ).astype(F32)
    ranks = dot(earlier.astype(BF16), (marks[0] + marks[1]).astype(BF16))
    chosen = [jnp.sum(m * logits, axis=1, keepdims=True) for m in marks]
    top = jnp.maximum(chosen[0], chosen[1])
    exps = [jnp.exp(c - top) for c in chosen]
    gates = [e / (exps[0] + exps[1]) for e in exps]
    slot_ids = lax.broadcasted_iota(jnp.int32, (rows, experts * capacity), 1)
    grad_out = cot_ref[...].astype(F32)
    picks = []
    for k in range(2):
        slot = jnp.sum(marks[k] * ranks, axis=1, keepdims=True).astype(jnp.int32)
        place = routes[:, k : k + 1] * capacity + slot
        picks.append((place == slot_ids).astype(F32).astype(BF16))
        pick_ref[k] = picks[k]
    send_rows = dot(picks[0] + picks[1], second, TN).astype(BF16)
    send_grads = dot(picks[0], (gates[0] * grad_out).astype(BF16), TN) + dot(
        picks[1], (gates[1] * grad_out).astype(BF16), TN
    )
    send_grads = send_grads.astype(BF16)
    for e in range(experts):
        here = slice(capacity * e, capacity * e + capacity)
        send_ref[e, :capacity, :] = send_rows[here]
        send_ref[e, capacity:, :] = send_grads[here]
    lane = lax.broadcasted_iota(jnp.int32, (rows, 128), 1)
    gates_ref[...] = jnp.where(lane == 0, gates[0], gates[1])


def dispatch(tokens, cotangent, heads, w_out, gain_two, w_router, routes, experts):
    rows, width = tokens.shape
    capacity = 3 * rows // experts
    return pl.pallas_call(
        lambda *refs: dispatch_kernel(experts, capacity, *refs),
        name="dispatch",
        out_shape=(
            jax.ShapeDtypeStruct((experts, 2 * capacity, width), BF16),
            jax.ShapeDtypeStruct((rows, width), BF16),
            jax.ShapeDtypeStruct((rows, width), F32),
            jax.ShapeDtypeStruct((rows, width), BF16),
            jax.ShapeDtypeStruct((2, rows, experts * capacity), BF16),
            jax.ShapeDtypeStruct((rows, 128), F32),
        ),
        in_specs=[vspec()] * 7,
        out_specs=(vspec(),) * 6,
        compiler_params=whole(),
    )(tokens, cotangent, heads, w_out, gain_two, w_router, routes)


def expert_kernel(rows_ref, w_ref, back_ref, dw_ref, x_s, g_s, y_s, dx_s):
    step = pl.program_id(0)
    sources, both, width = rows_ref.shape
    capacity = both // 2

    @pl.when(step == 0)
    def _():
        for s in range(sources):
            x_s[capacity * s : capacity * s + capacity, :] = rows_ref[s, :capacity, :]
            g_s[capacity * s : capacity * s + capacity, :] = rows_ref[s, capacity:, :]
        y_s[...] = jnp.zeros_like(y_s)
        dx_s[...] = jnp.zeros_like(dx_s)

    weights = w_ref[...].reshape(-1, 2 * width)
    w_in, w_back = weights[:, :width], weights[:, width:]
    pre = dot(x_s[...], w_in, NT)
    square = pre * pre
    curve = jnp.tanh(0.7978845608 * (pre + 0.044715 * square * pre))
    act = (0.5 * pre * (1.0 + curve)).astype(BF16)
    slope = 0.5 * (1.0 + curve) + 0.5 * pre * (1.0 - curve * curve) * (
        0.7978845608 * (1.0 + 3.0 * 0.044715 * square)
    )
    grad_pre = (dot(g_s[...], w_back, NT) * slope).astype(BF16)
    y_s[...] += dot(act, w_back)
    dx_s[...] += dot(grad_pre, w_in)
    dw_ref[:, :width] = dot(grad_pre, x_s[...], TN).astype(BF16)
    dw_ref[:, width:] = dot(act, g_s[...], TN).astype(BF16)

    @pl.when(step == pl.num_programs(0) - 1)
    def _():
        for s in range(sources):
            here = slice(capacity * s, capacity * s + capacity)
            back_ref[s, :capacity, :] = y_s[here, :].astype(BF16)
            back_ref[s, capacity:, :] = dx_s[here, :].astype(BF16)


def expert_both(rows, shared):
    sources, both, width = rows.shape
    count, given, wide = shared.shape
    each = given - 64
    at_once = 2
    chunk = at_once * each
    held = sources * both // 2
    return pl.pallas_call(
        expert_kernel,
        name="expert_both",
        grid=(count // at_once,),
        out_shape=(
            jax.ShapeDtypeStruct(rows.shape, BF16),
            jax.ShapeDtypeStruct((count * each, wide), BF16),
        ),
        in_specs=[
            pl.BlockSpec(rows.shape, lambda i: (0, 0, 0)),
            pl.BlockSpec((at_once, each, wide), lambda i: (i, 0, 0)),
        ],
        out_specs=(
            pl.BlockSpec(rows.shape, lambda i: (0, 0, 0)),
            pl.BlockSpec((chunk, wide), lambda i: (i, 0)),
        ),
        scratch_shapes=[
            pltpu.VMEM((held, width), BF16),
            pltpu.VMEM((held, width), BF16),
            pltpu.VMEM((held, width), F32),
            pltpu.VMEM((held, width), F32),
        ],
        compiler_params=whole(),
    )(rows, shared)


def combine_kernel(
    cot_ref,
    back_ref,
    pick_ref,
    gates_ref,
    mixed_ref,
    second_ref,
    att_ref,
    routes_ref,
    gain_ref,
    wr_ref,
    wo_ref,
    out_ref,
    grad_mixed_ref,
    heads_ref,
    sums_ref,
    y_s,
    dx_s,
):
    experts, both, width = back_ref.shape
    capacity = both // 2
    rows = cot_ref.shape[0]
    for s in range(experts):
        here = slice(capacity * s, capacity * s + capacity)
        y_s[here, :] = back_ref[s, :capacity, :]
        dx_s[here, :] = back_ref[s, capacity:, :]
    grad_out = cot_ref[...].astype(F32)
    mixed = mixed_ref[...]
    gates = [gates_ref[:, k : k + 1] for k in range(2)]
    picked = [dot(pick_ref[k], y_s[...]) for k in range(2)]
    out_ref[...] = (mixed + (gates[0] * picked[0] + gates[1] * picked[1])).astype(BF16)
    grad_gates = [jnp.sum(p * grad_out, axis=1, keepdims=True) for p in picked]
    mean = gates[0] * grad_gates[0] + gates[1] * grad_gates[1]
    grad_chosen = [gates[k] * (grad_gates[k] - mean) for k in range(2)]
    ids = lax.broadcasted_iota(jnp.int32, (rows, experts), 1)
    routes = routes_ref[...]
    grad_logits = jnp.where(routes[:, :1] == ids, grad_chosen[0], 0.0) + jnp.where(
        routes[:, 1:2] == ids, grad_chosen[1], 0.0
    )
    grad_second = dot(pick_ref[0], dx_s[...]) + dot(pick_ref[1], dx_s[...])
    grad_second = grad_second + dot(grad_logits, wr_ref[...].astype(F32), NT, HIGHEST)
    second = second_ref[...]
    grad_router = dot(grad_logits, second.astype(F32), TN, HIGHEST)
    scale = rms_scale(mixed)
    grad_gain = jnp.sum(grad_second * mixed * scale, axis=0, keepdims=True)
    grad_mixed = grad_out + norm_back(mixed, scale, gain_ref[...][None, :], grad_second)
    grad_mixed_ref[...] = grad_mixed
    grad_branch = grad_mixed.astype(BF16)
    grad_att = dot(grad_branch, wo_ref[...], NT).astype(BF16)
    heads = width // 64
    for h in range(heads):
        cols = slice(64 * h, 64 * h + 64)
        heads_ref[h] = jnp.concatenate([grad_att[:64, cols], grad_att[64:, cols]], axis=1)
    for h in range(heads, HEAD_SLOTS):
        heads_ref[h] = jnp.zeros_like(heads_ref[h])
    grad_wo = dot(att_ref[...], grad_branch, TN).astype(BF16)
    slots, each, unused = sums_ref.shape
    used = width // each
    for c in range(used):
        sums_ref[c] = grad_wo[each * c : each * c + each]
    small = jnp.concatenate([grad_router, jnp.broadcast_to(grad_gain, (8, width))], axis=0)
    for c in range(used, slots):
        sums_ref[c] = jnp.zeros_like(sums_ref[c])
    sums_ref[used, :16, :] = small.astype(BF16)


def combine(cotangent, back, picks, gates, mixed, second, attended, routes, gain_two, w_router, w_out):
    rows, width = cotangent.shape
    experts, both, unused = back.shape
    held = experts * both // 2
    return pl.pallas_call(
        combine_kernel,
        name="combine",
        out_shape=(
            jax.ShapeDtypeStruct((rows, width), BF16),
            jax.ShapeDtypeStruct((rows, width), F32),
            jax.ShapeDtypeStruct((HEAD_SLOTS, rows // 2, 128), BF16),
            jax.ShapeDtypeStruct((HEAD_SLOTS, 64, width), BF16),
        ),
        in_specs=[vspec()] * 11,
        out_specs=(vspec(),) * 4,
        scratch_shapes=[pltpu.VMEM((held, width), BF16), pltpu.VMEM((held, width), BF16)],
        compiler_params=whole(),
    )(
        cotangent,
        back,
        picks,
        gates,
        mixed,
        second,
        attended,
        routes,
        gain_two,
        w_router,
        w_out,
    )


def input_grad_kernel(tok_ref, gain_ref, grads_ref, wq_ref, wk_ref, wv_ref, mixed_ref, out_ref, dq_s, dk_s, dv_s):
    for j in range(dq_s.shape[1] // 128):
        cols = slice(128 * j, 128 * j + 128)
        one, two = grads_ref[2 * j], grads_ref[2 * j + 1]
        dq_s[:, cols] = jnp.concatenate([one[:128, :64], two[:128, :64]], axis=1)
        dk_s[:, cols] = jnp.concatenate([one[:128, 64:], two[:128, 64:]], axis=1)
        dv_s[:64, cols] = jnp.concatenate([one[128:, :64], two[128:, :64]], axis=1)
        dv_s[64:, cols] = jnp.concatenate([one[128:, 64:], two[128:, 64:]], axis=1)
    grad_normed = dot(dq_s[...], wq_ref[...], NT)
    grad_normed = grad_normed + dot(dk_s[...], wk_ref[...], NT)
    grad_normed = grad_normed + dot(dv_s[...], wv_ref[...], NT)
    inputs = tok_ref[...].astype(F32)
    out_ref[...] = mixed_ref[...] + norm_back(inputs, rms_scale(inputs), gain_ref[...][None, :], grad_normed)


def input_grad(tokens, gain_one, grads, w_query, w_key, w_value, grad_mixed):
    rows, width = tokens.shape
    return pl.pallas_call(
        input_grad_kernel,
        name="input_grad",
        out_shape=jax.ShapeDtypeStruct((rows, width), F32),
        in_specs=[vspec()] * 7,
        out_specs=vspec(),
        scratch_shapes=[pltpu.VMEM((rows, width), BF16)] * 3,
        compiler_params=whole(),
    )(tokens, gain_one, grads, w_query, w_key, w_value, grad_mixed)


def coordinates(index):
    context, expert = index // 8, index % 8
    return (context // 8 * 2 + expert % 2, expert // 2, context // 2 % 4, context % 2)


def device_at(x, y, z, core):
    return ((x // 2 * 4 + z) * 2 + core) * 8 + y * 2 + x % 2


def shifted(dim, by):
    pairs = []
    for index in range(128):
        place = list(coordinates(index))
        place[dim] = (place[dim] + by) % (2 if dim == 3 else 4)
        pairs.append((index, device_at(*place)))
    return pairs


AXES = ("context", "expert")


def direct_gather(block, dim):
    return jnp.stack([block] + [lax.ppermute(block, AXES, shifted(dim, -by)) for by in (1, 2, 3)])


def gather_all(piece):
    filled = direct_gather(direct_gather(piece, 2), 0)
    half = filled.shape[0] // 2
    ahead = lax.ppermute(filled, AXES, shifted(1, -1))
    behind = lax.ppermute(filled, AXES, shifted(1, 1))
    across = (
        lax.ppermute(ahead[:half], AXES, shifted(1, -1)),
        lax.ppermute(behind[half:], AXES, shifted(1, 1)),
    )
    mine = (filled, ahead, behind) + across
    other = tuple(lax.ppermute(part, AXES, shifted(3, 1)) for part in mine)
    return mine + other


def unpack_kernel(
    buckets,
    place_ref,
    wq_ref,
    wk_ref,
    wv_ref,
    *rest,
):
    parts, (dwq_ref, dwk_ref, dwv_ref, dwo_ref, bias_ref, small_ref, router_ref, gain_grad_ref) = rest[:10], rest[10:18]
    all_s, sems = rest[18:]
    expert = pl.program_id(0)

    @pl.when(expert == 0)
    def _():
        copies = []
        for core in range(2):
            for i in range(5):
                part = parts[5 * core + i]
                half = all_s.shape[2] // 2
                place = (
                    all_s.at[core, (0, 1, 3)[i]]
                    if i < 3
                    else all_s.at[core, 2, pl.ds(half * (i - 3), half)]
                )
                copies.append(pltpu.make_async_copy(part, place, sems.at[5 * core + i]))
        for copy in copies:
            copy.start()
        for copy in copies:
            copy.wait()

    my_x, my_y, my_z, my_core = (place_ref[i] for i in range(4))
    each = dwq_ref.shape[0]
    half = each // 2
    width = dwq_ref.shape[1]
    rel_y = lax.rem(expert // 2 - my_y + 4, 4)

    def rel(context):
        x = context // 8 * 2 + lax.rem(expert, 2)
        return (
            jnp.where(my_core == context % 2, 0, 1),
            rel_y,
            lax.rem(x - my_x + 4, 4),
            lax.rem(context // 2 % 4 - my_z + 4, 4),
        )

    at = each + half
    bias = []
    for j in range(width // 128):
        cols = slice(128 * j, 128 * j + 128)
        one, two = all_s[rel(2 * j)].astype(F32), all_s[rel(2 * j + 1)].astype(F32)
        dwq_ref[:, cols] = jnp.concatenate([one[:each, :64], two[:each, :64]], axis=1)
        dwk_ref[:, cols] = jnp.concatenate([one[:each, 64:], two[:each, 64:]], axis=1)
        dwv_ref[:half, cols] = jnp.concatenate([one[each:at, :64], two[each:at, :64]], axis=1)
        dwv_ref[half:, cols] = jnp.concatenate([one[each:at, 64:], two[each:at, 64:]], axis=1)
        bias += [one[at : at + 1], two[at : at + 1]]
        for i, block in enumerate((one, two)):
            for k in range(width // 128):
                dwo_ref[2 * j + i, :, 128 * k : 128 * k + 128] = block[at + 16 + 8 * k : at + 24 + 8 * k]
    bias_ref[...] = jnp.concatenate(bias, axis=0)[:, :buckets]
    block = all_s[rel(width // 64)].astype(F32)
    small = jnp.concatenate(
        [block[at + 16 + 8 * k : at + 24 + 8 * k] for k in range(width // 128)], axis=1
    )

    @pl.when(expert == 0)
    def _():
        router_ref[...] = small.T

    @pl.when(expert == 1)
    def _():
        small_ref[...] = small

    prod = (
        dwq_ref[...] * wq_ref[...].astype(F32)
        + dwk_ref[...] * wk_ref[...].astype(F32)
        + dwv_ref[...] * wv_ref[...].astype(F32)
    )
    gain_grad_ref[...] = dot(jnp.ones((8, width), F32), prod, NT, HIGHEST)


def unpack(place, parts, w_query, w_key, w_value, heads, buckets, experts):
    width = w_query.shape[0]
    each = width // experts
    held = parts[0].shape[2]
    rows = pl.BlockSpec((each, width), lambda i: (i, 0))
    return pl.pallas_call(
        lambda *refs: unpack_kernel(buckets, *refs),
        name="unpack",
        grid=(experts,),
        out_shape=(
            jax.ShapeDtypeStruct((width, width), F32),
            jax.ShapeDtypeStruct((width, width), F32),
            jax.ShapeDtypeStruct((width, width), F32),
            jax.ShapeDtypeStruct((heads, experts, 8, width), F32),
            jax.ShapeDtypeStruct((heads, buckets), F32),
            jax.ShapeDtypeStruct((8, width), F32),
            jax.ShapeDtypeStruct((width, 8), F32),
            jax.ShapeDtypeStruct((experts, 8, each), F32),
        ),
        in_specs=[sspec(), rows, rows, rows] + [pl.BlockSpec(memory_space=pl.ANY)] * 10,
        out_specs=(
            rows,
            rows,
            rows,
            pl.BlockSpec((heads, None, 8, width), lambda i: (0, i, 0, 0)),
            pl.BlockSpec((heads, buckets), lambda i: (0, 0)),
            pl.BlockSpec((8, width), lambda i: (0, 0)),
            pl.BlockSpec((width, 8), lambda i: (0, 0)),
            pl.BlockSpec((None, 8, each), lambda i: (i, 0, 0)),
        ),
        scratch_shapes=[
            pltpu.VMEM((2, 4, 4, 4, held, 128), BF16),
            pltpu.SemaphoreType.DMA((10,)),
        ],
        compiler_params=whole(),
    )(place, w_query, w_key, w_value, *parts)


def add_kernel(in_ref, out_ref):
    total = in_ref[0].astype(F32)
    for i in range(1, in_ref.shape[0]):
        total = total + in_ref[i].astype(F32)
    out_ref[...] = total.astype(BF16)


def add_up(received):
    return pl.pallas_call(
        add_kernel,
        name="add_up",
        out_shape=jax.ShapeDtypeStruct(received.shape[1:], BF16),
        in_specs=[vspec()],
        out_specs=vspec(),
        compiler_params=whole(),
    )(received)


def split_kernel(in_ref, first_ref, second_ref):
    width = first_ref.shape[1]
    first_ref[0] = in_ref[:, :width].astype(F32).T
    second_ref[0] = in_ref[:, width:].astype(F32).T


def split_back(grads):
    rows, wide = grads.shape
    width = wide // 2
    return pl.pallas_call(
        split_kernel,
        name="split_back",
        out_shape=(jax.ShapeDtypeStruct((1, width, rows), F32),) * 2,
        in_specs=[vspec()],
        out_specs=(vspec(),) * 2,
        compiler_params=whole(),
    )(grads)


def shards(
    tokens,
    gain_one,
    w_query,
    w_key,
    w_value,
    w_out,
    rel_table,
    gain_two,
    w_router,
    expert_in,
    expert_out,
    routes,
    cotangent,
):
    width = tokens.shape[2]
    heads, buckets = rel_table.shape
    experts = lax.axis_size("expert")
    inputs, grad_out, routes_here = tokens[0], cotangent[0], routes[0]
    context = lax.axis_index("context")
    head = jnp.minimum(context, heads - 1).astype(jnp.int32).reshape(1)

    share, packed = project(inputs, gain_one, w_query, w_key, w_value, expert_in, expert_out)
    qkv = lax.all_to_all(packed, "context", split_axis=0, concat_axis=0, tiled=True)
    shared = lax.all_gather(share, "context", axis=0, tiled=False)

    out_heads, keep, lse = attend(head, rel_table, qkv)
    out_rows = lax.all_to_all(out_heads, "context", split_axis=0, concat_axis=0, tiled=True)
    send, attended, mixed, second, picks, gates = dispatch(
        inputs, grad_out, out_rows, w_out, gain_two, w_router, routes_here, experts
    )
    received = lax.all_to_all(send, "expert", split_axis=0, concat_axis=0, tiled=True)
    back, weight_grads = expert_both(received, shared)
    returned = lax.all_to_all(back, "expert", split_axis=0, concat_axis=0, tiled=True)
    own_grads = lax.psum_scatter(weight_grads, "context", scatter_dimension=0, tiled=True)
    block_out, grad_mixed, grad_heads, sums = combine(
        grad_out, returned, picks, gates, mixed, second, attended, routes_here, gain_two, w_router, w_out
    )
    grad_here = lax.all_to_all(grad_heads, "context", split_axis=0, concat_axis=0, tiled=True)
    sums = lax.all_to_all(sums, "context", split_axis=0, concat_axis=0, tiled=True)

    dqkv, bias = attend_back(head, rel_table, qkv, grad_here, keep, lse)
    grads = lax.all_to_all(dqkv, "context", split_axis=0, concat_axis=0, tiled=True)
    terms = head_grads(dqkv, shared, bias, sums, experts)
    terms = lax.all_to_all(terms, "expert", split_axis=0, concat_axis=0, tiled=True)
    parts = gather_all(add_up(terms))
    grad_tokens = input_grad(inputs, gain_one, grads, w_query, w_key, w_value, grad_mixed)

    expert = lax.axis_index("expert")
    place = jnp.stack(coordinates(context * experts + expert)).astype(jnp.int32)
    dwq, dwk, dwv, dwo, bias, small, router, gain_grad = unpack(
        place, parts, w_query, w_key, w_value, heads, buckets, experts
    )
    grad_in, grad_back = split_back(own_grads)
    return (
        block_out[None],
        grad_tokens[None],
        gain_grad[:, 0, :].reshape(width) / gain_one,
        dwq,
        dwk,
        dwv,
        dwo.reshape(width, width),
        bias,
        small[0],
        router,
        grad_in,
        grad_back,
    )


def solution(mesh):
    return jax.shard_map(
        shards,
        mesh=mesh,
        in_specs=(
            P("expert", "context", None),
            P(),
            P(),
            P(),
            P(),
            P(),
            P(),
            P(),
            P(),
            P("expert", None, "context"),
            P("expert", None, "context"),
            P("expert", "context", None),
            P("expert", "context", None),
        ),
        out_specs=(
            P("expert", "context", None),
            P("expert", "context", None),
            P(),
            P(),
            P(),
            P(),
            P(),
            P(),
            P(),
            P(),
            P("expert", None, "context"),
            P("expert", None, "context"),
        ),
        check_vma=False,
    )
```

```python
import math

import jax
import jax.numpy as jnp
from jax import lax
from jax.experimental import pallas as pl
from jax.experimental.pallas import tpu as pltpu
from jax.sharding import PartitionSpec as P

MAX_DIST = 128
EPSILON = 1e-06
NEG_LARGE = -1e30
BLK = 256
HEAD_SLOTS = 16

F32 = jnp.float32
BF16 = jnp.bfloat16
HIGHEST = lax.Precision.HIGHEST

NN = (((1,), (0,)), ((), ()))
NT = (((1,), (1,)), ((), ()))
TN = (((0,), (0,)), ((), ()))


def dot(a, b, dims=NN, precision=None):
    return lax.dot_general(a, b, dims, precision=precision, preferred_element_type=F32)


def bucket_starts(buckets, far_reach):
    span = buckets // 2
    rest = [
        int(math.ceil(span * (far_reach / span) ** (step / (buckets - span))))
        for step in range(1, buckets - span)
    ]
    return list(range(span + 1)) + rest


def rms_scale(values):
    return lax.rsqrt(jnp.mean(values * values, axis=-1, keepdims=True) + EPSILON)


def norm_back(values, inv_root, gain_vec, grad_normed):
    weighted = grad_normed * gain_vec
    cubed = inv_root * inv_root * inv_root
    return inv_root * weighted - values * cubed * jnp.mean(
        weighted * values, axis=-1, keepdims=True
    )


def whole(vmem_mib=56):
    return pltpu.CompilerParams(vmem_limit_bytes=vmem_mib * 2**20)


def vspec():
    return pl.BlockSpec(memory_space=pltpu.VMEM)


def sspec():
    return pl.BlockSpec(memory_space=pltpu.SMEM)


def project_kernel(tok_ref, gain_ref, wq_ref, wk_ref, wv_ref, normed_ref, out_ref):
    inputs = tok_ref[...].astype(F32)
    normed = (inputs * rms_scale(inputs) * gain_ref[...][None, :]).astype(BF16)
    rows, width = normed.shape
    half = rows // 2
    normed_ref[...] = normed
    queries = (dot(normed, wq_ref[...]).astype(BF16).astype(F32) * 0.125).astype(BF16)
    keys = dot(normed, wk_ref[...]).astype(BF16)
    values = dot(normed, wv_ref[...]).astype(BF16)
    heads = width // 64
    for h in range(heads):
        cols = slice(64 * h, 64 * h + 64)
        out_ref[h, :rows, :] = jnp.concatenate([queries[:, cols], keys[:, cols]], axis=1)
        out_ref[h, rows:, :] = jnp.concatenate([values[:half, cols], values[half:, cols]], axis=1)
    for h in range(heads, HEAD_SLOTS):
        out_ref[h] = jnp.zeros_like(out_ref[h])


def project(tokens, gain_one, w_query, w_key, w_value):
    rows, width = tokens.shape
    return pl.pallas_call(
        project_kernel,
        name="project",
        out_shape=(
            jax.ShapeDtypeStruct((rows, width), BF16),
            jax.ShapeDtypeStruct((HEAD_SLOTS, rows + rows // 2, 128), BF16),
        ),
        in_specs=[vspec()] * 5,
        out_specs=(vspec(), vspec()),
        compiler_params=whole(),
    )(tokens, gain_one, w_query, w_key, w_value)


def bias_tile(table_ref, head, buckets, rows_first, shape, key_dim):
    sign = [1, -1] if key_dim == 1 else [-1, 1]
    dist = (
        rows_first
        + sign[0] * lax.broadcasted_iota(jnp.int32, shape, 0)
        + sign[1] * lax.broadcasted_iota(jnp.int32, shape, 1)
    )
    far = table_ref[head, buckets - 1]
    tile = jnp.full(shape, NEG_LARGE, F32)
    for b, start in enumerate(bucket_starts(buckets, MAX_DIST)):
        tile = jnp.where(dist >= start, table_ref[head, b] - far, tile)
    return tile


def unpack_qkv(qkv_ref, q_s, k_s, v_s, ones_lane):
    count = qkv_ref.shape[0]
    lane = lax.broadcasted_iota(jnp.int32, (64, 64), 1)
    one = jnp.where(lane == 0, 1.0, 0.0).astype(BF16)
    for c in range(count):
        pair = qkv_ref[c, :128, :]
        q_s[128 * c : 128 * c + 128, :] = pair[:, :64]
        k_s[128 * c : 128 * c + 128, :] = pair[:, 64:]
        two = qkv_ref[c, 128:192, :]
        top, bottom = two[:, :64], two[:, 64:]
        if ones_lane:
            top = jnp.concatenate([top, one], axis=1)
            bottom = jnp.concatenate([bottom, one], axis=1)
        v_s[128 * c : 128 * c + 64, :] = top
        v_s[128 * c + 64 : 128 * c + 128, :] = bottom


def attend_kernel(buckets, head_ref, table_ref, qkv_ref, out_ref, keep_ref, lse_ref, q_s, k_s, v_s, bias_s):
    head = head_ref[0]
    unpack_qkv(qkv_ref, q_s, k_s, v_s, True)
    bias_s[0] = bias_tile(table_ref, head, buckets, BLK, (BLK, BLK), 1)
    bias_s[1] = bias_tile(table_ref, head, buckets, 0, (BLK, BLK), 1)
    blocks = q_s.shape[0] // BLK

    for qb in range(blocks):
        query = q_s[BLK * qb : BLK * qb + BLK, :]
        near = max(qb - 1, 0) * BLK
        parts = []
        if near:
            parts.append((0, dot(query, k_s[:near, :], NT)))
        if qb:
            parts.append((near, dot(query, k_s[near : near + BLK, :], NT) + bias_s[0]))
        parts.append((BLK * qb, dot(query, k_s[BLK * qb : BLK * qb + BLK, :], NT) + bias_s[1]))
        top = parts[-1][1]
        top = jnp.maximum(top[:, :128], top[:, 128:])
        for unused, scores in parts[:-1]:
            for j in range(scores.shape[1] // 128):
                top = jnp.maximum(top, scores[:, 128 * j : 128 * j + 128])
        top = jnp.max(top, axis=1, keepdims=True)
        total = jnp.zeros((BLK, 128), F32)
        for first, scores in parts:
            weights = jnp.exp(scores - top).astype(BF16)
            total = total + dot(weights, v_s[first : first + scores.shape[1], :])
        norm = total[:, 64:65]
        out = total[:, :64] / norm
        log_total = top + jnp.log(norm)
        spread = jnp.broadcast_to(log_total, (BLK, 128)).T
        lse_ref[qb] = spread[:8, :]
        for part in range(BLK // 128):
            two = jnp.concatenate(
                [out[128 * part : 128 * part + 64], out[128 * part + 64 : 128 * part + 128]], axis=1
            )
            place = qb * (BLK // 128) + part
            out_ref[place] = two.astype(BF16)
            keep_ref[place] = two


def attend(head, rel_table, qkv):
    count = qkv.shape[0]
    length = 128 * count
    blocks = length // BLK
    return pl.pallas_call(
        lambda *refs: attend_kernel(rel_table.shape[1], *refs),
        name="attend",
        out_shape=(
            jax.ShapeDtypeStruct((count, 64, 128), BF16),
            jax.ShapeDtypeStruct((count, 64, 128), F32),
            jax.ShapeDtypeStruct((blocks, 8, BLK), F32),
        ),
        in_specs=[sspec(), sspec(), vspec()],
        out_specs=(vspec(), vspec(), vspec()),
        scratch_shapes=[
            pltpu.VMEM((length, 64), BF16),
            pltpu.VMEM((length, 64), BF16),
            pltpu.VMEM((length, 128), BF16),
            pltpu.VMEM((2, BLK, BLK), F32),
        ],
        compiler_params=whole(),
    )(head, rel_table, qkv)


def attend_back_kernel(
    buckets,
    head_ref,
    table_ref,
    qkv_ref,
    go_ref,
    keep_ref,
    lse_ref,
    dqkv_ref,
    bias_ref,
    q_s,
    k_s,
    v_s,
    kt_s,
    go_s,
    delta_s,
    dq_s,
    dk_s,
    dv_s,
    bias_s,
    acc_s,
):
    head = head_ref[0]
    length = q_s.shape[0]
    count = qkv_ref.shape[0]
    blocks = length // BLK
    unpack_qkv(qkv_ref, q_s, k_s, v_s, False)
    ones = jnp.ones((8, 64), F32)
    for c in range(count):
        kt_s[:, 128 * c : 128 * c + 128] = k_s[128 * c : 128 * c + 128, :].T
        two, kept = go_ref[c], keep_ref[c]
        go_s[128 * c : 128 * c + 64, :] = two[:, :64]
        go_s[128 * c + 64 : 128 * c + 128, :] = two[:, 64:]
        both = two.astype(F32) * kept
        prod = jnp.concatenate([both[:, :64], both[:, 64:]], axis=0)
        delta_s[:, 128 * c : 128 * c + 128] = dot(ones, prod, NT, HIGHEST)
    bias_s[0] = bias_tile(table_ref, head, buckets, BLK, (BLK, BLK), 0)
    bias_s[1] = bias_tile(table_ref, head, buckets, 0, (BLK, BLK), 0)
    acc_s[...] = jnp.zeros_like(acc_s)
    dk_s[...] = jnp.zeros_like(dk_s)
    dv_s[...] = jnp.zeros_like(dv_s)

    far_sum = jnp.zeros((8, BLK), F32)
    for qb in range(blocks):
        rows = slice(BLK * qb, BLK * qb + BLK)
        query, grad = q_s[rows, :], go_s[rows, :]
        lse = lse_ref[qb][:1, :]
        delta = delta_s[:1, rows]
        grad_query = jnp.zeros((64, BLK), F32)
        for kb in range(qb + 1):
            cols = slice(BLK * kb, BLK * kb + BLK)
            near = kb - qb + 1
            scores = dot(k_s[cols, :], query, NT)
            if near >= 0:
                scores = scores + bias_s[near]
            probs = jnp.exp(scores - lse)
            grad_probs = dot(v_s[cols, :], grad, NT)
            grad_scores = (probs * (grad_probs - delta)).astype(BF16)
            dv_s[cols, :] += dot(probs.astype(BF16), grad)
            dk_s[cols, :] += dot(grad_scores, query)
            grad_query = grad_query + dot(kt_s[:, cols], grad_scores)
            wide = grad_scores.astype(F32)
            if near < 0:
                far_sum = far_sum + jnp.sum(wide.reshape(BLK // 8, 8, BLK), axis=0)
            else:
                acc_s[near] += wide
        dq_s[:, rows] = grad_query

    for c in range(count):
        here = slice(128 * c, 128 * c + 128)
        dq_t = (dq_s[:, here] * 0.125).astype(BF16)
        dk = dk_s[here, :].astype(BF16)
        dv = dv_s[here, :].astype(BF16)
        dqkv_ref[c, :128, :] = jnp.concatenate([dq_t.T, dk], axis=1)
        dqkv_ref[c, 128:192, :] = jnp.concatenate([dv[:64], dv[64:]], axis=1)

    lane = lax.broadcasted_iota(jnp.int32, (16, 128), 1)
    dist0 = (
        BLK
        - lax.broadcasted_iota(jnp.int32, (BLK, BLK), 0)
        + lax.broadcasted_iota(jnp.int32, (BLK, BLK), 1)
    )
    dist1 = dist0 - BLK

    def total(values):
        return jnp.sum(jnp.sum(values, axis=1, keepdims=True), axis=0, keepdims=True)

    starts = bucket_starts(buckets, MAX_DIST)
    row = jnp.zeros((16, 128), F32)
    above = None
    for b in reversed(range(buckets)):
        reach = total(
            jnp.where(dist0 >= starts[b], acc_s[0], 0.0)
            + jnp.where(dist1 >= starts[b], acc_s[1], 0.0)
        )
        mine = reach + total(far_sum) if b == buckets - 1 else reach - above
        above = reach
        row = jnp.where(lane == b, mine, row)
    bias_ref[...] = row


def attend_back(head, rel_table, qkv, grad_heads, keep, lse):
    count = qkv.shape[0]
    length = 128 * count
    return pl.pallas_call(
        lambda *refs: attend_back_kernel(rel_table.shape[1], *refs),
        name="attend_back",
        out_shape=(
            jax.ShapeDtypeStruct(qkv.shape, BF16),
            jax.ShapeDtypeStruct((16, 128), F32),
        ),
        in_specs=[sspec(), sspec()] + [vspec()] * 4,
        out_specs=(vspec(), vspec()),
        scratch_shapes=[
            pltpu.VMEM((length, 64), BF16),
            pltpu.VMEM((length, 64), BF16),
            pltpu.VMEM((length, 64), BF16),
            pltpu.VMEM((64, length), BF16),
            pltpu.VMEM((length, 64), BF16),
            pltpu.VMEM((8, length), F32),
            pltpu.VMEM((64, length), F32),
            pltpu.VMEM((length, 64), F32),
            pltpu.VMEM((length, 64), F32),
            pltpu.VMEM((2, BLK, BLK), F32),
            pltpu.VMEM((2, BLK, BLK), F32),
        ],
        compiler_params=whole(),
    )(head, rel_table, qkv, grad_heads, keep, lse)


def head_grads_kernel(dqkv_ref, normed_ref, bias_ref, sums_ref, out_ref):
    count = dqkv_ref.shape[0]
    width = normed_ref.shape[2]
    tokens = count * 64
    first = normed_ref[:, :64, :].reshape(tokens, width)
    second = normed_ref[:, 64:, :].reshape(tokens, width)
    pairs = dot(dqkv_ref[:, :64, :].reshape(tokens, 128), first, TN) + dot(
        dqkv_ref[:, 64:128, :].reshape(tokens, 128), second, TN
    )
    two = dqkv_ref[:, 128:192, :].reshape(tokens, 128)
    third = dot(two, first, TN)[:64] + dot(two, second, TN)[64:]
    pairs, third = pairs.T, third.T
    total = sums_ref[0].astype(F32)
    for c in range(1, count):
        total = total + sums_ref[c].astype(F32)
    shares = out_ref.shape[0]
    each = width // shares
    row = bias_ref[...].astype(BF16)
    for s in range(shares):
        mine = slice(each * s, each * s + each)
        out_ref[s, :each, :] = pairs[mine].astype(BF16)
        last = third[mine].astype(BF16)
        out_ref[s, each : each + each // 2, :] = jnp.concatenate(
            [last[: each // 2], last[each // 2 :]], axis=1
        )
        at = each + each // 2
        out_ref[s, at : at + 16, :] = row
        part = total[8 * s : 8 * s + 8]
        out_ref[s, at + 16 :, :] = jnp.concatenate(
            [part[:, 128 * j : 128 * j + 128] for j in range(width // 128)], axis=0
        ).astype(BF16)


def head_grads(dqkv, normed_all, bias, sums, shares):
    width = normed_all.shape[2]
    each = width // shares
    held = each + each // 2 + 16 + width // 16
    return pl.pallas_call(
        head_grads_kernel,
        name="head_grads",
        out_shape=jax.ShapeDtypeStruct((shares, held, 128), BF16),
        in_specs=[vspec()] * 4,
        out_specs=vspec(),
        compiler_params=whole(),
    )(dqkv, normed_all, bias, sums)


def heads_to_rows(ref, scratch):
    for j in range(scratch.shape[1] // 128):
        one, two = ref[2 * j], ref[2 * j + 1]
        scratch[:64, 128 * j : 128 * j + 128] = jnp.concatenate([one[:, :64], two[:, :64]], axis=1)
        scratch[64:, 128 * j : 128 * j + 128] = jnp.concatenate([one[:, 64:], two[:, 64:]], axis=1)


def dispatch_kernel(
    experts,
    capacity,
    tok_ref,
    cot_ref,
    heads_ref,
    wo_ref,
    gain_ref,
    wr_ref,
    routes_ref,
    send_ref,
    att_ref,
    mixed_ref,
    second_ref,
    pick_ref,
    gates_ref,
):
    rows = tok_ref.shape[0]
    heads_to_rows(heads_ref, att_ref)
    mixed = tok_ref[...].astype(F32) + dot(att_ref[...], wo_ref[...])
    mixed_ref[...] = mixed
    second = (mixed * rms_scale(mixed) * gain_ref[...][None, :]).astype(BF16)
    second_ref[...] = second
    logits = dot(second, wr_ref[...])
    ids = lax.broadcasted_iota(jnp.int32, (rows, experts), 1)
    routes = routes_ref[...]
    marks = [(routes[:, k : k + 1] == ids).astype(F32) for k in range(2)]
    earlier = (
        lax.broadcasted_iota(jnp.int32, (rows, rows), 0)
        > lax.broadcasted_iota(jnp.int32, (rows, rows), 1)
    ).astype(F32)
    ranks = dot(earlier.astype(BF16), (marks[0] + marks[1]).astype(BF16))
    chosen = [jnp.sum(m * logits, axis=1, keepdims=True) for m in marks]
    top = jnp.maximum(chosen[0], chosen[1])
    exps = [jnp.exp(c - top) for c in chosen]
    gates = [e / (exps[0] + exps[1]) for e in exps]
    slot_ids = lax.broadcasted_iota(jnp.int32, (rows, experts * capacity), 1)
    grad_out = cot_ref[...].astype(F32)
    picks = []
    for k in range(2):
        slot = jnp.sum(marks[k] * ranks, axis=1, keepdims=True).astype(jnp.int32)
        place = routes[:, k : k + 1] * capacity + slot
        picks.append((place == slot_ids).astype(F32).astype(BF16))
        pick_ref[k] = picks[k]
    send_rows = dot(picks[0] + picks[1], second, TN).astype(BF16)
    send_grads = dot(picks[0], (gates[0] * grad_out).astype(BF16), TN) + dot(
        picks[1], (gates[1] * grad_out).astype(BF16), TN
    )
    send_grads = send_grads.astype(BF16)
    for e in range(experts):
        here = slice(capacity * e, capacity * e + capacity)
        send_ref[e, :capacity, :] = send_rows[here]
        send_ref[e, capacity:, :] = send_grads[here]
    lane = lax.broadcasted_iota(jnp.int32, (rows, 128), 1)
    gates_ref[...] = jnp.where(lane == 0, gates[0], gates[1])


def dispatch(tokens, cotangent, heads, w_out, gain_two, w_router, routes, experts):
    rows, width = tokens.shape
    capacity = 3 * rows // experts
    return pl.pallas_call(
        lambda *refs: dispatch_kernel(experts, capacity, *refs),
        name="dispatch",
        out_shape=(
            jax.ShapeDtypeStruct((experts, 2 * capacity, width), BF16),
            jax.ShapeDtypeStruct((rows, width), BF16),
            jax.ShapeDtypeStruct((rows, width), F32),
            jax.ShapeDtypeStruct((rows, width), BF16),
            jax.ShapeDtypeStruct((2, rows, experts * capacity), BF16),
            jax.ShapeDtypeStruct((rows, 128), F32),
        ),
        in_specs=[vspec()] * 7,
        out_specs=(vspec(),) * 6,
        compiler_params=whole(),
    )(tokens, cotangent, heads, w_out, gain_two, w_router, routes)


def expert_kernel(rows_ref, w_ref, back_ref, dw_ref, x_s, g_s, y_s, dx_s):
    step = pl.program_id(0)
    sources, both, width = rows_ref.shape
    capacity = both // 2

    @pl.when(step == 0)
    def _():
        for s in range(sources):
            x_s[capacity * s : capacity * s + capacity, :] = rows_ref[s, :capacity, :]
            g_s[capacity * s : capacity * s + capacity, :] = rows_ref[s, capacity:, :]
        y_s[...] = jnp.zeros_like(y_s)
        dx_s[...] = jnp.zeros_like(dx_s)

    each = w_ref.shape[1] // 2
    w_in = w_ref[:, :each, :].reshape(-1, width)
    w_back = w_ref[:, each:, :].reshape(-1, width)
    pre = dot(x_s[...], w_in, NT)
    square = pre * pre
    curve = jnp.tanh(0.7978845608 * (pre + 0.044715 * square * pre))
    act = (0.5 * pre * (1.0 + curve)).astype(BF16)
    slope = 0.5 * (1.0 + curve) + 0.5 * pre * (1.0 - curve * curve) * (
        0.7978845608 * (1.0 + 3.0 * 0.044715 * square)
    )
    grad_pre = (dot(g_s[...], w_back, NT) * slope).astype(BF16)
    y_s[...] += dot(act, w_back)
    dx_s[...] += dot(grad_pre, w_in)
    dw_ref[:, :each, :] = dot(grad_pre, x_s[...], TN).astype(BF16).reshape(-1, each, width)
    dw_ref[:, each:, :] = dot(act, g_s[...], TN).astype(BF16).reshape(-1, each, width)

    @pl.when(step == pl.num_programs(0) - 1)
    def _():
        for s in range(sources):
            here = slice(capacity * s, capacity * s + capacity)
            back_ref[s, :capacity, :] = y_s[here, :].astype(BF16)
            back_ref[s, capacity:, :] = dx_s[here, :].astype(BF16)


AT_ONCE = 2


def expert_both(rows, shared):
    sources, both, width = rows.shape
    count, given, unused = shared.shape
    held = sources * both // 2
    return pl.pallas_call(
        expert_kernel,
        name="expert_both",
        grid=(count // AT_ONCE,),
        out_shape=(
            jax.ShapeDtypeStruct(rows.shape, BF16),
            jax.ShapeDtypeStruct(shared.shape, BF16),
        ),
        in_specs=[
            pl.BlockSpec(rows.shape, lambda i: (0, 0, 0)),
            pl.BlockSpec((AT_ONCE, given, width), lambda i: (i, 0, 0)),
        ],
        out_specs=(
            pl.BlockSpec(rows.shape, lambda i: (0, 0, 0)),
            pl.BlockSpec((AT_ONCE, given, width), lambda i: (i, 0, 0)),
        ),
        scratch_shapes=[
            pltpu.VMEM((held, width), BF16),
            pltpu.VMEM((held, width), BF16),
            pltpu.VMEM((held, width), F32),
            pltpu.VMEM((held, width), F32),
        ],
        compiler_params=whole(),
    )(rows, shared)


def combine_kernel(
    cot_ref,
    back_ref,
    pick_ref,
    gates_ref,
    mixed_ref,
    second_ref,
    routes_ref,
    gain_ref,
    wr_ref,
    wo_ref,
    out_ref,
    grad_mixed_ref,
    heads_ref,
    small_ref,
    y_s,
    dx_s,
):
    experts, both, width = back_ref.shape
    capacity = both // 2
    rows = cot_ref.shape[0]
    for s in range(experts):
        here = slice(capacity * s, capacity * s + capacity)
        y_s[here, :] = back_ref[s, :capacity, :]
        dx_s[here, :] = back_ref[s, capacity:, :]
    grad_out = cot_ref[...].astype(F32)
    mixed = mixed_ref[...]
    gates = [gates_ref[:, k : k + 1] for k in range(2)]
    picked = [dot(pick_ref[k], y_s[...]) for k in range(2)]
    out_ref[...] = (mixed + (gates[0] * picked[0] + gates[1] * picked[1])).astype(BF16)
    grad_gates = [jnp.sum(p * grad_out, axis=1, keepdims=True) for p in picked]
    mean = gates[0] * grad_gates[0] + gates[1] * grad_gates[1]
    grad_chosen = [gates[k] * (grad_gates[k] - mean) for k in range(2)]
    ids = lax.broadcasted_iota(jnp.int32, (rows, experts), 1)
    routes = routes_ref[...]
    grad_logits = jnp.where(routes[:, :1] == ids, grad_chosen[0], 0.0) + jnp.where(
        routes[:, 1:2] == ids, grad_chosen[1], 0.0
    )
    grad_second = dot(pick_ref[0], dx_s[...]) + dot(pick_ref[1], dx_s[...])
    grad_second = grad_second + dot(grad_logits, wr_ref[...].astype(F32), NT, HIGHEST)
    second = second_ref[...]
    grad_router = dot(grad_logits, second.astype(F32), TN, HIGHEST)
    scale = rms_scale(mixed)
    grad_gain = jnp.sum(grad_second * mixed * scale, axis=0, keepdims=True)
    grad_mixed = grad_out + norm_back(mixed, scale, gain_ref[...][None, :], grad_second)
    grad_mixed_ref[...] = grad_mixed
    grad_branch = grad_mixed.astype(BF16)
    grad_att = dot(grad_branch, wo_ref[...], NT).astype(BF16)
    heads = width // 64
    for h in range(heads):
        cols = slice(64 * h, 64 * h + 64)
        heads_ref[h] = jnp.concatenate([grad_att[:64, cols], grad_att[64:, cols]], axis=1)
    for h in range(heads, HEAD_SLOTS):
        heads_ref[h] = jnp.zeros_like(heads_ref[h])
    small_ref[...] = jnp.concatenate([grad_router, jnp.broadcast_to(grad_gain, (8, width))], axis=0)


def out_grad_kernel(att_ref, grad_mixed_ref, small_ref, sums_ref):
    grad_wo = dot(att_ref[...], grad_mixed_ref[...].astype(BF16), TN).astype(BF16)
    slots, each, width = sums_ref.shape
    used = width // each
    for c in range(used):
        sums_ref[c] = grad_wo[each * c : each * c + each]
    for c in range(used, slots):
        sums_ref[c] = jnp.zeros_like(sums_ref[c])
    sums_ref[used, :16, :] = small_ref[...].astype(BF16)


def out_grad(attended, grad_mixed, small):
    width = attended.shape[1]
    return pl.pallas_call(
        out_grad_kernel,
        name="out_grad",
        out_shape=jax.ShapeDtypeStruct((HEAD_SLOTS, 64, width), BF16),
        in_specs=[vspec()] * 3,
        out_specs=vspec(),
        compiler_params=whole(),
    )(attended, grad_mixed, small)


def combine(cotangent, back, picks, gates, mixed, second, routes, gain_two, w_router, w_out):
    rows, width = cotangent.shape
    experts, both, unused = back.shape
    held = experts * both // 2
    return pl.pallas_call(
        combine_kernel,
        name="combine",
        out_shape=(
            jax.ShapeDtypeStruct((rows, width), BF16),
            jax.ShapeDtypeStruct((rows, width), F32),
            jax.ShapeDtypeStruct((HEAD_SLOTS, rows // 2, 128), BF16),
            jax.ShapeDtypeStruct((16, width), F32),
        ),
        in_specs=[vspec()] * 10,
        out_specs=(vspec(),) * 4,
        scratch_shapes=[pltpu.VMEM((held, width), BF16), pltpu.VMEM((held, width), BF16)],
        compiler_params=whole(),
    )(
        cotangent,
        back,
        picks,
        gates,
        mixed,
        second,
        routes,
        gain_two,
        w_router,
        w_out,
    )


def input_grad_kernel(tok_ref, gain_ref, grads_ref, wq_ref, wk_ref, wv_ref, mixed_ref, out_ref, dq_s, dk_s, dv_s):
    for j in range(dq_s.shape[1] // 128):
        cols = slice(128 * j, 128 * j + 128)
        one, two = grads_ref[2 * j], grads_ref[2 * j + 1]
        dq_s[:, cols] = jnp.concatenate([one[:128, :64], two[:128, :64]], axis=1)
        dk_s[:, cols] = jnp.concatenate([one[:128, 64:], two[:128, 64:]], axis=1)
        dv_s[:64, cols] = jnp.concatenate([one[128:, :64], two[128:, :64]], axis=1)
        dv_s[64:, cols] = jnp.concatenate([one[128:, 64:], two[128:, 64:]], axis=1)
    grad_normed = dot(dq_s[...], wq_ref[...], NT)
    grad_normed = grad_normed + dot(dk_s[...], wk_ref[...], NT)
    grad_normed = grad_normed + dot(dv_s[...], wv_ref[...], NT)
    inputs = tok_ref[...].astype(F32)
    out_ref[...] = mixed_ref[...] + norm_back(inputs, rms_scale(inputs), gain_ref[...][None, :], grad_normed)


def input_grad(tokens, gain_one, grads, w_query, w_key, w_value, grad_mixed):
    rows, width = tokens.shape
    return pl.pallas_call(
        input_grad_kernel,
        name="input_grad",
        out_shape=jax.ShapeDtypeStruct((rows, width), F32),
        in_specs=[vspec()] * 7,
        out_specs=vspec(),
        scratch_shapes=[pltpu.VMEM((rows, width), BF16)] * 3,
        compiler_params=whole(),
    )(tokens, gain_one, grads, w_query, w_key, w_value, grad_mixed)


def coordinates(index):
    context, expert = index // 8, index % 8
    return (context // 8 * 2 + expert % 2, expert // 2, context // 2 % 4, context % 2)


def device_at(x, y, z, core):
    return ((x // 2 * 4 + z) * 2 + core) * 8 + y * 2 + x % 2


def shifted(dim, by):
    pairs = []
    for index in range(128):
        place = list(coordinates(index))
        place[dim] = (place[dim] + by) % (2 if dim == 3 else 4)
        pairs.append((index, device_at(*place)))
    return pairs


AXES = ("context", "expert")


def direct_gather(block, dim):
    return jnp.stack([block] + [lax.ppermute(block, AXES, shifted(dim, -by)) for by in (1, 2, 3)])


def gather_all(piece, beside):
    filled, beside = lax.optimization_barrier((direct_gather(piece, 2), beside))
    filled = direct_gather(filled, 0)
    half = filled.shape[0] // 2
    ahead = lax.ppermute(filled, AXES, shifted(1, -1))
    behind = lax.ppermute(filled, AXES, shifted(1, 1))
    across = (
        lax.ppermute(ahead[:half], AXES, shifted(1, -1)),
        lax.ppermute(behind[half:], AXES, shifted(1, 1)),
    )
    mine = (filled, ahead, behind) + across
    other = tuple(lax.ppermute(part, AXES, shifted(3, 1)) for part in mine)
    return mine + other, beside


def unpack_kernel(
    buckets,
    place_ref,
    wq_ref,
    wk_ref,
    wv_ref,
    *rest,
):
    parts, (dwq_ref, dwk_ref, dwv_ref, dwo_ref, bias_ref, small_ref, router_ref, gain_grad_ref) = rest[:10], rest[10:18]
    all_s, sems = rest[18:]
    expert = pl.program_id(0)

    @pl.when(expert == 0)
    def _():
        copies = []
        for core in range(2):
            for i in range(5):
                part = parts[5 * core + i]
                half = all_s.shape[2] // 2
                place = (
                    all_s.at[core, (0, 1, 3)[i]]
                    if i < 3
                    else all_s.at[core, 2, pl.ds(half * (i - 3), half)]
                )
                copies.append(pltpu.make_async_copy(part, place, sems.at[5 * core + i]))
        for copy in copies:
            copy.start()
        for copy in copies:
            copy.wait()

    my_x, my_y, my_z, my_core = (place_ref[i] for i in range(4))
    each = dwq_ref.shape[0]
    half = each // 2
    width = dwq_ref.shape[1]
    rel_y = lax.rem(expert // 2 - my_y + 4, 4)

    def rel(context):
        x = context // 8 * 2 + lax.rem(expert, 2)
        return (
            jnp.where(my_core == context % 2, 0, 1),
            rel_y,
            lax.rem(x - my_x + 4, 4),
            lax.rem(context // 2 % 4 - my_z + 4, 4),
        )

    at = each + half
    bias = []
    for j in range(width // 128):
        cols = slice(128 * j, 128 * j + 128)
        one, two = all_s[rel(2 * j)].astype(F32), all_s[rel(2 * j + 1)].astype(F32)
        dwq_ref[:, cols] = jnp.concatenate([one[:each, :64], two[:each, :64]], axis=1)
        dwk_ref[:, cols] = jnp.concatenate([one[:each, 64:], two[:each, 64:]], axis=1)
        dwv_ref[:half, cols] = jnp.concatenate([one[each:at, :64], two[each:at, :64]], axis=1)
        dwv_ref[half:, cols] = jnp.concatenate([one[each:at, 64:], two[each:at, 64:]], axis=1)
        bias += [one[at : at + 1], two[at : at + 1]]
        for i, block in enumerate((one, two)):
            for k in range(width // 128):
                dwo_ref[2 * j + i, :, 128 * k : 128 * k + 128] = block[at + 16 + 8 * k : at + 24 + 8 * k]
    bias_ref[...] = jnp.concatenate(bias, axis=0)[:, :buckets]
    block = all_s[rel(width // 64)].astype(F32)
    small = jnp.concatenate(
        [block[at + 16 + 8 * k : at + 24 + 8 * k] for k in range(width // 128)], axis=1
    )

    @pl.when(expert == 0)
    def _():
        router_ref[...] = small

    @pl.when(expert == 1)
    def _():
        small_ref[...] = small

    prod = (
        dwq_ref[...] * wq_ref[...].astype(F32)
        + dwk_ref[...] * wk_ref[...].astype(F32)
        + dwv_ref[...] * wv_ref[...].astype(F32)
    )
    gain_grad_ref[...] = dot(jnp.ones((8, width), F32), prod, NT, HIGHEST)


def unpack(place, parts, w_query, w_key, w_value, heads, buckets, experts):
    width = w_query.shape[0]
    each = width // experts
    held = parts[0].shape[2]
    rows = pl.BlockSpec((each, width), lambda i: (i, 0))
    return pl.pallas_call(
        lambda *refs: unpack_kernel(buckets, *refs),
        name="unpack",
        grid=(experts,),
        out_shape=(
            jax.ShapeDtypeStruct((width, width), F32),
            jax.ShapeDtypeStruct((width, width), F32),
            jax.ShapeDtypeStruct((width, width), F32),
            jax.ShapeDtypeStruct((heads, experts, 8, width), F32),
            jax.ShapeDtypeStruct((heads, buckets), F32),
            jax.ShapeDtypeStruct((8, width), F32),
            jax.ShapeDtypeStruct((8, width), F32),
            jax.ShapeDtypeStruct((experts, 8, each), F32),
        ),
        in_specs=[sspec(), rows, rows, rows] + [pl.BlockSpec(memory_space=pl.ANY)] * 10,
        out_specs=(
            rows,
            rows,
            rows,
            pl.BlockSpec((heads, None, 8, width), lambda i: (0, i, 0, 0)),
            pl.BlockSpec((heads, buckets), lambda i: (0, 0)),
            pl.BlockSpec((8, width), lambda i: (0, 0)),
            pl.BlockSpec((8, width), lambda i: (0, 0)),
            pl.BlockSpec((None, 8, each), lambda i: (i, 0, 0)),
        ),
        scratch_shapes=[
            pltpu.VMEM((2, 4, 4, 4, held, 128), BF16),
            pltpu.SemaphoreType.DMA((10,)),
        ],
        compiler_params=whole(),
    )(place, w_query, w_key, w_value, *parts)


def add_kernel(in_ref, out_ref):
    total = in_ref[0].astype(F32)
    for i in range(1, in_ref.shape[0]):
        total = total + in_ref[i].astype(F32)
    out_ref[...] = total.astype(BF16)


def add_up(received):
    return pl.pallas_call(
        add_kernel,
        name="add_up",
        out_shape=jax.ShapeDtypeStruct(received.shape[1:], BF16),
        in_specs=[vspec()],
        out_specs=vspec(),
        compiler_params=whole(),
    )(received)


def shards(
    tokens,
    gain_one,
    w_query,
    w_key,
    w_value,
    w_out,
    rel_table,
    gain_two,
    w_router,
    expert_in,
    expert_out,
    routes,
    cotangent,
):
    width = tokens.shape[2]
    heads, buckets = rel_table.shape
    experts = lax.axis_size("expert")
    inputs, grad_out, routes_here = tokens[0], cotangent[0], routes[0]
    context = lax.axis_index("context")
    head = jnp.minimum(context, heads - 1).astype(jnp.int32).reshape(1)

    own_weights = jnp.concatenate([expert_in[0].T, expert_out[0].T], axis=0)
    shared = lax.all_gather(own_weights, "context", axis=0, tiled=False)
    normed, packed = project(inputs, gain_one, w_query, w_key, w_value)
    qkv = lax.all_to_all(packed, "context", split_axis=0, concat_axis=0, tiled=True)
    normed_all = lax.all_gather(normed, "context", axis=0, tiled=False)

    out_heads, keep, lse = attend(head, rel_table, qkv)
    out_rows = lax.all_to_all(out_heads, "context", split_axis=0, concat_axis=0, tiled=True)
    send, attended, mixed, second, picks, gates = dispatch(
        inputs, grad_out, out_rows, w_out, gain_two, w_router, routes_here, experts
    )
    received = lax.all_to_all(send, "expert", split_axis=0, concat_axis=0, tiled=True)
    back, weight_grads = expert_both(received, shared)
    returned = lax.all_to_all(back, "expert", split_axis=0, concat_axis=0, tiled=True)
    own_grads = lax.psum_scatter(weight_grads, "context", scatter_dimension=0, tiled=False)
    block_out, grad_mixed, grad_heads, small = combine(
        grad_out, returned, picks, gates, mixed, second, routes_here, gain_two, w_router, w_out
    )
    sums = out_grad(attended, grad_mixed, small)
    grad_here = lax.all_to_all(grad_heads, "context", split_axis=0, concat_axis=0, tiled=True)
    sums = lax.all_to_all(sums, "context", split_axis=0, concat_axis=0, tiled=True)

    dqkv, bias = attend_back(head, rel_table, qkv, grad_here, keep, lse)
    grads = lax.all_to_all(dqkv, "context", split_axis=0, concat_axis=0, tiled=True)
    terms = head_grads(dqkv, normed_all, bias, sums, experts)
    terms = lax.all_to_all(terms, "expert", split_axis=0, concat_axis=0, tiled=True)
    parts, grads = gather_all(add_up(terms), grads)
    grad_tokens = input_grad(inputs, gain_one, grads, w_query, w_key, w_value, grad_mixed)

    expert = lax.axis_index("expert")
    place = jnp.stack(coordinates(context * experts + expert)).astype(jnp.int32)
    dwq, dwk, dwv, dwo, bias, small, router, gain_grad = unpack(
        place, parts, w_query, w_key, w_value, heads, buckets, experts
    )
    own_grads = own_grads.astype(F32)
    hidden = own_grads.shape[0] // 2
    return (
        block_out[None],
        grad_tokens[None],
        gain_grad[:, 0, :].reshape(width) / gain_one,
        dwq,
        dwk,
        dwv,
        dwo.reshape(width, width),
        bias,
        small[0],
        router.T,
        own_grads[:hidden].T[None],
        own_grads[hidden:].T[None],
    )


def solution(mesh):
    return jax.shard_map(
        shards,
        mesh=mesh,
        in_specs=(
            P("expert", "context", None),
            P(),
            P(),
            P(),
            P(),
            P(),
            P(),
            P(),
            P(),
            P("expert", None, "context"),
            P("expert", None, "context"),
            P("expert", "context", None),
            P("expert", "context", None),
        ),
        out_specs=(
            P("expert", "context", None),
            P("expert", "context", None),
            P(),
            P(),
            P(),
            P(),
            P(),
            P(),
            P(),
            P(),
            P("expert", None, "context"),
            P("expert", None, "context"),
        ),
        check_vma=False,
    )
```

```python
import math

import jax
import jax.numpy as jnp
from jax import lax
from jax.experimental import pallas as pl
from jax.experimental.pallas import tpu as pltpu
from jax.sharding import PartitionSpec as P

MAX_DIST = 128
EPSILON = 1e-06
NEG_LARGE = -1e30
BLK = 256
HEAD_SLOTS = 16

F32 = jnp.float32
BF16 = jnp.bfloat16
HIGHEST = lax.Precision.HIGHEST

NN = (((1,), (0,)), ((), ()))
NT = (((1,), (1,)), ((), ()))
TN = (((0,), (0,)), ((), ()))


def dot(a, b, dims=NN, precision=None):
    return lax.dot_general(a, b, dims, precision=precision, preferred_element_type=F32)


def bucket_starts(buckets, far_reach):
    span = buckets // 2
    rest = [
        int(math.ceil(span * (far_reach / span) ** (step / (buckets - span))))
        for step in range(1, buckets - span)
    ]
    return list(range(span + 1)) + rest


def rms_scale(values):
    return lax.rsqrt(jnp.mean(values * values, axis=-1, keepdims=True) + EPSILON)


def norm_back(values, inv_root, gain_vec, grad_normed):
    weighted = grad_normed * gain_vec
    cubed = inv_root * inv_root * inv_root
    return inv_root * weighted - values * cubed * jnp.mean(
        weighted * values, axis=-1, keepdims=True
    )


def whole(vmem_mib=56):
    return pltpu.CompilerParams(vmem_limit_bytes=vmem_mib * 2**20)


def vspec():
    return pl.BlockSpec(memory_space=pltpu.VMEM)


def sspec():
    return pl.BlockSpec(memory_space=pltpu.SMEM)


def project_kernel(tok_ref, gain_ref, wq_ref, wk_ref, wv_ref, normed_ref, out_ref):
    inputs = tok_ref[...].astype(F32)
    normed = (inputs * rms_scale(inputs) * gain_ref[...][None, :]).astype(BF16)
    rows, width = normed.shape
    half = rows // 2
    normed_ref[...] = normed
    queries = (dot(normed, wq_ref[...]).astype(BF16).astype(F32) * 0.125).astype(BF16)
    keys = dot(normed, wk_ref[...]).astype(BF16)
    values = dot(normed, wv_ref[...]).astype(BF16)
    heads = width // 64
    for h in range(heads):
        cols = slice(64 * h, 64 * h + 64)
        out_ref[h, :rows, :] = jnp.concatenate([queries[:, cols], keys[:, cols]], axis=1)
        out_ref[h, rows:, :] = jnp.concatenate([values[:half, cols], values[half:, cols]], axis=1)
    for h in range(heads, HEAD_SLOTS):
        out_ref[h] = jnp.zeros_like(out_ref[h])


def project(tokens, gain_one, w_query, w_key, w_value):
    rows, width = tokens.shape
    return pl.pallas_call(
        project_kernel,
        name="project",
        cost_estimate=pl.CostEstimate(flops=500000000, bytes_accessed=6000000, transcendentals=0),
        out_shape=(
            jax.ShapeDtypeStruct((rows, width), BF16),
            jax.ShapeDtypeStruct((HEAD_SLOTS, rows + rows // 2, 128), BF16),
        ),
        in_specs=[vspec()] * 5,
        out_specs=(vspec(), vspec()),
        compiler_params=whole(),
    )(tokens, gain_one, w_query, w_key, w_value)


def bias_tile(table_ref, head, buckets, rows_first, shape, key_dim):
    sign = [1, -1] if key_dim == 1 else [-1, 1]
    dist = (
        rows_first
        + sign[0] * lax.broadcasted_iota(jnp.int32, shape, 0)
        + sign[1] * lax.broadcasted_iota(jnp.int32, shape, 1)
    )
    far = table_ref[head, buckets - 1]
    tile = jnp.full(shape, NEG_LARGE, F32)
    for b, start in enumerate(bucket_starts(buckets, MAX_DIST)):
        tile = jnp.where(dist >= start, table_ref[head, b] - far, tile)
    return tile


def unpack_qkv(qkv_ref, q_s, k_s, v_s, ones_lane):
    count = qkv_ref.shape[0]
    lane = lax.broadcasted_iota(jnp.int32, (64, 64), 1)
    one = jnp.where(lane == 0, 1.0, 0.0).astype(BF16)
    for c in range(count):
        pair = qkv_ref[c, :128, :]
        q_s[128 * c : 128 * c + 128, :] = pair[:, :64]
        k_s[128 * c : 128 * c + 128, :] = pair[:, 64:]
        two = qkv_ref[c, 128:192, :]
        top, bottom = two[:, :64], two[:, 64:]
        if ones_lane:
            top = jnp.concatenate([top, one], axis=1)
            bottom = jnp.concatenate([bottom, one], axis=1)
        v_s[128 * c : 128 * c + 64, :] = top
        v_s[128 * c + 64 : 128 * c + 128, :] = bottom


def attend_kernel(buckets, head_ref, table_ref, qkv_ref, out_ref, keep_ref, lse_ref, q_s, k_s, v_s, bias_s):
    head = head_ref[0]
    unpack_qkv(qkv_ref, q_s, k_s, v_s, True)
    bias_s[0] = bias_tile(table_ref, head, buckets, BLK, (BLK, BLK), 1)
    bias_s[1] = bias_tile(table_ref, head, buckets, 0, (BLK, BLK), 1)
    blocks = q_s.shape[0] // BLK

    for qb in range(blocks):
        query = q_s[BLK * qb : BLK * qb + BLK, :]
        near = max(qb - 1, 0) * BLK
        parts = []
        if near:
            parts.append((0, dot(query, k_s[:near, :], NT)))
        if qb:
            parts.append((near, dot(query, k_s[near : near + BLK, :], NT) + bias_s[0]))
        parts.append((BLK * qb, dot(query, k_s[BLK * qb : BLK * qb + BLK, :], NT) + bias_s[1]))
        top = parts[-1][1]
        top = jnp.maximum(top[:, :128], top[:, 128:])
        for unused, scores in parts[:-1]:
            for j in range(scores.shape[1] // 128):
                top = jnp.maximum(top, scores[:, 128 * j : 128 * j + 128])
        top = jnp.max(top, axis=1, keepdims=True)
        total = jnp.zeros((BLK, 128), F32)
        for first, scores in parts:
            weights = jnp.exp(scores - top).astype(BF16)
            total = total + dot(weights, v_s[first : first + scores.shape[1], :])
        norm = total[:, 64:65]
        out = total[:, :64] / norm
        log_total = top + jnp.log(norm)
        spread = jnp.broadcast_to(log_total, (BLK, 128)).T
        lse_ref[qb] = spread[:8, :]
        for part in range(BLK // 128):
            two = jnp.concatenate(
                [out[128 * part : 128 * part + 64], out[128 * part + 64 : 128 * part + 128]], axis=1
            )
            place = qb * (BLK // 128) + part
            out_ref[place] = two.astype(BF16)
            keep_ref[place] = two


def attend(head, rel_table, qkv):
    count = qkv.shape[0]
    length = 128 * count
    blocks = length // BLK
    return pl.pallas_call(
        lambda *refs: attend_kernel(rel_table.shape[1], *refs),
        name="attend",
        cost_estimate=pl.CostEstimate(flops=7000000000, bytes_accessed=3000000, transcendentals=3000000),
        out_shape=(
            jax.ShapeDtypeStruct((count, 64, 128), BF16),
            jax.ShapeDtypeStruct((count, 64, 128), F32),
            jax.ShapeDtypeStruct((blocks, 8, BLK), F32),
        ),
        in_specs=[sspec(), sspec(), vspec()],
        out_specs=(vspec(), vspec(), vspec()),
        scratch_shapes=[
            pltpu.VMEM((length, 64), BF16),
            pltpu.VMEM((length, 64), BF16),
            pltpu.VMEM((length, 128), BF16),
            pltpu.VMEM((2, BLK, BLK), F32),
        ],
        compiler_params=whole(),
    )(head, rel_table, qkv)


def attend_back_kernel(
    buckets,
    head_ref,
    table_ref,
    qkv_ref,
    go_ref,
    keep_ref,
    lse_ref,
    dqkv_ref,
    bias_ref,
    q_s,
    k_s,
    v_s,
    kt_s,
    go_s,
    delta_s,
    dq_s,
    dk_s,
    dv_s,
    bias_s,
    acc_s,
):
    head = head_ref[0]
    length = q_s.shape[0]
    count = qkv_ref.shape[0]
    blocks = length // BLK
    unpack_qkv(qkv_ref, q_s, k_s, v_s, False)
    ones = jnp.ones((8, 64), F32)
    for c in range(count):
        kt_s[:, 128 * c : 128 * c + 128] = k_s[128 * c : 128 * c + 128, :].T
        two, kept = go_ref[c], keep_ref[c]
        go_s[128 * c : 128 * c + 64, :] = two[:, :64]
        go_s[128 * c + 64 : 128 * c + 128, :] = two[:, 64:]
        both = two.astype(F32) * kept
        prod = jnp.concatenate([both[:, :64], both[:, 64:]], axis=0)
        delta_s[:, 128 * c : 128 * c + 128] = dot(ones, prod, NT, HIGHEST)
    bias_s[0] = bias_tile(table_ref, head, buckets, BLK, (BLK, BLK), 0)
    bias_s[1] = bias_tile(table_ref, head, buckets, 0, (BLK, BLK), 0)
    acc_s[...] = jnp.zeros_like(acc_s)
    dk_s[...] = jnp.zeros_like(dk_s)
    dv_s[...] = jnp.zeros_like(dv_s)

    far_sum = jnp.zeros((8, BLK), F32)
    for qb in range(blocks):
        rows = slice(BLK * qb, BLK * qb + BLK)
        query, grad = q_s[rows, :], go_s[rows, :]
        lse = lse_ref[qb][:1, :]
        delta = delta_s[:1, rows]
        grad_query = jnp.zeros((64, BLK), F32)
        for kb in range(qb + 1):
            cols = slice(BLK * kb, BLK * kb + BLK)
            near = kb - qb + 1
            scores = dot(k_s[cols, :], query, NT)
            if near >= 0:
                scores = scores + bias_s[near]
            probs = jnp.exp(scores - lse)
            grad_probs = dot(v_s[cols, :], grad, NT)
            grad_scores = (probs * (grad_probs - delta)).astype(BF16)
            dv_s[cols, :] += dot(probs.astype(BF16), grad)
            dk_s[cols, :] += dot(grad_scores, query)
            grad_query = grad_query + dot(kt_s[:, cols], grad_scores)
            wide = grad_scores.astype(F32)
            if near < 0:
                far_sum = far_sum + jnp.sum(wide.reshape(BLK // 8, 8, BLK), axis=0)
            else:
                acc_s[near] += wide
        dq_s[:, rows] = grad_query

    for c in range(count):
        here = slice(128 * c, 128 * c + 128)
        dq_t = (dq_s[:, here] * 0.125).astype(BF16)
        dk = dk_s[here, :].astype(BF16)
        dv = dv_s[here, :].astype(BF16)
        dqkv_ref[c, :128, :] = jnp.concatenate([dq_t.T, dk], axis=1)
        dqkv_ref[c, 128:192, :] = jnp.concatenate([dv[:64], dv[64:]], axis=1)

    lane = lax.broadcasted_iota(jnp.int32, (16, 128), 1)
    dist0 = (
        BLK
        - lax.broadcasted_iota(jnp.int32, (BLK, BLK), 0)
        + lax.broadcasted_iota(jnp.int32, (BLK, BLK), 1)
    )
    dist1 = dist0 - BLK

    def total(values):
        return jnp.sum(jnp.sum(values, axis=1, keepdims=True), axis=0, keepdims=True)

    starts = bucket_starts(buckets, MAX_DIST)
    row = jnp.zeros((16, 128), F32)
    above = None
    for b in reversed(range(buckets)):
        reach = total(
            jnp.where(dist0 >= starts[b], acc_s[0], 0.0)
            + jnp.where(dist1 >= starts[b], acc_s[1], 0.0)
        )
        mine = reach + total(far_sum) if b == buckets - 1 else reach - above
        above = reach
        row = jnp.where(lane == b, mine, row)
    bias_ref[...] = row


def attend_back(head, rel_table, qkv, grad_heads, keep, lse):
    count = qkv.shape[0]
    length = 128 * count
    return pl.pallas_call(
        lambda *refs: attend_back_kernel(rel_table.shape[1], *refs),
        name="attend_back",
        cost_estimate=pl.CostEstimate(flops=14000000000, bytes_accessed=4000000, transcendentals=3000000),
        out_shape=(
            jax.ShapeDtypeStruct(qkv.shape, BF16),
            jax.ShapeDtypeStruct((16, 128), F32),
        ),
        in_specs=[sspec(), sspec()] + [vspec()] * 4,
        out_specs=(vspec(), vspec()),
        scratch_shapes=[
            pltpu.VMEM((length, 64), BF16),
            pltpu.VMEM((length, 64), BF16),
            pltpu.VMEM((length, 64), BF16),
            pltpu.VMEM((64, length), BF16),
            pltpu.VMEM((length, 64), BF16),
            pltpu.VMEM((8, length), F32),
            pltpu.VMEM((64, length), F32),
            pltpu.VMEM((length, 64), F32),
            pltpu.VMEM((length, 64), F32),
            pltpu.VMEM((2, BLK, BLK), F32),
            pltpu.VMEM((2, BLK, BLK), F32),
        ],
        compiler_params=whole(),
    )(head, rel_table, qkv, grad_heads, keep, lse)


def head_grads_kernel(place_ref, dqkv_ref, mine_ref, other_ref, bias_ref, sums_ref, out_ref, turned_s):
    count = dqkv_ref.shape[0]
    width = mine_ref.shape[-1]
    held = mine_ref.shape[0] * mine_ref.shape[1]
    my_x, my_z, my_core = place_ref[0] // 2, place_ref[2], place_ref[3]
    for i in range(count):
        core, z, x = i // 8, i % 8 // 2, i % 2
        there = (lax.rem(my_x + x, 2) * 4 + lax.rem(my_z + z, 4)) * 2 + lax.rem(my_core + core, 2)
        turned_s[i] = dqkv_ref[there]
    pairs, third = 0.0, 0.0
    for core, normed_ref in enumerate((mine_ref, other_ref)):
        normed = normed_ref[...].reshape(held, 128, width)
        here = slice(held * core, held * core + held)
        two = turned_s[here, 128:192, :].reshape(held * 64, 128)
        for half in range(2):
            rows = slice(64 * half, 64 * half + 64)
            part = normed[:, rows, :].reshape(held * 64, width)
            pairs = pairs + dot(turned_s[here, rows, :].reshape(held * 64, 128), part, TN)
            third = third + dot(two, part, TN)[rows]
    pairs, third = pairs.T, third.T
    total = sums_ref[0].astype(F32)
    for c in range(1, count):
        total = total + sums_ref[c].astype(F32)
    shares = out_ref.shape[0]
    each = width // shares
    row = bias_ref[...].astype(BF16)
    for s in range(shares):
        mine = slice(each * s, each * s + each)
        out_ref[s, :each, :] = pairs[mine].astype(BF16)
        last = third[mine].astype(BF16)
        out_ref[s, each : each + each // 2, :] = jnp.concatenate(
            [last[: each // 2], last[each // 2 :]], axis=1
        )
        at = each + each // 2
        out_ref[s, at : at + 16, :] = row
        part = total[8 * s : 8 * s + 8]
        out_ref[s, at + 16 :, :] = jnp.concatenate(
            [part[:, 128 * j : 128 * j + 128] for j in range(width // 128)], axis=0
        ).astype(BF16)


def head_grads(place, dqkv, mine, other, bias, sums, shares):
    width = mine.shape[-1]
    each = width // shares
    held = each + each // 2 + 16 + width // 16
    return pl.pallas_call(
        head_grads_kernel,
        name="head_grads",
        cost_estimate=pl.CostEstimate(flops=3000000000, bytes_accessed=8000000, transcendentals=0),
        out_shape=jax.ShapeDtypeStruct((shares, held, 128), BF16),
        in_specs=[sspec()] + [vspec()] * 5,
        out_specs=vspec(),
        scratch_shapes=[pltpu.VMEM(dqkv.shape, BF16)],
        compiler_params=whole(),
    )(place, dqkv, mine, other, bias, sums)


def heads_to_rows(ref, scratch):
    for j in range(scratch.shape[1] // 128):
        one, two = ref[2 * j], ref[2 * j + 1]
        scratch[:64, 128 * j : 128 * j + 128] = jnp.concatenate([one[:, :64], two[:, :64]], axis=1)
        scratch[64:, 128 * j : 128 * j + 128] = jnp.concatenate([one[:, 64:], two[:, 64:]], axis=1)


def dispatch_kernel(
    experts,
    capacity,
    tok_ref,
    cot_ref,
    heads_ref,
    wo_ref,
    gain_ref,
    wr_ref,
    routes_ref,
    send_ref,
    att_ref,
    mixed_ref,
    second_ref,
    pick_ref,
    gates_ref,
):
    rows = tok_ref.shape[0]
    heads_to_rows(heads_ref, att_ref)
    mixed = tok_ref[...].astype(F32) + dot(att_ref[...], wo_ref[...])
    mixed_ref[...] = mixed
    second = (mixed * rms_scale(mixed) * gain_ref[...][None, :]).astype(BF16)
    second_ref[...] = second
    logits = dot(second, wr_ref[...])
    ids = lax.broadcasted_iota(jnp.int32, (rows, experts), 1)
    routes = routes_ref[...]
    marks = [(routes[:, k : k + 1] == ids).astype(F32) for k in range(2)]
    earlier = (
        lax.broadcasted_iota(jnp.int32, (rows, rows), 0)
        > lax.broadcasted_iota(jnp.int32, (rows, rows), 1)
    ).astype(F32)
    ranks = dot(earlier.astype(BF16), (marks[0] + marks[1]).astype(BF16))
    chosen = [jnp.sum(m * logits, axis=1, keepdims=True) for m in marks]
    top = jnp.maximum(chosen[0], chosen[1])
    exps = [jnp.exp(c - top) for c in chosen]
    gates = [e / (exps[0] + exps[1]) for e in exps]
    slot_ids = lax.broadcasted_iota(jnp.int32, (rows, experts * capacity), 1)
    grad_out = cot_ref[...].astype(F32)
    picks = []
    for k in range(2):
        slot = jnp.sum(marks[k] * ranks, axis=1, keepdims=True).astype(jnp.int32)
        place = routes[:, k : k + 1] * capacity + slot
        picks.append((place == slot_ids).astype(F32).astype(BF16))
        pick_ref[k] = picks[k]
    send_rows = dot(picks[0] + picks[1], second, TN).astype(BF16)
    send_grads = dot(picks[0], (gates[0] * grad_out).astype(BF16), TN) + dot(
        picks[1], (gates[1] * grad_out).astype(BF16), TN
    )
    send_grads = send_grads.astype(BF16)
    for e in range(experts):
        here = slice(capacity * e, capacity * e + capacity)
        send_ref[e, :capacity, :] = send_rows[here]
        send_ref[e, capacity:, :] = send_grads[here]
    lane = lax.broadcasted_iota(jnp.int32, (rows, 128), 1)
    gates_ref[...] = jnp.where(lane == 0, gates[0], gates[1])


def dispatch(tokens, cotangent, heads, w_out, gain_two, w_router, routes, experts):
    rows, width = tokens.shape
    capacity = 3 * rows // experts
    return pl.pallas_call(
        lambda *refs: dispatch_kernel(experts, capacity, *refs),
        name="dispatch",
        cost_estimate=pl.CostEstimate(flops=500000000, bytes_accessed=4000000, transcendentals=0),
        out_shape=(
            jax.ShapeDtypeStruct((experts, 2 * capacity, width), BF16),
            jax.ShapeDtypeStruct((rows, width), BF16),
            jax.ShapeDtypeStruct((rows, width), F32),
            jax.ShapeDtypeStruct((rows, width), BF16),
            jax.ShapeDtypeStruct((2, rows, experts * capacity), BF16),
            jax.ShapeDtypeStruct((rows, 128), F32),
        ),
        in_specs=[vspec()] * 7,
        out_specs=(vspec(),) * 6,
        compiler_params=whole(),
    )(tokens, cotangent, heads, w_out, gain_two, w_router, routes)


def expert_kernel(rows_ref, w_ref, back_ref, dw_ref, x_s, g_s, y_s, dx_s):
    step = pl.program_id(0)
    sources, both, width = rows_ref.shape
    capacity = both // 2

    @pl.when(step == 0)
    def _():
        for s in range(sources):
            x_s[capacity * s : capacity * s + capacity, :] = rows_ref[s, :capacity, :]
            g_s[capacity * s : capacity * s + capacity, :] = rows_ref[s, capacity:, :]
        y_s[...] = jnp.zeros_like(y_s)
        dx_s[...] = jnp.zeros_like(dx_s)

    each = w_ref.shape[1] // 2
    w_in = w_ref[:, :each, :].reshape(-1, width)
    w_back = w_ref[:, each:, :].reshape(-1, width)
    pre = dot(x_s[...], w_in, NT)
    square = pre * pre
    curve = jnp.tanh(0.7978845608 * (pre + 0.044715 * square * pre))
    act = (0.5 * pre * (1.0 + curve)).astype(BF16)
    slope = 0.5 * (1.0 + curve) + 0.5 * pre * (1.0 - curve * curve) * (
        0.7978845608 * (1.0 + 3.0 * 0.044715 * square)
    )
    grad_pre = (dot(g_s[...], w_back, NT) * slope).astype(BF16)
    y_s[...] += dot(act, w_back)
    dx_s[...] += dot(grad_pre, w_in)
    dw_ref[:, :each, :] = dot(grad_pre, x_s[...], TN).astype(BF16).reshape(-1, each, width)
    dw_ref[:, each:, :] = dot(act, g_s[...], TN).astype(BF16).reshape(-1, each, width)

    @pl.when(step == pl.num_programs(0) - 1)
    def _():
        for s in range(sources):
            here = slice(capacity * s, capacity * s + capacity)
            back_ref[s, :capacity, :] = y_s[here, :].astype(BF16)
            back_ref[s, capacity:, :] = dx_s[here, :].astype(BF16)


AT_ONCE = 4


def expert_both(rows, shared):
    sources, both, width = rows.shape
    count, given, unused = shared.shape
    held = sources * both // 2
    return pl.pallas_call(
        expert_kernel,
        name="expert_both",
        cost_estimate=pl.CostEstimate(flops=18000000000, bytes_accessed=22000000, transcendentals=5000000),
        grid=(count // AT_ONCE,),
        out_shape=(
            jax.ShapeDtypeStruct(rows.shape, BF16),
            jax.ShapeDtypeStruct(shared.shape, BF16),
        ),
        in_specs=[
            pl.BlockSpec(rows.shape, lambda i: (0, 0, 0)),
            pl.BlockSpec((AT_ONCE, given, width), lambda i: (i, 0, 0)),
        ],
        out_specs=(
            pl.BlockSpec(rows.shape, lambda i: (0, 0, 0)),
            pl.BlockSpec((AT_ONCE, given, width), lambda i: (i, 0, 0)),
        ),
        scratch_shapes=[
            pltpu.VMEM((held, width), BF16),
            pltpu.VMEM((held, width), BF16),
            pltpu.VMEM((held, width), F32),
            pltpu.VMEM((held, width), F32),
        ],
        compiler_params=whole(),
    )(rows, shared)


def combine_kernel(
    cot_ref,
    back_ref,
    pick_ref,
    gates_ref,
    mixed_ref,
    second_ref,
    routes_ref,
    gain_ref,
    wr_ref,
    wo_ref,
    out_ref,
    grad_mixed_ref,
    heads_ref,
    small_ref,
    y_s,
    dx_s,
):
    experts, both, width = back_ref.shape
    capacity = both // 2
    rows = cot_ref.shape[0]
    for s in range(experts):
        here = slice(capacity * s, capacity * s + capacity)
        y_s[here, :] = back_ref[s, :capacity, :]
        dx_s[here, :] = back_ref[s, capacity:, :]
    grad_out = cot_ref[...].astype(F32)
    mixed = mixed_ref[...]
    gates = [gates_ref[:, k : k + 1] for k in range(2)]
    picked = [dot(pick_ref[k], y_s[...]) for k in range(2)]
    out_ref[...] = (mixed + (gates[0] * picked[0] + gates[1] * picked[1])).astype(BF16)
    grad_gates = [jnp.sum(p * grad_out, axis=1, keepdims=True) for p in picked]
    mean = gates[0] * grad_gates[0] + gates[1] * grad_gates[1]
    grad_chosen = [gates[k] * (grad_gates[k] - mean) for k in range(2)]
    ids = lax.broadcasted_iota(jnp.int32, (rows, experts), 1)
    routes = routes_ref[...]
    grad_logits = jnp.where(routes[:, :1] == ids, grad_chosen[0], 0.0) + jnp.where(
        routes[:, 1:2] == ids, grad_chosen[1], 0.0
    )
    grad_second = dot(pick_ref[0], dx_s[...]) + dot(pick_ref[1], dx_s[...])
    grad_second = grad_second + dot(grad_logits, wr_ref[...].astype(F32), NT, HIGHEST)
    second = second_ref[...]
    grad_router = dot(grad_logits, second.astype(F32), TN, HIGHEST)
    scale = rms_scale(mixed)
    grad_gain = jnp.sum(grad_second * mixed * scale, axis=0, keepdims=True)
    grad_mixed = grad_out + norm_back(mixed, scale, gain_ref[...][None, :], grad_second)
    grad_mixed_ref[...] = grad_mixed
    grad_branch = grad_mixed.astype(BF16)
    grad_att = dot(grad_branch, wo_ref[...], NT).astype(BF16)
    heads = width // 64
    for h in range(heads):
        cols = slice(64 * h, 64 * h + 64)
        heads_ref[h] = jnp.concatenate([grad_att[:64, cols], grad_att[64:, cols]], axis=1)
    for h in range(heads, HEAD_SLOTS):
        heads_ref[h] = jnp.zeros_like(heads_ref[h])
    small_ref[...] = jnp.concatenate([grad_router, jnp.broadcast_to(grad_gain, (8, width))], axis=0)


def out_grad_kernel(att_ref, grad_mixed_ref, small_ref, sums_ref):
    grad_wo = dot(att_ref[...], grad_mixed_ref[...].astype(BF16), TN).astype(BF16)
    slots, each, width = sums_ref.shape
    used = width // each
    for c in range(used):
        sums_ref[c] = grad_wo[each * c : each * c + each]
    for c in range(used, slots):
        sums_ref[c] = jnp.zeros_like(sums_ref[c])
    sums_ref[used, :16, :] = small_ref[...].astype(BF16)


def out_grad(attended, grad_mixed, small):
    width = attended.shape[1]
    return pl.pallas_call(
        out_grad_kernel,
        name="out_grad",
        cost_estimate=pl.CostEstimate(flops=500000000, bytes_accessed=4000000, transcendentals=0),
        out_shape=jax.ShapeDtypeStruct((HEAD_SLOTS, 64, width), BF16),
        in_specs=[vspec()] * 3,
        out_specs=vspec(),
        compiler_params=whole(),
    )(attended, grad_mixed, small)


def combine(cotangent, back, picks, gates, mixed, second, routes, gain_two, w_router, w_out):
    rows, width = cotangent.shape
    experts, both, unused = back.shape
    held = experts * both // 2
    return pl.pallas_call(
        combine_kernel,
        name="combine",
        cost_estimate=pl.CostEstimate(flops=1000000000, bytes_accessed=5000000, transcendentals=0),
        out_shape=(
            jax.ShapeDtypeStruct((rows, width), BF16),
            jax.ShapeDtypeStruct((rows, width), F32),
            jax.ShapeDtypeStruct((HEAD_SLOTS, rows // 2, 128), BF16),
            jax.ShapeDtypeStruct((16, width), F32),
        ),
        in_specs=[vspec()] * 10,
        out_specs=(vspec(),) * 4,
        scratch_shapes=[pltpu.VMEM((held, width), BF16), pltpu.VMEM((held, width), BF16)],
        compiler_params=whole(),
    )(
        cotangent,
        back,
        picks,
        gates,
        mixed,
        second,
        routes,
        gain_two,
        w_router,
        w_out,
    )


def input_grad_kernel(tok_ref, gain_ref, grads_ref, wq_ref, wk_ref, wv_ref, mixed_ref, out_ref, dq_s, dk_s, dv_s):
    for j in range(dq_s.shape[1] // 128):
        cols = slice(128 * j, 128 * j + 128)
        one, two = grads_ref[2 * j], grads_ref[2 * j + 1]
        dq_s[:, cols] = jnp.concatenate([one[:128, :64], two[:128, :64]], axis=1)
        dk_s[:, cols] = jnp.concatenate([one[:128, 64:], two[:128, 64:]], axis=1)
        dv_s[:64, cols] = jnp.concatenate([one[128:, :64], two[128:, :64]], axis=1)
        dv_s[64:, cols] = jnp.concatenate([one[128:, 64:], two[128:, 64:]], axis=1)
    grad_normed = dot(dq_s[...], wq_ref[...], NT)
    grad_normed = grad_normed + dot(dk_s[...], wk_ref[...], NT)
    grad_normed = grad_normed + dot(dv_s[...], wv_ref[...], NT)
    inputs = tok_ref[...].astype(F32)
    out_ref[...] = mixed_ref[...] + norm_back(inputs, rms_scale(inputs), gain_ref[...][None, :], grad_normed)


def input_grad(tokens, gain_one, grads, w_query, w_key, w_value, grad_mixed):
    rows, width = tokens.shape
    return pl.pallas_call(
        input_grad_kernel,
        name="input_grad",
        cost_estimate=pl.CostEstimate(flops=500000000, bytes_accessed=5000000, transcendentals=0),
        out_shape=jax.ShapeDtypeStruct((rows, width), F32),
        in_specs=[vspec()] * 7,
        out_specs=vspec(),
        scratch_shapes=[pltpu.VMEM((rows, width), BF16)] * 3,
        compiler_params=whole(),
    )(tokens, gain_one, grads, w_query, w_key, w_value, grad_mixed)


def coordinates(index):
    context, expert = index // 8, index % 8
    return (context // 8 * 2 + expert % 2, expert // 2, context // 2 % 4, context % 2)


def device_at(x, y, z, core):
    return ((x // 2 * 4 + z) * 2 + core) * 8 + y * 2 + x % 2


def shifted(dim, by):
    pairs = []
    for index in range(128):
        place = list(coordinates(index))
        place[dim] = (place[dim] + by) % (2 if dim == 3 else 4)
        pairs.append((index, device_at(*place)))
    return pairs


AXES = ("context", "expert")


def direct_gather(block, dim):
    return jnp.stack([block] + [lax.ppermute(block, AXES, shifted(dim, -by)) for by in (1, 2, 3)])


def gather_all(piece, beside):
    filled = direct_gather(direct_gather(piece, 2), 0)
    half = filled.shape[0] // 2
    ahead = lax.ppermute(filled, AXES, shifted(1, -1))
    behind = lax.ppermute(filled, AXES, shifted(1, 1))
    ahead, behind, beside = lax.optimization_barrier((ahead, behind, beside))
    across = (
        lax.ppermute(ahead[:half], AXES, shifted(1, -1)),
        lax.ppermute(behind[half:], AXES, shifted(1, 1)),
    )
    mine = (filled, ahead, behind) + across
    other = tuple(lax.ppermute(part, AXES, shifted(3, 1)) for part in mine)
    return mine + other, beside


def unpack_kernel(
    buckets,
    place_ref,
    wq_ref,
    wk_ref,
    wv_ref,
    *rest,
):
    parts, (dwq_ref, dwk_ref, dwv_ref, dwo_ref, bias_ref, small_ref, router_ref, gain_grad_ref) = rest[:10], rest[10:18]
    all_s, sems = rest[18:]
    expert = pl.program_id(0)

    @pl.when(expert == 0)
    def _():
        copies = []
        for core in range(2):
            for i in range(5):
                part = parts[5 * core + i]
                half = all_s.shape[2] // 2
                place = (
                    all_s.at[core, (0, 1, 3)[i]]
                    if i < 3
                    else all_s.at[core, 2, pl.ds(half * (i - 3), half)]
                )
                copies.append(pltpu.make_async_copy(part, place, sems.at[5 * core + i]))
        for copy in copies:
            copy.start()
        for copy in copies:
            copy.wait()

    my_x, my_y, my_z, my_core = (place_ref[i] for i in range(4))
    each = dwq_ref.shape[0]
    half = each // 2
    width = dwq_ref.shape[1]
    rel_y = lax.rem(expert // 2 - my_y + 4, 4)

    def rel(context):
        x = context // 8 * 2 + lax.rem(expert, 2)
        return (
            jnp.where(my_core == context % 2, 0, 1),
            rel_y,
            lax.rem(x - my_x + 4, 4),
            lax.rem(context // 2 % 4 - my_z + 4, 4),
        )

    at = each + half
    bias = []
    for j in range(width // 128):
        cols = slice(128 * j, 128 * j + 128)
        one, two = all_s[rel(2 * j)].astype(F32), all_s[rel(2 * j + 1)].astype(F32)
        dwq_ref[:, cols] = jnp.concatenate([one[:each, :64], two[:each, :64]], axis=1)
        dwk_ref[:, cols] = jnp.concatenate([one[:each, 64:], two[:each, 64:]], axis=1)
        dwv_ref[:half, cols] = jnp.concatenate([one[each:at, :64], two[each:at, :64]], axis=1)
        dwv_ref[half:, cols] = jnp.concatenate([one[each:at, 64:], two[each:at, 64:]], axis=1)
        bias += [one[at : at + 1], two[at : at + 1]]
        for i, block in enumerate((one, two)):
            for k in range(width // 128):
                dwo_ref[2 * j + i, :, 128 * k : 128 * k + 128] = block[at + 16 + 8 * k : at + 24 + 8 * k]
    bias_ref[...] = jnp.concatenate(bias, axis=0)[:, :buckets]
    block = all_s[rel(width // 64)].astype(F32)
    small = jnp.concatenate(
        [block[at + 16 + 8 * k : at + 24 + 8 * k] for k in range(width // 128)], axis=1
    )

    @pl.when(expert == 0)
    def _():
        router_ref[...] = small

    @pl.when(expert == 1)
    def _():
        small_ref[...] = small

    prod = (
        dwq_ref[...] * wq_ref[...].astype(F32)
        + dwk_ref[...] * wk_ref[...].astype(F32)
        + dwv_ref[...] * wv_ref[...].astype(F32)
    )
    gain_grad_ref[...] = dot(jnp.ones((8, width), F32), prod, NT, HIGHEST)


def unpack(place, parts, w_query, w_key, w_value, heads, buckets, experts):
    width = w_query.shape[0]
    each = width // experts
    held = parts[0].shape[2]
    rows = pl.BlockSpec((each, width), lambda i: (i, 0))
    return pl.pallas_call(
        lambda *refs: unpack_kernel(buckets, *refs),
        name="unpack",
        cost_estimate=pl.CostEstimate(flops=1000000000, bytes_accessed=24000000, transcendentals=0),
        grid=(experts,),
        out_shape=(
            jax.ShapeDtypeStruct((width, width), F32),
            jax.ShapeDtypeStruct((width, width), F32),
            jax.ShapeDtypeStruct((width, width), F32),
            jax.ShapeDtypeStruct((heads, experts, 8, width), F32),
            jax.ShapeDtypeStruct((heads, buckets), F32),
            jax.ShapeDtypeStruct((8, width), F32),
            jax.ShapeDtypeStruct((8, width), F32),
            jax.ShapeDtypeStruct((experts, 8, each), F32),
        ),
        in_specs=[sspec(), rows, rows, rows] + [pl.BlockSpec(memory_space=pl.ANY)] * 10,
        out_specs=(
            rows,
            rows,
            rows,
            pl.BlockSpec((heads, None, 8, width), lambda i: (0, i, 0, 0)),
            pl.BlockSpec((heads, buckets), lambda i: (0, 0)),
            pl.BlockSpec((8, width), lambda i: (0, 0)),
            pl.BlockSpec((8, width), lambda i: (0, 0)),
            pl.BlockSpec((None, 8, each), lambda i: (i, 0, 0)),
        ),
        scratch_shapes=[
            pltpu.VMEM((2, 4, 4, 4, held, 128), BF16),
            pltpu.SemaphoreType.DMA((10,)),
        ],
        compiler_params=whole(),
    )(place, w_query, w_key, w_value, *parts)


def add_kernel(in_ref, out_ref):
    total = in_ref[0].astype(F32)
    for i in range(1, in_ref.shape[0]):
        total = total + in_ref[i].astype(F32)
    out_ref[...] = total.astype(BF16)


def add_up(received):
    return pl.pallas_call(
        add_kernel,
        name="add_up",
        out_shape=jax.ShapeDtypeStruct(received.shape[1:], BF16),
        in_specs=[vspec()],
        out_specs=vspec(),
        compiler_params=whole(),
    )(received)


def shards(
    tokens,
    gain_one,
    w_query,
    w_key,
    w_value,
    w_out,
    rel_table,
    gain_two,
    w_router,
    expert_in,
    expert_out,
    routes,
    cotangent,
):
    width = tokens.shape[2]
    heads, buckets = rel_table.shape
    experts = lax.axis_size("expert")
    inputs, grad_out, routes_here = tokens[0], cotangent[0], routes[0]
    context = lax.axis_index("context")
    head = jnp.minimum(context, heads - 1).astype(jnp.int32).reshape(1)

    own_weights = jnp.concatenate([expert_in[0].T, expert_out[0].T], axis=0)
    shared = lax.all_gather(own_weights, "context", axis=0, tiled=False)
    normed, packed = project(inputs, gain_one, w_query, w_key, w_value)
    qkv = lax.all_to_all(packed, "context", split_axis=0, concat_axis=0, tiled=True)
    expert = lax.axis_index("expert")
    place = jnp.stack(coordinates(context * experts + expert)).astype(jnp.int32)
    normed, qkv = lax.optimization_barrier((normed, qkv))
    normed_two = jnp.stack([normed, lax.ppermute(normed, AXES, shifted(0, 2))])

    out_heads, keep, lse = attend(head, rel_table, qkv)
    out_rows = lax.all_to_all(out_heads, "context", split_axis=0, concat_axis=0, tiled=True)
    send, attended, mixed, second, picks, gates = dispatch(
        inputs, grad_out, out_rows, w_out, gain_two, w_router, routes_here, experts
    )
    received = lax.all_to_all(send, "expert", split_axis=0, concat_axis=0, tiled=True)
    normed_two, received, shared = lax.optimization_barrier((normed_two, received, shared))
    normed_mine = direct_gather(normed_two, 2)
    back, weight_grads = expert_both(received, shared)
    returned = lax.all_to_all(back, "expert", split_axis=0, concat_axis=0, tiled=True)
    normed_mine, returned = lax.optimization_barrier((normed_mine, returned))
    normed_other = lax.ppermute(normed_mine, AXES, shifted(3, 1))
    own_grads = lax.psum_scatter(weight_grads, "context", scatter_dimension=0, tiled=False)
    block_out, grad_mixed, grad_heads, small = combine(
        grad_out, returned, picks, gates, mixed, second, routes_here, gain_two, w_router, w_out
    )
    sums = out_grad(attended, grad_mixed, small)
    grad_here = lax.all_to_all(grad_heads, "context", split_axis=0, concat_axis=0, tiled=True)
    sums = lax.all_to_all(sums, "context", split_axis=0, concat_axis=0, tiled=True)

    dqkv, bias = attend_back(head, rel_table, qkv, grad_here, keep, lse)
    grads = lax.all_to_all(dqkv, "context", split_axis=0, concat_axis=0, tiled=True)
    terms = head_grads(place, dqkv, normed_mine, normed_other, bias, sums, experts)
    terms, grads = lax.optimization_barrier((terms, grads))
    terms = lax.all_to_all(terms, "expert", split_axis=0, concat_axis=0, tiled=True)
    grad_tokens = input_grad(inputs, gain_one, grads, w_query, w_key, w_value, grad_mixed)
    own_grads = own_grads.astype(F32)
    hidden = own_grads.shape[0] // 2
    parts, (grad_tokens, grad_in, grad_back) = gather_all(
        add_up(terms), (grad_tokens, own_grads[:hidden], own_grads[hidden:])
    )

    dwq, dwk, dwv, dwo, bias, small, router, gain_grad = unpack(
        place, parts, w_query, w_key, w_value, heads, buckets, experts
    )
    return (
        block_out[None],
        grad_tokens[None],
        gain_grad[:, 0, :].reshape(width) / gain_one,
        dwq,
        dwk,
        dwv,
        dwo.reshape(width, width),
        bias,
        small[0],
        router.T,
        grad_in.T[None],
        grad_back.T[None],
    )


def solution(mesh):
    return jax.shard_map(
        shards,
        mesh=mesh,
        in_specs=(
            P("expert", "context", None),
            P(),
            P(),
            P(),
            P(),
            P(),
            P(),
            P(),
            P(),
            P("expert", None, "context"),
            P("expert", None, "context"),
            P("expert", "context", None),
            P("expert", "context", None),
        ),
        out_specs=(
            P("expert", "context", None),
            P("expert", "context", None),
            P(),
            P(),
            P(),
            P(),
            P(),
            P(),
            P(),
            P(),
            P("expert", None, "context"),
            P("expert", None, "context"),
        ),
        check_vma=False,
    )
```

```python
import math

import jax
import jax.numpy as jnp
from jax import lax
from jax.experimental import pallas as pl
from jax.experimental.pallas import tpu as pltpu
from jax.sharding import PartitionSpec as P

MAX_DIST = 128
EPSILON = 1e-06
NEG_LARGE = -1e30
BLK = 256
HEAD_SLOTS = 16

F32 = jnp.float32
BF16 = jnp.bfloat16
HIGHEST = lax.Precision.HIGHEST

NN = (((1,), (0,)), ((), ()))
NT = (((1,), (1,)), ((), ()))
TN = (((0,), (0,)), ((), ()))


def dot(a, b, dims=NN, precision=None):
    return lax.dot_general(a, b, dims, precision=precision, preferred_element_type=F32)


def bucket_starts(buckets, far_reach):
    span = buckets // 2
    rest = [
        int(math.ceil(span * (far_reach / span) ** (step / (buckets - span))))
        for step in range(1, buckets - span)
    ]
    return list(range(span + 1)) + rest


def rms_scale(values):
    return lax.rsqrt(jnp.mean(values * values, axis=-1, keepdims=True) + EPSILON)


def norm_back(values, inv_root, gain_vec, grad_normed):
    weighted = grad_normed * gain_vec
    cubed = inv_root * inv_root * inv_root
    return inv_root * weighted - values * cubed * jnp.mean(
        weighted * values, axis=-1, keepdims=True
    )


def whole(vmem_mib=56):
    return pltpu.CompilerParams(vmem_limit_bytes=vmem_mib * 2**20)


def vspec():
    return pl.BlockSpec(memory_space=pltpu.VMEM)


def sspec():
    return pl.BlockSpec(memory_space=pltpu.SMEM)


def project_kernel(tok_ref, gain_ref, wq_ref, wk_ref, wv_ref, normed_ref, out_ref):
    inputs = tok_ref[...].astype(F32)
    normed = (inputs * rms_scale(inputs) * gain_ref[...][None, :]).astype(BF16)
    rows, width = normed.shape
    half = rows // 2
    normed_ref[...] = normed
    queries = (dot(normed, wq_ref[...]).astype(BF16).astype(F32) * 0.125).astype(BF16)
    keys = dot(normed, wk_ref[...]).astype(BF16)
    values = dot(normed, wv_ref[...]).astype(BF16)
    heads = width // 64
    for h in range(heads):
        cols = slice(64 * h, 64 * h + 64)
        out_ref[h, :rows, :] = jnp.concatenate([queries[:, cols], keys[:, cols]], axis=1)
        out_ref[h, rows:, :] = jnp.concatenate([values[:half, cols], values[half:, cols]], axis=1)
    for h in range(heads, HEAD_SLOTS):
        out_ref[h] = jnp.zeros_like(out_ref[h])


def project(tokens, gain_one, w_query, w_key, w_value):
    rows, width = tokens.shape
    return pl.pallas_call(
        project_kernel,
        name="project",
        cost_estimate=pl.CostEstimate(flops=500000000, bytes_accessed=6000000, transcendentals=0),
        out_shape=(
            jax.ShapeDtypeStruct((rows, width), BF16),
            jax.ShapeDtypeStruct((HEAD_SLOTS, rows + rows // 2, 128), BF16),
        ),
        in_specs=[vspec()] * 5,
        out_specs=(vspec(), vspec()),
        compiler_params=whole(),
    )(tokens, gain_one, w_query, w_key, w_value)


def bias_tile(table_ref, head, buckets, rows_first, shape, key_dim):
    sign = [1, -1] if key_dim == 1 else [-1, 1]
    dist = (
        rows_first
        + sign[0] * lax.broadcasted_iota(jnp.int32, shape, 0)
        + sign[1] * lax.broadcasted_iota(jnp.int32, shape, 1)
    )
    far = table_ref[head, buckets - 1]
    tile = jnp.full(shape, NEG_LARGE, F32)
    for b, start in enumerate(bucket_starts(buckets, MAX_DIST)):
        tile = jnp.where(dist >= start, table_ref[head, b] - far, tile)
    return tile


def unpack_qkv(qkv_ref, q_s, k_s, v_s, ones_lane):
    count = qkv_ref.shape[0]
    lane = lax.broadcasted_iota(jnp.int32, (64, 64), 1)
    one = jnp.where(lane == 0, 1.0, 0.0).astype(BF16)
    for c in range(count):
        pair = qkv_ref[c, :128, :]
        q_s[128 * c : 128 * c + 128, :] = pair[:, :64]
        k_s[128 * c : 128 * c + 128, :] = pair[:, 64:]
        two = qkv_ref[c, 128:192, :]
        top, bottom = two[:, :64], two[:, 64:]
        if ones_lane:
            top = jnp.concatenate([top, one], axis=1)
            bottom = jnp.concatenate([bottom, one], axis=1)
        v_s[128 * c : 128 * c + 64, :] = top
        v_s[128 * c + 64 : 128 * c + 128, :] = bottom


def attend_kernel(buckets, head_ref, table_ref, qkv_ref, out_ref, keep_ref, lse_ref, q_s, k_s, v_s, bias_s):
    head = head_ref[0]
    unpack_qkv(qkv_ref, q_s, k_s, v_s, True)
    bias_s[0] = bias_tile(table_ref, head, buckets, BLK, (BLK, BLK), 1)
    bias_s[1] = bias_tile(table_ref, head, buckets, 0, (BLK, BLK), 1)
    blocks = q_s.shape[0] // BLK

    for qb in range(blocks):
        query = q_s[BLK * qb : BLK * qb + BLK, :]
        near = max(qb - 1, 0) * BLK
        parts = []
        if near:
            parts.append((0, dot(query, k_s[:near, :], NT)))
        if qb:
            parts.append((near, dot(query, k_s[near : near + BLK, :], NT) + bias_s[0]))
        parts.append((BLK * qb, dot(query, k_s[BLK * qb : BLK * qb + BLK, :], NT) + bias_s[1]))
        top = parts[-1][1]
        top = jnp.maximum(top[:, :128], top[:, 128:])
        for unused, scores in parts[:-1]:
            for j in range(scores.shape[1] // 128):
                top = jnp.maximum(top, scores[:, 128 * j : 128 * j + 128])
        top = jnp.max(top, axis=1, keepdims=True)
        total = jnp.zeros((BLK, 128), F32)
        for first, scores in parts:
            weights = jnp.exp(scores - top).astype(BF16)
            total = total + dot(weights, v_s[first : first + scores.shape[1], :])
        norm = total[:, 64:65]
        out = total[:, :64] / norm
        log_total = top + jnp.log(norm)
        spread = jnp.broadcast_to(log_total, (BLK, 128)).T
        lse_ref[qb] = spread[:8, :]
        for part in range(BLK // 128):
            two = jnp.concatenate(
                [out[128 * part : 128 * part + 64], out[128 * part + 64 : 128 * part + 128]], axis=1
            )
            place = qb * (BLK // 128) + part
            out_ref[place] = two.astype(BF16)
            keep_ref[place] = two


def attend(head, rel_table, qkv):
    count = qkv.shape[0]
    length = 128 * count
    blocks = length // BLK
    return pl.pallas_call(
        lambda *refs: attend_kernel(rel_table.shape[1], *refs),
        name="attend",
        cost_estimate=pl.CostEstimate(flops=7000000000, bytes_accessed=3000000, transcendentals=3000000),
        out_shape=(
            jax.ShapeDtypeStruct((count, 64, 128), BF16),
            jax.ShapeDtypeStruct((count, 64, 128), F32),
            jax.ShapeDtypeStruct((blocks, 8, BLK), F32),
        ),
        in_specs=[sspec(), sspec(), vspec()],
        out_specs=(vspec(), vspec(), vspec()),
        scratch_shapes=[
            pltpu.VMEM((length, 64), BF16),
            pltpu.VMEM((length, 64), BF16),
            pltpu.VMEM((length, 128), BF16),
            pltpu.VMEM((2, BLK, BLK), F32),
        ],
        compiler_params=whole(),
    )(head, rel_table, qkv)


def attend_back_kernel(
    buckets,
    head_ref,
    table_ref,
    qkv_ref,
    go_ref,
    keep_ref,
    lse_ref,
    dqkv_ref,
    bias_ref,
    q_s,
    k_s,
    v_s,
    kt_s,
    go_s,
    delta_s,
    dq_s,
    dk_s,
    dv_s,
    bias_s,
    acc_s,
):
    head = head_ref[0]
    length = q_s.shape[0]
    count = qkv_ref.shape[0]
    blocks = length // BLK
    unpack_qkv(qkv_ref, q_s, k_s, v_s, False)
    ones = jnp.ones((8, 64), F32)
    for c in range(count):
        kt_s[:, 128 * c : 128 * c + 128] = k_s[128 * c : 128 * c + 128, :].T
        two, kept = go_ref[c], keep_ref[c]
        go_s[128 * c : 128 * c + 64, :] = two[:, :64]
        go_s[128 * c + 64 : 128 * c + 128, :] = two[:, 64:]
        both = two.astype(F32) * kept
        prod = jnp.concatenate([both[:, :64], both[:, 64:]], axis=0)
        delta_s[:, 128 * c : 128 * c + 128] = dot(ones, prod, NT, HIGHEST)
    bias_s[0] = bias_tile(table_ref, head, buckets, BLK, (BLK, BLK), 0)
    bias_s[1] = bias_tile(table_ref, head, buckets, 0, (BLK, BLK), 0)
    acc_s[...] = jnp.zeros_like(acc_s)
    dk_s[...] = jnp.zeros_like(dk_s)
    dv_s[...] = jnp.zeros_like(dv_s)

    far_sum = jnp.zeros((8, BLK), F32)
    for qb in range(blocks):
        rows = slice(BLK * qb, BLK * qb + BLK)
        query, grad = q_s[rows, :], go_s[rows, :]
        lse = lse_ref[qb][:1, :]
        delta = delta_s[:1, rows]
        grad_query = jnp.zeros((64, BLK), F32)
        for kb in range(qb + 1):
            cols = slice(BLK * kb, BLK * kb + BLK)
            near = kb - qb + 1
            scores = dot(k_s[cols, :], query, NT)
            if near >= 0:
                scores = scores + bias_s[near]
            probs = jnp.exp(scores - lse)
            grad_probs = dot(v_s[cols, :], grad, NT)
            grad_scores = (probs * (grad_probs - delta)).astype(BF16)
            dv_s[cols, :] += dot(probs.astype(BF16), grad)
            dk_s[cols, :] += dot(grad_scores, query)
            grad_query = grad_query + dot(kt_s[:, cols], grad_scores)
            wide = grad_scores.astype(F32)
            if near < 0:
                far_sum = far_sum + jnp.sum(wide.reshape(BLK // 8, 8, BLK), axis=0)
            else:
                acc_s[near] += wide
        dq_s[:, rows] = grad_query

    for c in range(count):
        here = slice(128 * c, 128 * c + 128)
        dq_t = (dq_s[:, here] * 0.125).astype(BF16)
        dk = dk_s[here, :].astype(BF16)
        dv = dv_s[here, :].astype(BF16)
        dqkv_ref[c, :128, :] = jnp.concatenate([dq_t.T, dk], axis=1)
        dqkv_ref[c, 128:192, :] = jnp.concatenate([dv[:64], dv[64:]], axis=1)

    lane = lax.broadcasted_iota(jnp.int32, (16, 128), 1)
    dist0 = (
        BLK
        - lax.broadcasted_iota(jnp.int32, (BLK, BLK), 0)
        + lax.broadcasted_iota(jnp.int32, (BLK, BLK), 1)
    )
    dist1 = dist0 - BLK

    def total(values):
        return jnp.sum(jnp.sum(values, axis=1, keepdims=True), axis=0, keepdims=True)

    starts = bucket_starts(buckets, MAX_DIST)
    row = jnp.zeros((16, 128), F32)
    above = None
    for b in reversed(range(buckets)):
        reach = total(
            jnp.where(dist0 >= starts[b], acc_s[0], 0.0)
            + jnp.where(dist1 >= starts[b], acc_s[1], 0.0)
        )
        mine = reach + total(far_sum) if b == buckets - 1 else reach - above
        above = reach
        row = jnp.where(lane == b, mine, row)
    bias_ref[...] = row


def attend_back(head, rel_table, qkv, grad_heads, keep, lse):
    count = qkv.shape[0]
    length = 128 * count
    return pl.pallas_call(
        lambda *refs: attend_back_kernel(rel_table.shape[1], *refs),
        name="attend_back",
        cost_estimate=pl.CostEstimate(flops=14000000000, bytes_accessed=4000000, transcendentals=3000000),
        out_shape=(
            jax.ShapeDtypeStruct(qkv.shape, BF16),
            jax.ShapeDtypeStruct((16, 128), F32),
        ),
        in_specs=[sspec(), sspec()] + [vspec()] * 4,
        out_specs=(vspec(), vspec()),
        scratch_shapes=[
            pltpu.VMEM((length, 64), BF16),
            pltpu.VMEM((length, 64), BF16),
            pltpu.VMEM((length, 64), BF16),
            pltpu.VMEM((64, length), BF16),
            pltpu.VMEM((length, 64), BF16),
            pltpu.VMEM((8, length), F32),
            pltpu.VMEM((64, length), F32),
            pltpu.VMEM((length, 64), F32),
            pltpu.VMEM((length, 64), F32),
            pltpu.VMEM((2, BLK, BLK), F32),
            pltpu.VMEM((2, BLK, BLK), F32),
        ],
        compiler_params=whole(),
    )(head, rel_table, qkv, grad_heads, keep, lse)


def head_grads_kernel(place_ref, dqkv_ref, mine_ref, other_ref, bias_ref, sums_ref, out_ref, turned_s):
    count = dqkv_ref.shape[0]
    width = mine_ref.shape[-1]
    held = mine_ref.shape[0] * mine_ref.shape[1]
    my_x, my_z, my_core = place_ref[0] // 2, place_ref[2], place_ref[3]
    for i in range(count):
        core, z, x = i // 8, i % 8 // 2, i % 2
        there = (lax.rem(my_x + x, 2) * 4 + lax.rem(my_z + z, 4)) * 2 + lax.rem(my_core + core, 2)
        turned_s[i] = dqkv_ref[there]
    pairs, third = 0.0, 0.0
    for core, normed_ref in enumerate((mine_ref, other_ref)):
        normed = normed_ref[...].reshape(held, 128, width)
        here = slice(held * core, held * core + held)
        two = turned_s[here, 128:192, :].reshape(held * 64, 128)
        for half in range(2):
            rows = slice(64 * half, 64 * half + 64)
            part = normed[:, rows, :].reshape(held * 64, width)
            pairs = pairs + dot(turned_s[here, rows, :].reshape(held * 64, 128), part, TN)
            third = third + dot(two, part, TN)[rows]
    pairs, third = pairs.T, third.T
    total = sums_ref[0].astype(F32)
    for c in range(1, sums_ref.shape[0]):
        total = total + sums_ref[c].astype(F32)
    shares = out_ref.shape[0]
    each = width // shares
    row = bias_ref[...].astype(BF16)
    for s in range(shares):
        mine = slice(each * s, each * s + each)
        out_ref[s, :each, :] = pairs[mine].astype(BF16)
        last = third[mine].astype(BF16)
        out_ref[s, each : each + each // 2, :] = jnp.concatenate(
            [last[: each // 2], last[each // 2 :]], axis=1
        )
        at = each + each // 2
        out_ref[s, at : at + 16, :] = row
        part = total[8 * s : 8 * s + 8]
        out_ref[s, at + 16 :, :] = jnp.concatenate(
            [part[:, 128 * j : 128 * j + 128] for j in range(width // 128)], axis=0
        ).astype(BF16)


def head_grads(place, dqkv, mine, other, bias, sums, shares):
    width = mine.shape[-1]
    each = width // shares
    held = each + each // 2 + 16 + width // 16
    return pl.pallas_call(
        head_grads_kernel,
        name="head_grads",
        cost_estimate=pl.CostEstimate(flops=3000000000, bytes_accessed=8000000, transcendentals=0),
        out_shape=jax.ShapeDtypeStruct((shares, held, 128), BF16),
        in_specs=[sspec()] + [vspec()] * 5,
        out_specs=vspec(),
        scratch_shapes=[pltpu.VMEM(dqkv.shape, BF16)],
        compiler_params=whole(),
    )(place, dqkv, mine, other, bias, sums)


def heads_to_rows(ref, scratch):
    for j in range(scratch.shape[1] // 128):
        one, two = ref[2 * j], ref[2 * j + 1]
        scratch[:64, 128 * j : 128 * j + 128] = jnp.concatenate([one[:, :64], two[:, :64]], axis=1)
        scratch[64:, 128 * j : 128 * j + 128] = jnp.concatenate([one[:, 64:], two[:, 64:]], axis=1)


def dispatch_kernel(
    experts,
    capacity,
    tok_ref,
    cot_ref,
    heads_ref,
    wo_ref,
    gain_ref,
    wr_ref,
    routes_ref,
    send_ref,
    att_ref,
    mixed_ref,
    second_ref,
    pick_ref,
    gates_ref,
):
    rows = tok_ref.shape[0]
    heads_to_rows(heads_ref, att_ref)
    mixed = tok_ref[...].astype(F32) + dot(att_ref[...], wo_ref[...])
    mixed_ref[...] = mixed
    second = (mixed * rms_scale(mixed) * gain_ref[...][None, :]).astype(BF16)
    second_ref[...] = second
    logits = dot(second, wr_ref[...])
    ids = lax.broadcasted_iota(jnp.int32, (rows, experts), 1)
    routes = routes_ref[...]
    marks = [(routes[:, k : k + 1] == ids).astype(F32) for k in range(2)]
    earlier = (
        lax.broadcasted_iota(jnp.int32, (rows, rows), 0)
        > lax.broadcasted_iota(jnp.int32, (rows, rows), 1)
    ).astype(F32)
    ranks = dot(earlier.astype(BF16), (marks[0] + marks[1]).astype(BF16))
    chosen = [jnp.sum(m * logits, axis=1, keepdims=True) for m in marks]
    top = jnp.maximum(chosen[0], chosen[1])
    exps = [jnp.exp(c - top) for c in chosen]
    gates = [e / (exps[0] + exps[1]) for e in exps]
    slot_ids = lax.broadcasted_iota(jnp.int32, (rows, experts * capacity), 1)
    grad_out = cot_ref[...].astype(F32)
    picks = []
    for k in range(2):
        slot = jnp.sum(marks[k] * ranks, axis=1, keepdims=True).astype(jnp.int32)
        place = routes[:, k : k + 1] * capacity + slot
        picks.append((place == slot_ids).astype(F32).astype(BF16))
        pick_ref[k] = picks[k]
    send_rows = dot(picks[0] + picks[1], second, TN).astype(BF16)
    send_grads = dot(picks[0], (gates[0] * grad_out).astype(BF16), TN) + dot(
        picks[1], (gates[1] * grad_out).astype(BF16), TN
    )
    send_grads = send_grads.astype(BF16)
    for e in range(experts):
        here = slice(capacity * e, capacity * e + capacity)
        send_ref[e, :capacity, :] = send_rows[here]
        send_ref[e, capacity:, :] = send_grads[here]
    lane = lax.broadcasted_iota(jnp.int32, (rows, 128), 1)
    gates_ref[...] = jnp.where(lane == 0, gates[0], gates[1])


def dispatch(tokens, cotangent, heads, w_out, gain_two, w_router, routes, experts):
    rows, width = tokens.shape
    capacity = 3 * rows // experts
    return pl.pallas_call(
        lambda *refs: dispatch_kernel(experts, capacity, *refs),
        name="dispatch",
        cost_estimate=pl.CostEstimate(flops=500000000, bytes_accessed=4000000, transcendentals=0),
        out_shape=(
            jax.ShapeDtypeStruct((experts, 2 * capacity, width), BF16),
            jax.ShapeDtypeStruct((rows, width), BF16),
            jax.ShapeDtypeStruct((rows, width), F32),
            jax.ShapeDtypeStruct((rows, width), BF16),
            jax.ShapeDtypeStruct((2, rows, experts * capacity), BF16),
            jax.ShapeDtypeStruct((rows, 128), F32),
        ),
        in_specs=[vspec()] * 7,
        out_specs=(vspec(),) * 6,
        compiler_params=whole(),
    )(tokens, cotangent, heads, w_out, gain_two, w_router, routes)


def expert_kernel(rows_ref, w_ref, back_ref, dw_ref, x_s, g_s, y_s, dx_s):
    step = pl.program_id(0)
    sources, both, width = rows_ref.shape
    capacity = both // 2

    @pl.when(step == 0)
    def _():
        for s in range(sources):
            x_s[capacity * s : capacity * s + capacity, :] = rows_ref[s, :capacity, :]
            g_s[capacity * s : capacity * s + capacity, :] = rows_ref[s, capacity:, :]
        y_s[...] = jnp.zeros_like(y_s)
        dx_s[...] = jnp.zeros_like(dx_s)

    each = w_ref.shape[1] // 2
    w_in = w_ref[:, :each, :].reshape(-1, width)
    w_back = w_ref[:, each:, :].reshape(-1, width)
    pre = dot(x_s[...], w_in, NT)
    square = pre * pre
    curve = jnp.tanh(0.7978845608 * (pre + 0.044715 * square * pre))
    act = (0.5 * pre * (1.0 + curve)).astype(BF16)
    slope = 0.5 * (1.0 + curve) + 0.5 * pre * (1.0 - curve * curve) * (
        0.7978845608 * (1.0 + 3.0 * 0.044715 * square)
    )
    grad_pre = (dot(g_s[...], w_back, NT) * slope).astype(BF16)
    y_s[...] += dot(act, w_back)
    dx_s[...] += dot(grad_pre, w_in)
    dw_ref[:, :each, :] = dot(grad_pre, x_s[...], TN).astype(BF16).reshape(-1, each, width)
    dw_ref[:, each:, :] = dot(act, g_s[...], TN).astype(BF16).reshape(-1, each, width)

    @pl.when(step == pl.num_programs(0) - 1)
    def _():
        for s in range(sources):
            here = slice(capacity * s, capacity * s + capacity)
            back_ref[s, :capacity, :] = y_s[here, :].astype(BF16)
            back_ref[s, capacity:, :] = dx_s[here, :].astype(BF16)


AT_ONCE = 4


def expert_both(rows, shared):
    sources, both, width = rows.shape
    count, given, unused = shared.shape
    held = sources * both // 2
    return pl.pallas_call(
        expert_kernel,
        name="expert_both",
        cost_estimate=pl.CostEstimate(flops=18000000000, bytes_accessed=22000000, transcendentals=5000000),
        grid=(count // AT_ONCE,),
        out_shape=(
            jax.ShapeDtypeStruct(rows.shape, BF16),
            jax.ShapeDtypeStruct(shared.shape, BF16),
        ),
        in_specs=[
            pl.BlockSpec(rows.shape, lambda i: (0, 0, 0)),
            pl.BlockSpec((AT_ONCE, given, width), lambda i: (i, 0, 0)),
        ],
        out_specs=(
            pl.BlockSpec(rows.shape, lambda i: (0, 0, 0)),
            pl.BlockSpec((AT_ONCE, given, width), lambda i: (i, 0, 0)),
        ),
        scratch_shapes=[
            pltpu.VMEM((held, width), BF16),
            pltpu.VMEM((held, width), BF16),
            pltpu.VMEM((held, width), F32),
            pltpu.VMEM((held, width), F32),
        ],
        compiler_params=whole(),
    )(rows, shared)


def combine_kernel(
    cot_ref,
    back_ref,
    pick_ref,
    gates_ref,
    mixed_ref,
    second_ref,
    routes_ref,
    gain_ref,
    wr_ref,
    wo_ref,
    out_ref,
    grad_mixed_ref,
    heads_ref,
    small_ref,
    y_s,
    dx_s,
):
    experts, both, width = back_ref.shape
    capacity = both // 2
    rows = cot_ref.shape[0]
    for s in range(experts):
        here = slice(capacity * s, capacity * s + capacity)
        y_s[here, :] = back_ref[s, :capacity, :]
        dx_s[here, :] = back_ref[s, capacity:, :]
    grad_out = cot_ref[...].astype(F32)
    mixed = mixed_ref[...]
    gates = [gates_ref[:, k : k + 1] for k in range(2)]
    picked = [dot(pick_ref[k], y_s[...]) for k in range(2)]
    out_ref[...] = (mixed + (gates[0] * picked[0] + gates[1] * picked[1])).astype(BF16)
    grad_gates = [jnp.sum(p * grad_out, axis=1, keepdims=True) for p in picked]
    mean = gates[0] * grad_gates[0] + gates[1] * grad_gates[1]
    grad_chosen = [gates[k] * (grad_gates[k] - mean) for k in range(2)]
    ids = lax.broadcasted_iota(jnp.int32, (rows, experts), 1)
    routes = routes_ref[...]
    grad_logits = jnp.where(routes[:, :1] == ids, grad_chosen[0], 0.0) + jnp.where(
        routes[:, 1:2] == ids, grad_chosen[1], 0.0
    )
    grad_second = dot(pick_ref[0], dx_s[...]) + dot(pick_ref[1], dx_s[...])
    grad_second = grad_second + dot(grad_logits, wr_ref[...].astype(F32), NT, HIGHEST)
    second = second_ref[...]
    grad_router = dot(grad_logits, second.astype(F32), TN, HIGHEST)
    scale = rms_scale(mixed)
    grad_gain = jnp.sum(grad_second * mixed * scale, axis=0, keepdims=True)
    grad_mixed = grad_out + norm_back(mixed, scale, gain_ref[...][None, :], grad_second)
    grad_mixed_ref[...] = grad_mixed
    grad_branch = grad_mixed.astype(BF16)
    grad_att = dot(grad_branch, wo_ref[...], NT).astype(BF16)
    heads = width // 64
    for h in range(heads):
        cols = slice(64 * h, 64 * h + 64)
        heads_ref[h] = jnp.concatenate([grad_att[:64, cols], grad_att[64:, cols]], axis=1)
    for h in range(heads, HEAD_SLOTS):
        heads_ref[h] = jnp.zeros_like(heads_ref[h])
    small_ref[...] = jnp.concatenate([grad_router, jnp.broadcast_to(grad_gain, (8, width))], axis=0)


def out_grad_kernel(place_ref, att_ref, grad_mixed_ref, small_ref, keep_ref, pass_ref, all_s):
    grad_wo = dot(att_ref[...], grad_mixed_ref[...].astype(BF16), TN).astype(BF16)
    slots, each, width = all_s.shape
    used = width // each
    for c in range(used):
        all_s[c] = grad_wo[each * c : each * c + each]
    for c in range(used, slots):
        all_s[c] = jnp.zeros_like(all_s[c])
    all_s[used, :16, :] = small_ref[...].astype(BF16)
    core = place_ref[3]
    for c in range(slots // 2):
        keep_ref[c] = all_s[2 * c + core]
        pass_ref[c] = all_s[2 * c + 1 - core]


def out_grad(place, attended, grad_mixed, small):
    width = attended.shape[1]
    return pl.pallas_call(
        out_grad_kernel,
        name="out_grad",
        cost_estimate=pl.CostEstimate(flops=500000000, bytes_accessed=4000000, transcendentals=0),
        out_shape=(jax.ShapeDtypeStruct((HEAD_SLOTS // 2, 64, width), BF16),) * 2,
        in_specs=[sspec()] + [vspec()] * 3,
        out_specs=(vspec(),) * 2,
        scratch_shapes=[pltpu.VMEM((HEAD_SLOTS, 64, width), BF16)],
        compiler_params=whole(),
    )(place, attended, grad_mixed, small)


def combine(cotangent, back, picks, gates, mixed, second, routes, gain_two, w_router, w_out):
    rows, width = cotangent.shape
    experts, both, unused = back.shape
    held = experts * both // 2
    return pl.pallas_call(
        combine_kernel,
        name="combine",
        cost_estimate=pl.CostEstimate(flops=1000000000, bytes_accessed=5000000, transcendentals=0),
        out_shape=(
            jax.ShapeDtypeStruct((rows, width), BF16),
            jax.ShapeDtypeStruct((rows, width), F32),
            jax.ShapeDtypeStruct((HEAD_SLOTS, rows // 2, 128), BF16),
            jax.ShapeDtypeStruct((16, width), F32),
        ),
        in_specs=[vspec()] * 10,
        out_specs=(vspec(),) * 4,
        scratch_shapes=[pltpu.VMEM((held, width), BF16), pltpu.VMEM((held, width), BF16)],
        compiler_params=whole(),
    )(
        cotangent,
        back,
        picks,
        gates,
        mixed,
        second,
        routes,
        gain_two,
        w_router,
        w_out,
    )


def input_grad_kernel(tok_ref, gain_ref, grads_ref, wq_ref, wk_ref, wv_ref, mixed_ref, out_ref, dq_s, dk_s, dv_s):
    for j in range(dq_s.shape[1] // 128):
        cols = slice(128 * j, 128 * j + 128)
        one, two = grads_ref[2 * j], grads_ref[2 * j + 1]
        dq_s[:, cols] = jnp.concatenate([one[:128, :64], two[:128, :64]], axis=1)
        dk_s[:, cols] = jnp.concatenate([one[:128, 64:], two[:128, 64:]], axis=1)
        dv_s[:64, cols] = jnp.concatenate([one[128:, :64], two[128:, :64]], axis=1)
        dv_s[64:, cols] = jnp.concatenate([one[128:, 64:], two[128:, 64:]], axis=1)
    grad_normed = dot(dq_s[...], wq_ref[...], NT)
    grad_normed = grad_normed + dot(dk_s[...], wk_ref[...], NT)
    grad_normed = grad_normed + dot(dv_s[...], wv_ref[...], NT)
    inputs = tok_ref[...].astype(F32)
    out_ref[...] = mixed_ref[...] + norm_back(inputs, rms_scale(inputs), gain_ref[...][None, :], grad_normed)


def input_grad(tokens, gain_one, grads, w_query, w_key, w_value, grad_mixed):
    rows, width = tokens.shape
    return pl.pallas_call(
        input_grad_kernel,
        name="input_grad",
        cost_estimate=pl.CostEstimate(flops=500000000, bytes_accessed=5000000, transcendentals=0),
        out_shape=jax.ShapeDtypeStruct((rows, width), F32),
        in_specs=[vspec()] * 7,
        out_specs=vspec(),
        scratch_shapes=[pltpu.VMEM((rows, width), BF16)] * 3,
        compiler_params=whole(),
    )(tokens, gain_one, grads, w_query, w_key, w_value, grad_mixed)


def coordinates(index):
    context, expert = index // 8, index % 8
    return (context // 8 * 2 + expert % 2, expert // 2, context // 2 % 4, context % 2)


def device_at(x, y, z, core):
    return ((x // 2 * 4 + z) * 2 + core) * 8 + y * 2 + x % 2


def shifted(dim, by):
    pairs = []
    for index in range(128):
        place = list(coordinates(index))
        place[dim] = (place[dim] + by) % (2 if dim == 3 else 4)
        pairs.append((index, device_at(*place)))
    return pairs


AXES = ("context", "expert")


def direct_gather(block, dim):
    return jnp.stack([block] + [lax.ppermute(block, AXES, shifted(dim, -by)) for by in (1, 2, 3)])


def gather_last(filled, beside):
    half = filled.shape[0] // 2
    ahead = lax.ppermute(filled, AXES, shifted(1, -1))
    behind = lax.ppermute(filled, AXES, shifted(1, 1))
    ahead, behind, beside = lax.optimization_barrier((ahead, behind, beside))
    across = (
        lax.ppermute(ahead[:half], AXES, shifted(1, -1)),
        lax.ppermute(behind[half:], AXES, shifted(1, 1)),
    )
    mine = (filled, ahead, behind) + across
    other = tuple(lax.ppermute(part, AXES, shifted(3, 1)) for part in mine)
    return mine + other, beside


def unpack_kernel(
    buckets,
    place_ref,
    wq_ref,
    wk_ref,
    wv_ref,
    *rest,
):
    parts, (dwq_ref, dwk_ref, dwv_ref, dwo_ref, bias_ref, small_ref, router_ref, gain_grad_ref) = rest[:10], rest[10:18]
    all_s, sems = rest[18:]
    expert = pl.program_id(0)

    @pl.when(expert == 0)
    def _():
        copies = []
        for core in range(2):
            for i in range(5):
                part = parts[5 * core + i]
                half = all_s.shape[2] // 2
                place = (
                    all_s.at[core, (0, 1, 3)[i]]
                    if i < 3
                    else all_s.at[core, 2, pl.ds(half * (i - 3), half)]
                )
                copies.append(pltpu.make_async_copy(part, place, sems.at[5 * core + i]))
        for copy in copies:
            copy.start()
        for copy in copies:
            copy.wait()

    my_x, my_y, my_z, my_core = (place_ref[i] for i in range(4))
    each = dwq_ref.shape[0]
    half = each // 2
    width = dwq_ref.shape[1]
    rel_y = lax.rem(expert // 2 - my_y + 4, 4)

    def rel(context):
        x = context // 8 * 2 + lax.rem(expert, 2)
        return (
            jnp.where(my_core == context % 2, 0, 1),
            rel_y,
            lax.rem(x - my_x + 4, 4),
            lax.rem(context // 2 % 4 - my_z + 4, 4),
        )

    at = each + half
    bias = []
    for j in range(width // 128):
        cols = slice(128 * j, 128 * j + 128)
        one, two = all_s[rel(2 * j)], all_s[rel(2 * j + 1)]
        left = jnp.concatenate([one[:at, :64], two[:at, :64]], axis=1).astype(F32)
        right = jnp.concatenate([one[:at, 64:], two[:at, 64:]], axis=1).astype(F32)
        dwq_ref[:, cols] = left[:each]
        dwk_ref[:, cols] = right[:each]
        dwv_ref[:half, cols] = left[each:]
        dwv_ref[half:, cols] = right[each:]
        one, two = one[at:].astype(F32), two[at:].astype(F32)
        bias += [one[:1], two[:1]]
        for i, block in enumerate((one, two)):
            for k in range(width // 128):
                dwo_ref[2 * j + i, :, 128 * k : 128 * k + 128] = block[16 + 8 * k : 24 + 8 * k]
    bias_ref[...] = jnp.concatenate(bias, axis=0)[:, :buckets]
    block = all_s[rel(width // 64)].astype(F32)
    small = jnp.concatenate(
        [block[at + 16 + 8 * k : at + 24 + 8 * k] for k in range(width // 128)], axis=1
    )

    @pl.when(expert == 0)
    def _():
        router_ref[...] = small

    @pl.when(expert == 1)
    def _():
        small_ref[...] = small

    prod = (
        dwq_ref[...] * wq_ref[...].astype(F32)
        + dwk_ref[...] * wk_ref[...].astype(F32)
        + dwv_ref[...] * wv_ref[...].astype(F32)
    )
    gain_grad_ref[...] = dot(jnp.ones((8, width), F32), prod, NT, HIGHEST)


def unpack(place, parts, w_query, w_key, w_value, heads, buckets, experts):
    width = w_query.shape[0]
    each = width // experts
    held = parts[0].shape[2]
    rows = pl.BlockSpec((each, width), lambda i: (i, 0))
    return pl.pallas_call(
        lambda *refs: unpack_kernel(buckets, *refs),
        name="unpack",
        cost_estimate=pl.CostEstimate(flops=1000000000, bytes_accessed=24000000, transcendentals=0),
        grid=(experts,),
        out_shape=(
            jax.ShapeDtypeStruct((width, width), F32),
            jax.ShapeDtypeStruct((width, width), F32),
            jax.ShapeDtypeStruct((width, width), F32),
            jax.ShapeDtypeStruct((heads, experts, 8, width), F32),
            jax.ShapeDtypeStruct((heads, buckets), F32),
            jax.ShapeDtypeStruct((8, width), F32),
            jax.ShapeDtypeStruct((8, width), F32),
            jax.ShapeDtypeStruct((experts, 8, each), F32),
        ),
        in_specs=[sspec(), rows, rows, rows] + [pl.BlockSpec(memory_space=pl.ANY)] * 10,
        out_specs=(
            rows,
            rows,
            rows,
            pl.BlockSpec((heads, None, 8, width), lambda i: (0, i, 0, 0)),
            pl.BlockSpec((heads, buckets), lambda i: (0, 0)),
            pl.BlockSpec((8, width), lambda i: (0, 0)),
            pl.BlockSpec((8, width), lambda i: (0, 0)),
            pl.BlockSpec((None, 8, each), lambda i: (i, 0, 0)),
        ),
        scratch_shapes=[
            pltpu.VMEM((2, 4, 4, 4, held, 128), BF16),
            pltpu.SemaphoreType.DMA((10,)),
        ],
        compiler_params=whole(),
    )(place, w_query, w_key, w_value, *parts)


def add_kernel(in_ref, out_ref):
    total = in_ref[0].astype(F32)
    for i in range(1, in_ref.shape[0]):
        total = total + in_ref[i].astype(F32)
    out_ref[...] = total.astype(BF16)


def add_up(received):
    return pl.pallas_call(
        add_kernel,
        name="add_up",
        out_shape=jax.ShapeDtypeStruct(received.shape[1:], BF16),
        in_specs=[vspec()],
        out_specs=vspec(),
        compiler_params=whole(),
    )(received)


def shards(
    tokens,
    gain_one,
    w_query,
    w_key,
    w_value,
    w_out,
    rel_table,
    gain_two,
    w_router,
    expert_in,
    expert_out,
    routes,
    cotangent,
):
    width = tokens.shape[2]
    heads, buckets = rel_table.shape
    experts = lax.axis_size("expert")
    inputs, grad_out, routes_here = tokens[0], cotangent[0], routes[0]
    context = lax.axis_index("context")
    head = jnp.minimum(context, heads - 1).astype(jnp.int32).reshape(1)

    own_weights = jnp.concatenate([expert_in[0].T, expert_out[0].T], axis=0)
    shared = lax.all_gather(own_weights, "context", axis=0, tiled=False)
    normed, packed = project(inputs, gain_one, w_query, w_key, w_value)
    qkv = lax.all_to_all(packed, "context", split_axis=0, concat_axis=0, tiled=True)
    expert = lax.axis_index("expert")
    place = jnp.stack(coordinates(context * experts + expert)).astype(jnp.int32)
    normed, qkv = lax.optimization_barrier((normed, qkv))
    normed_two = jnp.stack([normed, lax.ppermute(normed, AXES, shifted(0, 2))])

    out_heads, keep, lse = attend(head, rel_table, qkv)
    out_rows = lax.all_to_all(out_heads, "context", split_axis=0, concat_axis=0, tiled=True)
    send, attended, mixed, second, picks, gates = dispatch(
        inputs, grad_out, out_rows, w_out, gain_two, w_router, routes_here, experts
    )
    received = lax.all_to_all(send, "expert", split_axis=0, concat_axis=0, tiled=True)
    normed_two, received, shared = lax.optimization_barrier((normed_two, received, shared))
    normed_mine = direct_gather(normed_two, 2)
    back, weight_grads = expert_both(received, shared)
    returned = lax.all_to_all(back, "expert", split_axis=0, concat_axis=0, tiled=True)
    normed_mine, returned = lax.optimization_barrier((normed_mine, returned))
    normed_other = lax.ppermute(normed_mine, AXES, shifted(3, 1))
    own_grads = lax.psum_scatter(weight_grads, "context", scatter_dimension=0, tiled=False)
    block_out, grad_mixed, grad_heads, small = combine(
        grad_out, returned, picks, gates, mixed, second, routes_here, gain_two, w_router, w_out
    )
    keep_sums, pass_sums = out_grad(place, attended, grad_mixed, small)
    other_sums = lax.ppermute(pass_sums, AXES, shifted(3, 1))
    sums = (keep_sums.astype(F32) + other_sums.astype(F32)).astype(BF16)
    grad_here = lax.all_to_all(grad_heads, "context", split_axis=0, concat_axis=0, tiled=True)
    same_core = [[2 * i + core for i in range(8)] for core in range(2)]
    sums, grad_here = lax.optimization_barrier((sums, grad_here))
    sums = lax.all_to_all(
        sums, "context", split_axis=0, concat_axis=0, axis_index_groups=same_core, tiled=True
    )

    dqkv, bias = attend_back(head, rel_table, qkv, grad_here, keep, lse)
    terms = head_grads(place, dqkv, normed_mine, normed_other, bias, sums, experts)
    terms = lax.all_to_all(terms, "expert", split_axis=0, concat_axis=0, tiled=True)
    filled, dqkv = lax.optimization_barrier((direct_gather(direct_gather(add_up(terms), 2), 0), dqkv))
    grads = lax.all_to_all(dqkv, "context", split_axis=0, concat_axis=0, tiled=True)
    own_grads = own_grads.astype(F32)
    hidden = own_grads.shape[0] // 2
    parts, (grads, grad_in, grad_back) = gather_last(
        filled, (grads, own_grads[:hidden], own_grads[hidden:])
    )
    grad_tokens = input_grad(inputs, gain_one, grads, w_query, w_key, w_value, grad_mixed)

    dwq, dwk, dwv, dwo, bias, small, router, gain_grad = unpack(
        place, parts, w_query, w_key, w_value, heads, buckets, experts
    )
    return (
        block_out[None],
        grad_tokens[None],
        gain_grad[:, 0, :].reshape(width) / gain_one,
        dwq,
        dwk,
        dwv,
        dwo.reshape(width, width),
        bias,
        small[0],
        router.T,
        grad_in.T[None],
        grad_back.T[None],
    )


def solution(mesh):
    return jax.shard_map(
        shards,
        mesh=mesh,
        in_specs=(
            P("expert", "context", None),
            P(),
            P(),
            P(),
            P(),
            P(),
            P(),
            P(),
            P(),
            P("expert", None, "context"),
            P("expert", None, "context"),
            P("expert", "context", None),
            P("expert", "context", None),
        ),
        out_specs=(
            P("expert", "context", None),
            P("expert", "context", None),
            P(),
            P(),
            P(),
            P(),
            P(),
            P(),
            P(),
            P(),
            P("expert", None, "context"),
            P("expert", None, "context"),
        ),
        check_vma=False,
    )
```

```python
import math

import jax
import jax.numpy as jnp
from jax import lax
from jax.experimental import pallas as pl
from jax.experimental.pallas import tpu as pltpu
from jax.sharding import PartitionSpec as P

MAX_DIST = 128
EPSILON = 1e-06
NEG_LARGE = -1e30
BLK = 256
HEAD_SLOTS = 16

F32 = jnp.float32
BF16 = jnp.bfloat16
HIGHEST = lax.Precision.HIGHEST

NN = (((1,), (0,)), ((), ()))
NT = (((1,), (1,)), ((), ()))
TN = (((0,), (0,)), ((), ()))


def dot(a, b, dims=NN, precision=None):
    return lax.dot_general(a, b, dims, precision=precision, preferred_element_type=F32)


def bucket_starts(buckets, far_reach):
    span = buckets // 2
    rest = [
        int(math.ceil(span * (far_reach / span) ** (step / (buckets - span))))
        for step in range(1, buckets - span)
    ]
    return list(range(span + 1)) + rest


def rms_scale(values):
    return lax.rsqrt(jnp.mean(values * values, axis=-1, keepdims=True) + EPSILON)


def norm_back(values, inv_root, gain_vec, grad_normed):
    weighted = grad_normed * gain_vec
    cubed = inv_root * inv_root * inv_root
    return inv_root * weighted - values * cubed * jnp.mean(
        weighted * values, axis=-1, keepdims=True
    )


def whole(vmem_mib=56):
    return pltpu.CompilerParams(vmem_limit_bytes=vmem_mib * 2**20)


def vspec():
    return pl.BlockSpec(memory_space=pltpu.VMEM)


def sspec():
    return pl.BlockSpec(memory_space=pltpu.SMEM)


def project_kernel(tok_ref, gain_ref, wq_ref, wk_ref, wv_ref, normed_ref, out_ref):
    inputs = tok_ref[...].astype(F32)
    normed = (inputs * rms_scale(inputs) * gain_ref[...][None, :]).astype(BF16)
    rows, width = normed.shape
    half = rows // 2
    normed_ref[...] = normed
    queries = (dot(normed, wq_ref[...]).astype(BF16).astype(F32) * 0.125).astype(BF16)
    keys = dot(normed, wk_ref[...]).astype(BF16)
    values = dot(normed, wv_ref[...]).astype(BF16)
    heads = width // 64
    for h in range(heads):
        cols = slice(64 * h, 64 * h + 64)
        out_ref[h, :rows, :] = jnp.concatenate([queries[:, cols], keys[:, cols]], axis=1)
        out_ref[h, rows:, :] = jnp.concatenate([values[:half, cols], values[half:, cols]], axis=1)
    for h in range(heads, HEAD_SLOTS):
        out_ref[h] = jnp.zeros_like(out_ref[h])


def project(tokens, gain_one, w_query, w_key, w_value):
    rows, width = tokens.shape
    return pl.pallas_call(
        project_kernel,
        name="project",
        cost_estimate=pl.CostEstimate(flops=500000000, bytes_accessed=6000000, transcendentals=0),
        out_shape=(
            jax.ShapeDtypeStruct((rows, width), BF16),
            jax.ShapeDtypeStruct((HEAD_SLOTS, rows + rows // 2, 128), BF16),
        ),
        in_specs=[vspec()] * 5,
        out_specs=(vspec(), vspec()),
        compiler_params=whole(),
    )(tokens, gain_one, w_query, w_key, w_value)


def bias_tile(table_ref, head, buckets, rows_first, shape, key_dim):
    sign = [1, -1] if key_dim == 1 else [-1, 1]
    dist = (
        rows_first
        + sign[0] * lax.broadcasted_iota(jnp.int32, shape, 0)
        + sign[1] * lax.broadcasted_iota(jnp.int32, shape, 1)
    )
    far = table_ref[head, buckets - 1]
    tile = jnp.full(shape, NEG_LARGE, F32)
    for b, start in enumerate(bucket_starts(buckets, MAX_DIST)):
        tile = jnp.where(dist >= start, table_ref[head, b] - far, tile)
    return tile


def unpack_qkv(qkv_ref, q_s, k_s, v_s, ones_lane):
    count = qkv_ref.shape[0]
    lane = lax.broadcasted_iota(jnp.int32, (64, 64), 1)
    one = jnp.where(lane == 0, 1.0, 0.0).astype(BF16)
    for c in range(count):
        pair = qkv_ref[c, :128, :]
        q_s[128 * c : 128 * c + 128, :] = pair[:, :64]
        k_s[128 * c : 128 * c + 128, :] = pair[:, 64:]
        two = qkv_ref[c, 128:192, :]
        top, bottom = two[:, :64], two[:, 64:]
        if ones_lane:
            top = jnp.concatenate([top, one], axis=1)
            bottom = jnp.concatenate([bottom, one], axis=1)
        v_s[128 * c : 128 * c + 64, :] = top
        v_s[128 * c + 64 : 128 * c + 128, :] = bottom


def attend_kernel(buckets, head_ref, table_ref, qkv_ref, out_ref, keep_ref, lse_ref, q_s, k_s, v_s, bias_s):
    head = head_ref[0]
    unpack_qkv(qkv_ref, q_s, k_s, v_s, True)
    bias_s[0] = bias_tile(table_ref, head, buckets, BLK, (BLK, BLK), 1)
    bias_s[1] = bias_tile(table_ref, head, buckets, 0, (BLK, BLK), 1)
    blocks = q_s.shape[0] // BLK

    for qb in range(blocks):
        query = q_s[BLK * qb : BLK * qb + BLK, :]
        near = max(qb - 1, 0) * BLK
        parts = []
        if near:
            parts.append((0, dot(query, k_s[:near, :], NT)))
        if qb:
            parts.append((near, dot(query, k_s[near : near + BLK, :], NT) + bias_s[0]))
        parts.append((BLK * qb, dot(query, k_s[BLK * qb : BLK * qb + BLK, :], NT) + bias_s[1]))
        top = parts[-1][1]
        top = jnp.maximum(top[:, :128], top[:, 128:])
        for unused, scores in parts[:-1]:
            for j in range(scores.shape[1] // 128):
                top = jnp.maximum(top, scores[:, 128 * j : 128 * j + 128])
        top = jnp.max(top, axis=1, keepdims=True)
        total = jnp.zeros((BLK, 128), F32)
        for first, scores in parts:
            weights = jnp.exp(scores - top).astype(BF16)
            total = total + dot(weights, v_s[first : first + scores.shape[1], :])
        norm = total[:, 64:65]
        out = total[:, :64] / norm
        log_total = top + jnp.log(norm)
        spread = jnp.broadcast_to(log_total, (BLK, 128)).T
        lse_ref[qb] = spread[:8, :]
        for part in range(BLK // 128):
            two = jnp.concatenate(
                [out[128 * part : 128 * part + 64], out[128 * part + 64 : 128 * part + 128]], axis=1
            )
            place = qb * (BLK // 128) + part
            out_ref[place] = two.astype(BF16)
            keep_ref[place] = two


def attend(head, rel_table, qkv):
    count = qkv.shape[0]
    length = 128 * count
    blocks = length // BLK
    return pl.pallas_call(
        lambda *refs: attend_kernel(rel_table.shape[1], *refs),
        name="attend",
        cost_estimate=pl.CostEstimate(flops=7000000000, bytes_accessed=3000000, transcendentals=3000000),
        out_shape=(
            jax.ShapeDtypeStruct((count, 64, 128), BF16),
            jax.ShapeDtypeStruct((count, 64, 128), F32),
            jax.ShapeDtypeStruct((blocks, 8, BLK), F32),
        ),
        in_specs=[sspec(), sspec(), vspec()],
        out_specs=(vspec(), vspec(), vspec()),
        scratch_shapes=[
            pltpu.VMEM((length, 64), BF16),
            pltpu.VMEM((length, 64), BF16),
            pltpu.VMEM((length, 128), BF16),
            pltpu.VMEM((2, BLK, BLK), F32),
        ],
        compiler_params=whole(),
    )(head, rel_table, qkv)


def attend_back_kernel(
    buckets,
    head_ref,
    table_ref,
    qkv_ref,
    go_ref,
    keep_ref,
    lse_ref,
    dqkv_ref,
    bias_ref,
    q_s,
    k_s,
    v_s,
    kt_s,
    go_s,
    delta_s,
    dq_s,
    dk_s,
    dv_s,
    bias_s,
    acc_s,
):
    head = head_ref[0]
    length = q_s.shape[0]
    count = qkv_ref.shape[0]
    blocks = length // BLK
    unpack_qkv(qkv_ref, q_s, k_s, v_s, False)
    for c in range(count):
        kt_s[:, 128 * c : 128 * c + 128] = k_s[128 * c : 128 * c + 128, :].T
        two, kept = go_ref[c], keep_ref[c]
        go_s[128 * c : 128 * c + 64, :] = two[:, :64]
        go_s[128 * c + 64 : 128 * c + 128, :] = two[:, 64:]
        both = two.astype(F32) * kept
        turned = both.T
        delta = jnp.concatenate(
            [
                jnp.sum(turned[:64], axis=0, keepdims=True),
                jnp.sum(turned[64:], axis=0, keepdims=True),
            ],
            axis=1,
        )
        delta_s[:, 128 * c : 128 * c + 128] = jnp.broadcast_to(delta, (8, 128))
    bias_s[0] = bias_tile(table_ref, head, buckets, BLK, (BLK, BLK), 0)
    bias_s[1] = bias_tile(table_ref, head, buckets, 0, (BLK, BLK), 0)
    acc_s[...] = jnp.zeros_like(acc_s)
    dk_s[...] = jnp.zeros_like(dk_s)
    dv_s[...] = jnp.zeros_like(dv_s)

    far_sum = jnp.zeros((8, BLK), F32)
    for qb in range(blocks):
        rows = slice(BLK * qb, BLK * qb + BLK)
        query, grad = q_s[rows, :], go_s[rows, :]
        lse = lse_ref[qb][:1, :]
        delta = delta_s[:1, rows]
        grad_query = jnp.zeros((64, BLK), F32)
        for kb in range(qb + 1):
            cols = slice(BLK * kb, BLK * kb + BLK)
            near = kb - qb + 1
            scores = dot(k_s[cols, :], query, NT)
            if near >= 0:
                scores = scores + bias_s[near]
            probs = jnp.exp(scores - lse)
            grad_probs = dot(v_s[cols, :], grad, NT)
            grad_scores = (probs * (grad_probs - delta)).astype(BF16)
            dv_s[cols, :] += dot(probs.astype(BF16), grad)
            dk_s[cols, :] += dot(grad_scores, query)
            grad_query = grad_query + dot(kt_s[:, cols], grad_scores)
            wide = grad_scores.astype(F32)
            if near < 0:
                far_sum = far_sum + jnp.sum(wide.reshape(BLK // 8, 8, BLK), axis=0)
            else:
                acc_s[near] += wide
        dq_s[:, rows] = grad_query

    for c in range(count):
        here = slice(128 * c, 128 * c + 128)
        dq_t = (dq_s[:, here] * 0.125).astype(BF16)
        dk = dk_s[here, :].astype(BF16)
        dv = dv_s[here, :].astype(BF16)
        dqkv_ref[c, :128, :] = jnp.concatenate([dq_t.T, dk], axis=1)
        dqkv_ref[c, 128:192, :] = jnp.concatenate([dv[:64], dv[64:]], axis=1)

    lane = lax.broadcasted_iota(jnp.int32, (16, 128), 1)
    dist0 = (
        BLK
        - lax.broadcasted_iota(jnp.int32, (BLK, BLK), 0)
        + lax.broadcasted_iota(jnp.int32, (BLK, BLK), 1)
    )
    dist1 = dist0 - BLK

    def total(values):
        return jnp.sum(jnp.sum(values, axis=1, keepdims=True), axis=0, keepdims=True)

    starts = bucket_starts(buckets, MAX_DIST)
    row = jnp.zeros((16, 128), F32)
    above = None
    for b in reversed(range(buckets)):
        reach = total(
            jnp.where(dist0 >= starts[b], acc_s[0], 0.0)
            + jnp.where(dist1 >= starts[b], acc_s[1], 0.0)
        )
        mine = reach + total(far_sum) if b == buckets - 1 else reach - above
        above = reach
        row = jnp.where(lane == b, mine, row)
    bias_ref[...] = row


def attend_back(head, rel_table, qkv, grad_heads, keep, lse):
    count = qkv.shape[0]
    length = 128 * count
    return pl.pallas_call(
        lambda *refs: attend_back_kernel(rel_table.shape[1], *refs),
        name="attend_back",
        cost_estimate=pl.CostEstimate(flops=14000000000, bytes_accessed=4000000, transcendentals=3000000),
        out_shape=(
            jax.ShapeDtypeStruct(qkv.shape, BF16),
            jax.ShapeDtypeStruct((16, 128), F32),
        ),
        in_specs=[sspec(), sspec()] + [vspec()] * 4,
        out_specs=(vspec(), vspec()),
        scratch_shapes=[
            pltpu.VMEM((length, 64), BF16),
            pltpu.VMEM((length, 64), BF16),
            pltpu.VMEM((length, 64), BF16),
            pltpu.VMEM((64, length), BF16),
            pltpu.VMEM((length, 64), BF16),
            pltpu.VMEM((8, length), F32),
            pltpu.VMEM((64, length), F32),
            pltpu.VMEM((length, 64), F32),
            pltpu.VMEM((length, 64), F32),
            pltpu.VMEM((2, BLK, BLK), F32),
            pltpu.VMEM((2, BLK, BLK), F32),
        ],
        compiler_params=whole(),
    )(head, rel_table, qkv, grad_heads, keep, lse)


def head_grads_kernel(place_ref, dqkv_ref, mine_ref, other_ref, bias_ref, sums_ref, out_ref, turned_s):
    count = dqkv_ref.shape[0]
    width = mine_ref.shape[-1]
    held = mine_ref.shape[0] * mine_ref.shape[1]
    my_x, my_z, my_core = place_ref[0] // 2, place_ref[2], place_ref[3]
    for i in range(count):
        core, z, x = i // 8, i % 8 // 2, i % 2
        there = (lax.rem(my_x + x, 2) * 4 + lax.rem(my_z + z, 4)) * 2 + lax.rem(my_core + core, 2)
        turned_s[i] = dqkv_ref[there]
    pairs, third = 0.0, 0.0
    for core, normed_ref in enumerate((mine_ref, other_ref)):
        normed = normed_ref[...].reshape(held, 128, width)
        here = slice(held * core, held * core + held)
        two = turned_s[here, 128:192, :].reshape(held * 64, 128)
        for half in range(2):
            rows = slice(64 * half, 64 * half + 64)
            part = normed[:, rows, :].reshape(held * 64, width)
            pairs = pairs + dot(turned_s[here, rows, :].reshape(held * 64, 128), part, TN)
            third = third + dot(two, part, TN)[rows]
    pairs, third = pairs.T, third.T
    total = sums_ref[0].astype(F32)
    for c in range(1, sums_ref.shape[0]):
        total = total + sums_ref[c].astype(F32)
    shares = out_ref.shape[0]
    each = width // shares
    row = bias_ref[...].astype(BF16)
    for s in range(shares):
        mine = slice(each * s, each * s + each)
        out_ref[s, :each, :] = pairs[mine].astype(BF16)
        last = third[mine].astype(BF16)
        out_ref[s, each : each + each // 2, :] = jnp.concatenate(
            [last[: each // 2], last[each // 2 :]], axis=1
        )
        at = each + each // 2
        out_ref[s, at : at + 16, :] = row
        part = total[8 * s : 8 * s + 8]
        out_ref[s, at + 16 :, :] = jnp.concatenate(
            [part[:, 128 * j : 128 * j + 128] for j in range(width // 128)], axis=0
        ).astype(BF16)


def head_grads(place, dqkv, mine, other, bias, sums, shares):
    width = mine.shape[-1]
    each = width // shares
    held = each + each // 2 + 16 + width // 16
    return pl.pallas_call(
        head_grads_kernel,
        name="head_grads",
        cost_estimate=pl.CostEstimate(flops=3000000000, bytes_accessed=8000000, transcendentals=0),
        out_shape=jax.ShapeDtypeStruct((shares, held, 128), BF16),
        in_specs=[sspec()] + [vspec()] * 5,
        out_specs=vspec(),
        scratch_shapes=[pltpu.VMEM(dqkv.shape, BF16)],
        compiler_params=whole(),
    )(place, dqkv, mine, other, bias, sums)


def heads_to_rows(ref, scratch):
    for j in range(scratch.shape[1] // 128):
        one, two = ref[2 * j], ref[2 * j + 1]
        scratch[:64, 128 * j : 128 * j + 128] = jnp.concatenate([one[:, :64], two[:, :64]], axis=1)
        scratch[64:, 128 * j : 128 * j + 128] = jnp.concatenate([one[:, 64:], two[:, 64:]], axis=1)


def dispatch_kernel(
    experts,
    capacity,
    tok_ref,
    cot_ref,
    heads_ref,
    wo_ref,
    gain_ref,
    wr_ref,
    routes_ref,
    send_ref,
    att_ref,
    mixed_ref,
    second_ref,
    pick_ref,
    gates_ref,
):
    rows = tok_ref.shape[0]
    heads_to_rows(heads_ref, att_ref)
    mixed = tok_ref[...].astype(F32) + dot(att_ref[...], wo_ref[...])
    mixed_ref[...] = mixed
    second = (mixed * rms_scale(mixed) * gain_ref[...][None, :]).astype(BF16)
    second_ref[...] = second
    logits = dot(second, wr_ref[...])
    ids = lax.broadcasted_iota(jnp.int32, (rows, experts), 1)
    routes = routes_ref[...]
    marks = [(routes[:, k : k + 1] == ids).astype(F32) for k in range(2)]
    earlier = (
        lax.broadcasted_iota(jnp.int32, (rows, rows), 0)
        > lax.broadcasted_iota(jnp.int32, (rows, rows), 1)
    ).astype(F32)
    ranks = dot(earlier.astype(BF16), (marks[0] + marks[1]).astype(BF16))
    chosen = [jnp.sum(m * logits, axis=1, keepdims=True) for m in marks]
    top = jnp.maximum(chosen[0], chosen[1])
    exps = [jnp.exp(c - top) for c in chosen]
    gates = [e / (exps[0] + exps[1]) for e in exps]
    slot_ids = lax.broadcasted_iota(jnp.int32, (rows, experts * capacity), 1)
    grad_out = cot_ref[...].astype(F32)
    picks = []
    for k in range(2):
        slot = jnp.sum(marks[k] * ranks, axis=1, keepdims=True).astype(jnp.int32)
        place = routes[:, k : k + 1] * capacity + slot
        picks.append((place == slot_ids).astype(F32).astype(BF16))
        pick_ref[k] = picks[k]
    send_rows = dot(picks[0] + picks[1], second, TN).astype(BF16)
    send_grads = dot(picks[0], (gates[0] * grad_out).astype(BF16), TN) + dot(
        picks[1], (gates[1] * grad_out).astype(BF16), TN
    )
    send_grads = send_grads.astype(BF16)
    for e in range(experts):
        here = slice(capacity * e, capacity * e + capacity)
        send_ref[e, :capacity, :] = send_rows[here]
        send_ref[e, capacity:, :] = send_grads[here]
    lane = lax.broadcasted_iota(jnp.int32, (rows, 128), 1)
    gates_ref[...] = jnp.where(lane == 0, gates[0], gates[1])


def dispatch(tokens, cotangent, heads, w_out, gain_two, w_router, routes, experts):
    rows, width = tokens.shape
    capacity = 3 * rows // experts
    return pl.pallas_call(
        lambda *refs: dispatch_kernel(experts, capacity, *refs),
        name="dispatch",
        cost_estimate=pl.CostEstimate(flops=500000000, bytes_accessed=4000000, transcendentals=0),
        out_shape=(
            jax.ShapeDtypeStruct((experts, 2 * capacity, width), BF16),
            jax.ShapeDtypeStruct((rows, width), BF16),
            jax.ShapeDtypeStruct((rows, width), F32),
            jax.ShapeDtypeStruct((rows, width), BF16),
            jax.ShapeDtypeStruct((2, rows, experts * capacity), BF16),
            jax.ShapeDtypeStruct((rows, 128), F32),
        ),
        in_specs=[vspec()] * 7,
        out_specs=(vspec(),) * 6,
        compiler_params=whole(),
    )(tokens, cotangent, heads, w_out, gain_two, w_router, routes)


def expert_kernel(rows_ref, w_ref, back_ref, dw_ref, x_s, g_s, y_s, dx_s):
    step = pl.program_id(0)
    sources, both, width = rows_ref.shape
    capacity = both // 2

    @pl.when(step == 0)
    def _():
        for s in range(sources):
            x_s[capacity * s : capacity * s + capacity, :] = rows_ref[s, :capacity, :]
            g_s[capacity * s : capacity * s + capacity, :] = rows_ref[s, capacity:, :]
        y_s[...] = jnp.zeros_like(y_s)
        dx_s[...] = jnp.zeros_like(dx_s)

    each = w_ref.shape[1] // 2
    w_in = w_ref[:, :each, :].reshape(-1, width)
    w_back = w_ref[:, each:, :].reshape(-1, width)
    pre = dot(x_s[...], w_in, NT)
    square = pre * pre
    curve = jnp.tanh(0.7978845608 * (pre + 0.044715 * square * pre))
    act = (0.5 * pre * (1.0 + curve)).astype(BF16)
    slope = 0.5 * (1.0 + curve) + 0.5 * pre * (1.0 - curve * curve) * (
        0.7978845608 * (1.0 + 3.0 * 0.044715 * square)
    )
    grad_pre = (dot(g_s[...], w_back, NT) * slope).astype(BF16)
    y_s[...] += dot(act, w_back)
    dx_s[...] += dot(grad_pre, w_in)
    dw_ref[:, :each, :] = dot(grad_pre, x_s[...], TN).astype(BF16).reshape(-1, each, width)
    dw_ref[:, each:, :] = dot(act, g_s[...], TN).astype(BF16).reshape(-1, each, width)

    @pl.when(step == pl.num_programs(0) - 1)
    def _():
        for s in range(sources):
            here = slice(capacity * s, capacity * s + capacity)
            back_ref[s, :capacity, :] = y_s[here, :].astype(BF16)
            back_ref[s, capacity:, :] = dx_s[here, :].astype(BF16)


AT_ONCE = 4


def expert_both(rows, shared):
    sources, both, width = rows.shape
    count, given, unused = shared.shape
    held = sources * both // 2
    return pl.pallas_call(
        expert_kernel,
        name="expert_both",
        cost_estimate=pl.CostEstimate(flops=18000000000, bytes_accessed=22000000, transcendentals=5000000),
        grid=(count // AT_ONCE,),
        out_shape=(
            jax.ShapeDtypeStruct(rows.shape, BF16),
            jax.ShapeDtypeStruct(shared.shape, BF16),
        ),
        in_specs=[
            pl.BlockSpec(rows.shape, lambda i: (0, 0, 0)),
            pl.BlockSpec((AT_ONCE, given, width), lambda i: (i, 0, 0)),
        ],
        out_specs=(
            pl.BlockSpec(rows.shape, lambda i: (0, 0, 0)),
            pl.BlockSpec((AT_ONCE, given, width), lambda i: (i, 0, 0)),
        ),
        scratch_shapes=[
            pltpu.VMEM((held, width), BF16),
            pltpu.VMEM((held, width), BF16),
            pltpu.VMEM((held, width), F32),
            pltpu.VMEM((held, width), F32),
        ],
        compiler_params=whole(),
    )(rows, shared)


def combine_kernel(
    cot_ref,
    back_ref,
    pick_ref,
    gates_ref,
    mixed_ref,
    second_ref,
    routes_ref,
    gain_ref,
    wr_ref,
    wo_ref,
    out_ref,
    grad_mixed_ref,
    heads_ref,
    small_ref,
    y_s,
    dx_s,
):
    experts, both, width = back_ref.shape
    capacity = both // 2
    rows = cot_ref.shape[0]
    for s in range(experts):
        here = slice(capacity * s, capacity * s + capacity)
        y_s[here, :] = back_ref[s, :capacity, :]
        dx_s[here, :] = back_ref[s, capacity:, :]
    grad_out = cot_ref[...].astype(F32)
    mixed = mixed_ref[...]
    gates = [gates_ref[:, k : k + 1] for k in range(2)]
    picked = [dot(pick_ref[k], y_s[...]) for k in range(2)]
    out_ref[...] = (mixed + (gates[0] * picked[0] + gates[1] * picked[1])).astype(BF16)
    grad_gates = [jnp.sum(p * grad_out, axis=1, keepdims=True) for p in picked]
    mean = gates[0] * grad_gates[0] + gates[1] * grad_gates[1]
    grad_chosen = [gates[k] * (grad_gates[k] - mean) for k in range(2)]
    ids = lax.broadcasted_iota(jnp.int32, (rows, experts), 1)
    routes = routes_ref[...]
    grad_logits = jnp.where(routes[:, :1] == ids, grad_chosen[0], 0.0) + jnp.where(
        routes[:, 1:2] == ids, grad_chosen[1], 0.0
    )
    grad_second = dot(pick_ref[0], dx_s[...]) + dot(pick_ref[1], dx_s[...])
    grad_second = grad_second + dot(grad_logits, wr_ref[...].astype(F32), NT, HIGHEST)
    second = second_ref[...]
    grad_router = dot(grad_logits, second.astype(F32), TN, HIGHEST)
    scale = rms_scale(mixed)
    grad_gain = jnp.sum(grad_second * mixed * scale, axis=0, keepdims=True)
    grad_mixed = grad_out + norm_back(mixed, scale, gain_ref[...][None, :], grad_second)
    grad_mixed_ref[...] = grad_mixed
    grad_branch = grad_mixed.astype(BF16)
    grad_att = dot(grad_branch, wo_ref[...], NT).astype(BF16)
    heads = width // 64
    for h in range(heads):
        cols = slice(64 * h, 64 * h + 64)
        heads_ref[h] = jnp.concatenate([grad_att[:64, cols], grad_att[64:, cols]], axis=1)
    for h in range(heads, HEAD_SLOTS):
        heads_ref[h] = jnp.zeros_like(heads_ref[h])
    small_ref[...] = jnp.concatenate([grad_router, jnp.broadcast_to(grad_gain, (8, width))], axis=0)


def out_grad_kernel(place_ref, att_ref, grad_mixed_ref, small_ref, keep_ref, pass_ref, all_s):
    grad_wo = dot(att_ref[...], grad_mixed_ref[...].astype(BF16), TN).astype(BF16)
    slots, each, width = all_s.shape
    used = width // each
    for c in range(used):
        all_s[c] = grad_wo[each * c : each * c + each]
    for c in range(used, slots):
        all_s[c] = jnp.zeros_like(all_s[c])
    all_s[used, :16, :] = small_ref[...].astype(BF16)
    core = place_ref[3]
    for c in range(slots // 2):
        keep_ref[c] = all_s[2 * c + core]
        pass_ref[c] = all_s[2 * c + 1 - core]


def out_grad(place, attended, grad_mixed, small):
    width = attended.shape[1]
    return pl.pallas_call(
        out_grad_kernel,
        name="out_grad",
        cost_estimate=pl.CostEstimate(flops=500000000, bytes_accessed=4000000, transcendentals=0),
        out_shape=(jax.ShapeDtypeStruct((HEAD_SLOTS // 2, 64, width), BF16),) * 2,
        in_specs=[sspec()] + [vspec()] * 3,
        out_specs=(vspec(),) * 2,
        scratch_shapes=[pltpu.VMEM((HEAD_SLOTS, 64, width), BF16)],
        compiler_params=whole(),
    )(place, attended, grad_mixed, small)


def combine(cotangent, back, picks, gates, mixed, second, routes, gain_two, w_router, w_out):
    rows, width = cotangent.shape
    experts, both, unused = back.shape
    held = experts * both // 2
    return pl.pallas_call(
        combine_kernel,
        name="combine",
        cost_estimate=pl.CostEstimate(flops=1000000000, bytes_accessed=5000000, transcendentals=0),
        out_shape=(
            jax.ShapeDtypeStruct((rows, width), BF16),
            jax.ShapeDtypeStruct((rows, width), F32),
            jax.ShapeDtypeStruct((HEAD_SLOTS, rows // 2, 128), BF16),
            jax.ShapeDtypeStruct((16, width), F32),
        ),
        in_specs=[vspec()] * 10,
        out_specs=(vspec(),) * 4,
        scratch_shapes=[pltpu.VMEM((held, width), BF16), pltpu.VMEM((held, width), BF16)],
        compiler_params=whole(),
    )(
        cotangent,
        back,
        picks,
        gates,
        mixed,
        second,
        routes,
        gain_two,
        w_router,
        w_out,
    )


def input_grad_kernel(tok_ref, gain_ref, grads_ref, wq_ref, wk_ref, wv_ref, mixed_ref, out_ref, dq_s, dk_s, dv_s):
    for j in range(dq_s.shape[1] // 128):
        cols = slice(128 * j, 128 * j + 128)
        one, two = grads_ref[2 * j], grads_ref[2 * j + 1]
        dq_s[:, cols] = jnp.concatenate([one[:128, :64], two[:128, :64]], axis=1)
        dk_s[:, cols] = jnp.concatenate([one[:128, 64:], two[:128, 64:]], axis=1)
        dv_s[:64, cols] = jnp.concatenate([one[128:, :64], two[128:, :64]], axis=1)
        dv_s[64:, cols] = jnp.concatenate([one[128:, 64:], two[128:, 64:]], axis=1)
    grad_normed = dot(dq_s[...], wq_ref[...], NT)
    grad_normed = grad_normed + dot(dk_s[...], wk_ref[...], NT)
    grad_normed = grad_normed + dot(dv_s[...], wv_ref[...], NT)
    inputs = tok_ref[...].astype(F32)
    out_ref[...] = mixed_ref[...] + norm_back(inputs, rms_scale(inputs), gain_ref[...][None, :], grad_normed)


def input_grad(tokens, gain_one, grads, w_query, w_key, w_value, grad_mixed):
    rows, width = tokens.shape
    return pl.pallas_call(
        input_grad_kernel,
        name="input_grad",
        cost_estimate=pl.CostEstimate(flops=500000000, bytes_accessed=5000000, transcendentals=0),
        out_shape=jax.ShapeDtypeStruct((rows, width), F32),
        in_specs=[vspec()] * 7,
        out_specs=vspec(),
        scratch_shapes=[pltpu.VMEM((rows, width), BF16)] * 3,
        compiler_params=whole(),
    )(tokens, gain_one, grads, w_query, w_key, w_value, grad_mixed)


def coordinates(index):
    context, expert = index // 8, index % 8
    return (context // 8 * 2 + expert % 2, expert // 2, context // 2 % 4, context % 2)


def device_at(x, y, z, core):
    return ((x // 2 * 4 + z) * 2 + core) * 8 + y * 2 + x % 2


def shifted(dim, by):
    pairs = []
    for index in range(128):
        place = list(coordinates(index))
        place[dim] = (place[dim] + by) % (2 if dim == 3 else 4)
        pairs.append((index, device_at(*place)))
    return pairs


AXES = ("context", "expert")


def direct_gather(block, dim):
    return jnp.stack([block] + [lax.ppermute(block, AXES, shifted(dim, -by)) for by in (1, 2, 3)])


def gather_last(filled, beside):
    half = filled.shape[0] // 2
    ahead = lax.ppermute(filled, AXES, shifted(1, -1))
    behind = lax.ppermute(filled, AXES, shifted(1, 1))
    ahead, behind, beside = lax.optimization_barrier((ahead, behind, beside))
    across = (
        lax.ppermute(ahead[:half], AXES, shifted(1, -1)),
        lax.ppermute(behind[half:], AXES, shifted(1, 1)),
    )
    mine = (filled, ahead, behind) + across
    other = tuple(lax.ppermute(part, AXES, shifted(3, 1)) for part in mine)
    return mine + other, beside


def unpack_kernel(
    buckets,
    place_ref,
    wq_ref,
    wk_ref,
    wv_ref,
    *rest,
):
    parts, (dwq_ref, dwk_ref, dwv_ref, dwo_ref, bias_ref, small_ref, router_ref, gain_grad_ref) = rest[:10], rest[10:18]
    all_s, sems = rest[18:]
    expert = pl.program_id(0)

    @pl.when(expert == 0)
    def _():
        copies = []
        for core in range(2):
            for i in range(5):
                part = parts[5 * core + i]
                half = all_s.shape[2] // 2
                place = (
                    all_s.at[core, (0, 1, 3)[i]]
                    if i < 3
                    else all_s.at[core, 2, pl.ds(half * (i - 3), half)]
                )
                copies.append(pltpu.make_async_copy(part, place, sems.at[5 * core + i]))
        for copy in copies:
            copy.start()
        for copy in copies:
            copy.wait()

    my_x, my_y, my_z, my_core = (place_ref[i] for i in range(4))
    each = dwq_ref.shape[0]
    half = each // 2
    width = dwq_ref.shape[1]
    rel_y = lax.rem(expert // 2 - my_y + 4, 4)

    def rel(context):
        x = context // 8 * 2 + lax.rem(expert, 2)
        return (
            jnp.where(my_core == context % 2, 0, 1),
            rel_y,
            lax.rem(x - my_x + 4, 4),
            lax.rem(context // 2 % 4 - my_z + 4, 4),
        )

    at = each + half
    bias = []
    for j in range(width // 128):
        cols = slice(128 * j, 128 * j + 128)
        one, two = all_s[rel(2 * j)], all_s[rel(2 * j + 1)]
        left = jnp.concatenate([one[:at, :64], two[:at, :64]], axis=1).astype(F32)
        right = jnp.concatenate([one[:at, 64:], two[:at, 64:]], axis=1).astype(F32)
        dwq_ref[:, cols] = left[:each]
        dwk_ref[:, cols] = right[:each]
        dwv_ref[:half, cols] = left[each:]
        dwv_ref[half:, cols] = right[each:]
        one, two = one[at:].astype(F32), two[at:].astype(F32)
        bias += [one[:1], two[:1]]
        for i, block in enumerate((one, two)):
            for k in range(width // 128):
                dwo_ref[2 * j + i, :, 128 * k : 128 * k + 128] = block[16 + 8 * k : 24 + 8 * k]
    bias_ref[...] = jnp.concatenate(bias, axis=0)[:, :buckets]
    block = all_s[rel(width // 64)].astype(F32)
    small = jnp.concatenate(
        [block[at + 16 + 8 * k : at + 24 + 8 * k] for k in range(width // 128)], axis=1
    )

    @pl.when(expert == 0)
    def _():
        router_ref[...] = small

    @pl.when(expert == 1)
    def _():
        small_ref[...] = small

    prod = (
        dwq_ref[...] * wq_ref[...].astype(F32)
        + dwk_ref[...] * wk_ref[...].astype(F32)
        + dwv_ref[...] * wv_ref[...].astype(F32)
    )
    lanes = prod[:, :128]
    for j in range(1, width // 128):
        lanes = lanes + prod[:, 128 * j : 128 * j + 128]
    gain_grad_ref[...] = jnp.broadcast_to(jnp.sum(lanes.T, axis=0, keepdims=True), (8, each))


def unpack(place, parts, w_query, w_key, w_value, heads, buckets, experts):
    width = w_query.shape[0]
    each = width // experts
    held = parts[0].shape[2]
    rows = pl.BlockSpec((each, width), lambda i: (i, 0))
    return pl.pallas_call(
        lambda *refs: unpack_kernel(buckets, *refs),
        name="unpack",
        cost_estimate=pl.CostEstimate(flops=1000000000, bytes_accessed=24000000, transcendentals=0),
        grid=(experts,),
        out_shape=(
            jax.ShapeDtypeStruct((width, width), F32),
            jax.ShapeDtypeStruct((width, width), F32),
            jax.ShapeDtypeStruct((width, width), F32),
            jax.ShapeDtypeStruct((heads, experts, 8, width), F32),
            jax.ShapeDtypeStruct((heads, buckets), F32),
            jax.ShapeDtypeStruct((8, width), F32),
            jax.ShapeDtypeStruct((8, width), F32),
            jax.ShapeDtypeStruct((experts, 8, each), F32),
        ),
        in_specs=[sspec(), rows, rows, rows] + [pl.BlockSpec(memory_space=pl.ANY)] * 10,
        out_specs=(
            rows,
            rows,
            rows,
            pl.BlockSpec((heads, None, 8, width), lambda i: (0, i, 0, 0)),
            pl.BlockSpec((heads, buckets), lambda i: (0, 0)),
            pl.BlockSpec((8, width), lambda i: (0, 0)),
            pl.BlockSpec((8, width), lambda i: (0, 0)),
            pl.BlockSpec((None, 8, each), lambda i: (i, 0, 0)),
        ),
        scratch_shapes=[
            pltpu.VMEM((2, 4, 4, 4, held, 128), BF16),
            pltpu.SemaphoreType.DMA((10,)),
        ],
        compiler_params=whole(),
    )(place, w_query, w_key, w_value, *parts)


def add_kernel(in_ref, out_ref):
    total = in_ref[0].astype(F32)
    for i in range(1, in_ref.shape[0]):
        total = total + in_ref[i].astype(F32)
    out_ref[...] = total.astype(BF16)


def add_up(received):
    return pl.pallas_call(
        add_kernel,
        name="add_up",
        out_shape=jax.ShapeDtypeStruct(received.shape[1:], BF16),
        in_specs=[vspec()],
        out_specs=vspec(),
        compiler_params=whole(),
    )(received)


def shards(
    tokens,
    gain_one,
    w_query,
    w_key,
    w_value,
    w_out,
    rel_table,
    gain_two,
    w_router,
    expert_in,
    expert_out,
    routes,
    cotangent,
):
    width = tokens.shape[2]
    heads, buckets = rel_table.shape
    experts = lax.axis_size("expert")
    inputs, grad_out, routes_here = tokens[0], cotangent[0], routes[0]
    context = lax.axis_index("context")
    head = jnp.minimum(context, heads - 1).astype(jnp.int32).reshape(1)

    own_weights = jnp.concatenate([expert_in[0].T, expert_out[0].T], axis=0)
    shared = lax.all_gather(own_weights, "context", axis=0, tiled=False)
    normed, packed = project(inputs, gain_one, w_query, w_key, w_value)
    qkv = lax.all_to_all(packed, "context", split_axis=0, concat_axis=0, tiled=True)
    expert = lax.axis_index("expert")
    place = jnp.stack(coordinates(context * experts + expert)).astype(jnp.int32)
    normed, qkv = lax.optimization_barrier((normed, qkv))
    normed_two = jnp.stack([normed, lax.ppermute(normed, AXES, shifted(0, 2))])

    out_heads, keep, lse = attend(head, rel_table, qkv)
    out_rows = lax.all_to_all(out_heads, "context", split_axis=0, concat_axis=0, tiled=True)
    send, attended, mixed, second, picks, gates = dispatch(
        inputs, grad_out, out_rows, w_out, gain_two, w_router, routes_here, experts
    )
    received = lax.all_to_all(send, "expert", split_axis=0, concat_axis=0, tiled=True)
    normed_two, received, shared = lax.optimization_barrier((normed_two, received, shared))
    normed_mine = direct_gather(normed_two, 2)
    back, weight_grads = expert_both(received, shared)
    returned = lax.all_to_all(back, "expert", split_axis=0, concat_axis=0, tiled=True)
    normed_mine, returned = lax.optimization_barrier((normed_mine, returned))
    normed_other = lax.ppermute(normed_mine, AXES, shifted(3, 1))
    own_grads = lax.psum_scatter(weight_grads, "context", scatter_dimension=0, tiled=False)
    block_out, grad_mixed, grad_heads, small = combine(
        grad_out, returned, picks, gates, mixed, second, routes_here, gain_two, w_router, w_out
    )
    keep_sums, pass_sums = out_grad(place, attended, grad_mixed, small)
    other_sums = lax.ppermute(pass_sums, AXES, shifted(3, 1))
    sums = (keep_sums.astype(F32) + other_sums.astype(F32)).astype(BF16)
    grad_here = lax.all_to_all(grad_heads, "context", split_axis=0, concat_axis=0, tiled=True)
    same_core = [[2 * i + core for i in range(8)] for core in range(2)]
    sums, grad_here = lax.optimization_barrier((sums, grad_here))
    sums = lax.all_to_all(
        sums, "context", split_axis=0, concat_axis=0, axis_index_groups=same_core, tiled=True
    )

    dqkv, bias = attend_back(head, rel_table, qkv, grad_here, keep, lse)
    terms = head_grads(place, dqkv, normed_mine, normed_other, bias, sums, experts)
    terms = lax.all_to_all(terms, "expert", split_axis=0, concat_axis=0, tiled=True)
    filled, dqkv = lax.optimization_barrier((direct_gather(direct_gather(add_up(terms), 2), 0), dqkv))
    grads = lax.all_to_all(dqkv, "context", split_axis=0, concat_axis=0, tiled=True)
    own_grads = own_grads.astype(F32)
    hidden = own_grads.shape[0] // 2
    parts, (grads, grad_in, grad_back) = gather_last(
        filled, (grads, own_grads[:hidden], own_grads[hidden:])
    )
    grad_tokens = input_grad(inputs, gain_one, grads, w_query, w_key, w_value, grad_mixed)

    dwq, dwk, dwv, dwo, bias, small, router, gain_grad = unpack(
        place, parts, w_query, w_key, w_value, heads, buckets, experts
    )
    return (
        block_out[None],
        grad_tokens[None],
        gain_grad[:, 0, :].reshape(width) / gain_one,
        dwq,
        dwk,
        dwv,
        dwo.reshape(width, width),
        bias,
        small[0],
        router.T,
        grad_in.T[None],
        grad_back.T[None],
    )


def solution(mesh):
    return jax.shard_map(
        shards,
        mesh=mesh,
        in_specs=(
            P("expert", "context", None),
            P(),
            P(),
            P(),
            P(),
            P(),
            P(),
            P(),
            P(),
            P("expert", None, "context"),
            P("expert", None, "context"),
            P("expert", "context", None),
            P("expert", "context", None),
        ),
        out_specs=(
            P("expert", "context", None),
            P("expert", "context", None),
            P(),
            P(),
            P(),
            P(),
            P(),
            P(),
            P(),
            P(),
            P("expert", None, "context"),
            P("expert", None, "context"),
        ),
        check_vma=False,
    )
```

```python
import math

import jax
import jax.numpy as jnp
from jax import lax
from jax.experimental import pallas as pl
from jax.experimental.pallas import tpu as pltpu
from jax.sharding import PartitionSpec as P

MAX_DIST = 128
EPSILON = 1e-06
NEG_LARGE = -1e30
BLK = 256
HEAD_SLOTS = 16

F32 = jnp.float32
BF16 = jnp.bfloat16
HIGHEST = lax.Precision.HIGHEST

NN = (((1,), (0,)), ((), ()))
NT = (((1,), (1,)), ((), ()))
TN = (((0,), (0,)), ((), ()))


def dot(a, b, dims=NN, precision=None):
    return lax.dot_general(a, b, dims, precision=precision, preferred_element_type=F32)


def bucket_starts(buckets, far_reach):
    span = buckets // 2
    rest = [
        int(math.ceil(span * (far_reach / span) ** (step / (buckets - span))))
        for step in range(1, buckets - span)
    ]
    return list(range(span + 1)) + rest


def rms_scale(values):
    return lax.rsqrt(jnp.mean(values * values, axis=-1, keepdims=True) + EPSILON)


def norm_back(values, inv_root, gain_vec, grad_normed):
    weighted = grad_normed * gain_vec
    cubed = inv_root * inv_root * inv_root
    return inv_root * weighted - values * cubed * jnp.mean(
        weighted * values, axis=-1, keepdims=True
    )


def whole(vmem_mib=56):
    return pltpu.CompilerParams(vmem_limit_bytes=vmem_mib * 2**20)


def vspec():
    return pl.BlockSpec(memory_space=pltpu.VMEM)


def sspec():
    return pl.BlockSpec(memory_space=pltpu.SMEM)


def project_kernel(tok_ref, gain_ref, wq_ref, wk_ref, wv_ref, normed_ref, out_ref):
    inputs = tok_ref[...].astype(F32)
    normed = (inputs * rms_scale(inputs) * gain_ref[...][None, :]).astype(BF16)
    rows, width = normed.shape
    half = rows // 2
    normed_ref[...] = normed
    queries = (dot(normed, wq_ref[...]).astype(BF16).astype(F32) * 0.125).astype(BF16)
    keys = dot(normed, wk_ref[...]).astype(BF16)
    values = dot(normed, wv_ref[...]).astype(BF16)
    heads = width // 64
    for h in range(heads):
        cols = slice(64 * h, 64 * h + 64)
        out_ref[h, :rows, :] = jnp.concatenate([queries[:, cols], keys[:, cols]], axis=1)
        out_ref[h, rows:, :] = jnp.concatenate([values[:half, cols], values[half:, cols]], axis=1)
    for h in range(heads, HEAD_SLOTS):
        out_ref[h] = jnp.zeros_like(out_ref[h])


def project(tokens, gain_one, w_query, w_key, w_value):
    rows, width = tokens.shape
    return pl.pallas_call(
        project_kernel,
        name="project",
        cost_estimate=pl.CostEstimate(flops=500000000, bytes_accessed=6000000, transcendentals=0),
        out_shape=(
            jax.ShapeDtypeStruct((rows, width), BF16),
            jax.ShapeDtypeStruct((HEAD_SLOTS, rows + rows // 2, 128), BF16),
        ),
        in_specs=[vspec()] * 5,
        out_specs=(vspec(), vspec()),
        compiler_params=whole(),
    )(tokens, gain_one, w_query, w_key, w_value)


def bias_tile(table_ref, head, buckets, rows_first, shape, key_dim):
    sign = [1, -1] if key_dim == 1 else [-1, 1]
    dist = (
        rows_first
        + sign[0] * lax.broadcasted_iota(jnp.int32, shape, 0)
        + sign[1] * lax.broadcasted_iota(jnp.int32, shape, 1)
    )
    far = table_ref[head, buckets - 1]
    tile = jnp.full(shape, NEG_LARGE, F32)
    for b, start in enumerate(bucket_starts(buckets, MAX_DIST)):
        tile = jnp.where(dist >= start, table_ref[head, b] - far, tile)
    return tile


def unpack_qkv(qkv_ref, q_s, k_s, v_s, ones_lane):
    count = qkv_ref.shape[0]
    lane = lax.broadcasted_iota(jnp.int32, (64, 64), 1)
    one = jnp.where(lane == 0, 1.0, 0.0).astype(BF16)
    for c in range(count):
        pair = qkv_ref[c, :128, :]
        q_s[128 * c : 128 * c + 128, :] = pair[:, :64]
        k_s[128 * c : 128 * c + 128, :] = pair[:, 64:]
        two = qkv_ref[c, 128:192, :]
        top, bottom = two[:, :64], two[:, 64:]
        if ones_lane:
            top = jnp.concatenate([top, one], axis=1)
            bottom = jnp.concatenate([bottom, one], axis=1)
        v_s[128 * c : 128 * c + 64, :] = top
        v_s[128 * c + 64 : 128 * c + 128, :] = bottom


def attend_kernel(buckets, head_ref, table_ref, qkv_ref, out_ref, keep_ref, lse_ref, q_s, k_s, v_s, bias_s):
    head = head_ref[0]
    unpack_qkv(qkv_ref, q_s, k_s, v_s, True)
    bias_s[0] = bias_tile(table_ref, head, buckets, BLK, (BLK, BLK), 1)
    bias_s[1] = bias_tile(table_ref, head, buckets, 0, (BLK, BLK), 1)
    blocks = q_s.shape[0] // BLK

    for qb in range(blocks):
        query = q_s[BLK * qb : BLK * qb + BLK, :]
        near = max(qb - 1, 0) * BLK
        parts = []
        if near:
            parts.append((0, dot(query, k_s[:near, :], NT)))
        if qb:
            parts.append((near, dot(query, k_s[near : near + BLK, :], NT) + bias_s[0]))
        parts.append((BLK * qb, dot(query, k_s[BLK * qb : BLK * qb + BLK, :], NT) + bias_s[1]))
        top = parts[-1][1]
        top = jnp.maximum(top[:, :128], top[:, 128:])
        for unused, scores in parts[:-1]:
            for j in range(scores.shape[1] // 128):
                top = jnp.maximum(top, scores[:, 128 * j : 128 * j + 128])
        top = jnp.max(top, axis=1, keepdims=True)
        total = jnp.zeros((BLK, 128), F32)
        for first, scores in parts:
            weights = jnp.exp(scores - top).astype(BF16)
            total = total + dot(weights, v_s[first : first + scores.shape[1], :])
        norm = total[:, 64:65]
        out = total[:, :64] / norm
        log_total = top + jnp.log(norm)
        spread = jnp.broadcast_to(log_total, (BLK, 128)).T
        lse_ref[qb] = spread[:8, :]
        for part in range(BLK // 128):
            two = jnp.concatenate(
                [out[128 * part : 128 * part + 64], out[128 * part + 64 : 128 * part + 128]], axis=1
            )
            place = qb * (BLK // 128) + part
            out_ref[place] = two.astype(BF16)
            keep_ref[place] = two


def attend(head, rel_table, qkv):
    count = qkv.shape[0]
    length = 128 * count
    blocks = length // BLK
    return pl.pallas_call(
        lambda *refs: attend_kernel(rel_table.shape[1], *refs),
        name="attend",
        cost_estimate=pl.CostEstimate(flops=7000000000, bytes_accessed=3000000, transcendentals=3000000),
        out_shape=(
            jax.ShapeDtypeStruct((count, 64, 128), BF16),
            jax.ShapeDtypeStruct((count, 64, 128), F32),
            jax.ShapeDtypeStruct((blocks, 8, BLK), F32),
        ),
        in_specs=[sspec(), sspec(), vspec()],
        out_specs=(vspec(), vspec(), vspec()),
        scratch_shapes=[
            pltpu.VMEM((length, 64), BF16),
            pltpu.VMEM((length, 64), BF16),
            pltpu.VMEM((length, 128), BF16),
            pltpu.VMEM((2, BLK, BLK), F32),
        ],
        compiler_params=whole(),
    )(head, rel_table, qkv)


def attend_back_kernel(
    buckets,
    head_ref,
    table_ref,
    qkv_ref,
    go_ref,
    keep_ref,
    lse_ref,
    dqkv_ref,
    bias_ref,
    q_s,
    k_s,
    v_s,
    kt_s,
    go_s,
    delta_s,
    dq_s,
    dk_s,
    dv_s,
    bias_s,
    acc_s,
):
    head = head_ref[0]
    length = q_s.shape[0]
    count = qkv_ref.shape[0]
    blocks = length // BLK
    unpack_qkv(qkv_ref, q_s, k_s, v_s, False)
    for c in range(count):
        kt_s[:, 128 * c : 128 * c + 128] = k_s[128 * c : 128 * c + 128, :].T
        two, kept = go_ref[c], keep_ref[c]
        go_s[128 * c : 128 * c + 64, :] = two[:, :64]
        go_s[128 * c + 64 : 128 * c + 128, :] = two[:, 64:]
        both = two.astype(F32) * kept
        turned = both.T
        delta = jnp.concatenate(
            [
                jnp.sum(turned[:64], axis=0, keepdims=True),
                jnp.sum(turned[64:], axis=0, keepdims=True),
            ],
            axis=1,
        )
        delta_s[:, 128 * c : 128 * c + 128] = jnp.broadcast_to(delta, (8, 128))
    bias_s[0] = bias_tile(table_ref, head, buckets, BLK, (BLK, BLK), 0)
    bias_s[1] = bias_tile(table_ref, head, buckets, 0, (BLK, BLK), 0)
    acc_s[...] = jnp.zeros_like(acc_s)
    dk_s[...] = jnp.zeros_like(dk_s)
    dv_s[...] = jnp.zeros_like(dv_s)

    far_sum = jnp.zeros((8, BLK), F32)
    for qb in range(blocks):
        rows = slice(BLK * qb, BLK * qb + BLK)
        query, grad = q_s[rows, :], go_s[rows, :]
        lse = lse_ref[qb][:1, :]
        delta = delta_s[:1, rows]
        grad_query = jnp.zeros((64, BLK), F32)
        for kb in range(qb + 1):
            cols = slice(BLK * kb, BLK * kb + BLK)
            near = kb - qb + 1
            scores = dot(k_s[cols, :], query, NT)
            if near >= 0:
                scores = scores + bias_s[near]
            probs = jnp.exp(scores - lse)
            grad_probs = dot(v_s[cols, :], grad, NT)
            grad_scores = (probs * (grad_probs - delta)).astype(BF16)
            dv_s[cols, :] += dot(probs.astype(BF16), grad)
            dk_s[cols, :] += dot(grad_scores, query)
            grad_query = grad_query + dot(kt_s[:, cols], grad_scores)
            wide = grad_scores.astype(F32)
            if near < 0:
                far_sum = far_sum + jnp.sum(wide.reshape(BLK // 8, 8, BLK), axis=0)
            else:
                acc_s[near] += wide
        dq_s[:, rows] = grad_query

    for c in range(count):
        here = slice(128 * c, 128 * c + 128)
        dq_t = (dq_s[:, here] * 0.125).astype(BF16)
        dk = dk_s[here, :].astype(BF16)
        dv = dv_s[here, :].astype(BF16)
        dqkv_ref[c, :128, :] = jnp.concatenate([dq_t.T, dk], axis=1)
        dqkv_ref[c, 128:192, :] = jnp.concatenate([dv[:64], dv[64:]], axis=1)

    lane = lax.broadcasted_iota(jnp.int32, (16, 128), 1)
    dist0 = (
        BLK
        - lax.broadcasted_iota(jnp.int32, (BLK, BLK), 0)
        + lax.broadcasted_iota(jnp.int32, (BLK, BLK), 1)
    )
    dist1 = dist0 - BLK

    def total(values):
        return jnp.sum(jnp.sum(values, axis=1, keepdims=True), axis=0, keepdims=True)

    starts = bucket_starts(buckets, MAX_DIST)
    row = jnp.zeros((16, 128), F32)
    above = None
    for b in reversed(range(buckets)):
        reach = total(
            jnp.where(dist0 >= starts[b], acc_s[0], 0.0)
            + jnp.where(dist1 >= starts[b], acc_s[1], 0.0)
        )
        mine = reach + total(far_sum) if b == buckets - 1 else reach - above
        above = reach
        row = jnp.where(lane == b, mine, row)
    bias_ref[...] = row


def attend_back(head, rel_table, qkv, grad_heads, keep, lse):
    count = qkv.shape[0]
    length = 128 * count
    return pl.pallas_call(
        lambda *refs: attend_back_kernel(rel_table.shape[1], *refs),
        name="attend_back",
        cost_estimate=pl.CostEstimate(flops=14000000000, bytes_accessed=4000000, transcendentals=3000000),
        out_shape=(
            jax.ShapeDtypeStruct(qkv.shape, BF16),
            jax.ShapeDtypeStruct((16, 128), F32),
        ),
        in_specs=[sspec(), sspec()] + [vspec()] * 4,
        out_specs=(vspec(), vspec()),
        scratch_shapes=[
            pltpu.VMEM((length, 64), BF16),
            pltpu.VMEM((length, 64), BF16),
            pltpu.VMEM((length, 64), BF16),
            pltpu.VMEM((64, length), BF16),
            pltpu.VMEM((length, 64), BF16),
            pltpu.VMEM((8, length), F32),
            pltpu.VMEM((64, length), F32),
            pltpu.VMEM((length, 64), F32),
            pltpu.VMEM((length, 64), F32),
            pltpu.VMEM((2, BLK, BLK), F32),
            pltpu.VMEM((2, BLK, BLK), F32),
        ],
        compiler_params=whole(),
    )(head, rel_table, qkv, grad_heads, keep, lse)


def head_grads_kernel(place_ref, dqkv_ref, mine_ref, other_ref, bias_ref, sums_ref, out_ref, turned_s):
    count = dqkv_ref.shape[0]
    width = mine_ref.shape[-1]
    held = mine_ref.shape[0] * mine_ref.shape[1]
    my_x, my_z, my_core = place_ref[0] // 2, place_ref[2], place_ref[3]
    for i in range(count):
        core, z, x = i // 8, i % 8 // 2, i % 2
        there = (lax.rem(my_x + x, 2) * 4 + lax.rem(my_z + z, 4)) * 2 + lax.rem(my_core + core, 2)
        turned_s[i] = dqkv_ref[there]
    pairs, third = 0.0, 0.0
    for core, normed_ref in enumerate((mine_ref, other_ref)):
        normed = normed_ref[...].reshape(held, 128, width)
        here = slice(held * core, held * core + held)
        two = turned_s[here, 128:192, :].reshape(held * 64, 128)
        for half in range(2):
            rows = slice(64 * half, 64 * half + 64)
            part = normed[:, rows, :].reshape(held * 64, width)
            pairs = pairs + dot(turned_s[here, rows, :].reshape(held * 64, 128), part, TN)
            third = third + dot(two, part, TN)[rows]
    pairs, third = pairs.T, third.T
    total = sums_ref[0].astype(F32)
    for c in range(1, sums_ref.shape[0]):
        total = total + sums_ref[c].astype(F32)
    shares = out_ref.shape[0]
    each = width // shares
    row = bias_ref[...].astype(BF16)
    for s in range(shares):
        mine = slice(each * s, each * s + each)
        out_ref[s, :each, :] = pairs[mine].astype(BF16)
        last = third[mine].astype(BF16)
        out_ref[s, each : each + each // 2, :] = jnp.concatenate(
            [last[: each // 2], last[each // 2 :]], axis=1
        )
        at = each + each // 2
        out_ref[s, at : at + 16, :] = row
        part = total[8 * s : 8 * s + 8]
        out_ref[s, at + 16 :, :] = jnp.concatenate(
            [part[:, 128 * j : 128 * j + 128] for j in range(width // 128)], axis=0
        ).astype(BF16)


def head_grads(place, dqkv, mine, other, bias, sums, shares):
    width = mine.shape[-1]
    each = width // shares
    held = each + each // 2 + 16 + width // 16
    return pl.pallas_call(
        head_grads_kernel,
        name="head_grads",
        cost_estimate=pl.CostEstimate(flops=3000000000, bytes_accessed=8000000, transcendentals=0),
        out_shape=jax.ShapeDtypeStruct((shares, held, 128), BF16),
        in_specs=[sspec()] + [vspec()] * 5,
        out_specs=vspec(),
        scratch_shapes=[pltpu.VMEM(dqkv.shape, BF16)],
        compiler_params=whole(),
    )(place, dqkv, mine, other, bias, sums)


def heads_to_rows(ref, scratch):
    for j in range(scratch.shape[1] // 128):
        one, two = ref[2 * j], ref[2 * j + 1]
        scratch[:64, 128 * j : 128 * j + 128] = jnp.concatenate([one[:, :64], two[:, :64]], axis=1)
        scratch[64:, 128 * j : 128 * j + 128] = jnp.concatenate([one[:, 64:], two[:, 64:]], axis=1)


def dispatch_kernel(
    experts,
    capacity,
    tok_ref,
    cot_ref,
    heads_ref,
    wo_ref,
    gain_ref,
    wr_ref,
    routes_ref,
    send_ref,
    att_ref,
    mixed_ref,
    second_ref,
    pick_ref,
    gates_ref,
):
    rows = tok_ref.shape[0]
    heads_to_rows(heads_ref, att_ref)
    mixed = tok_ref[...].astype(F32) + dot(att_ref[...], wo_ref[...])
    mixed_ref[...] = mixed
    second = (mixed * rms_scale(mixed) * gain_ref[...][None, :]).astype(BF16)
    second_ref[...] = second
    logits = dot(second, wr_ref[...])
    ids = lax.broadcasted_iota(jnp.int32, (rows, experts), 1)
    routes = routes_ref[...]
    marks = [(routes[:, k : k + 1] == ids).astype(F32) for k in range(2)]
    earlier = (
        lax.broadcasted_iota(jnp.int32, (rows, rows), 0)
        > lax.broadcasted_iota(jnp.int32, (rows, rows), 1)
    ).astype(F32)
    ranks = dot(earlier.astype(BF16), (marks[0] + marks[1]).astype(BF16))
    chosen = [jnp.sum(m * logits, axis=1, keepdims=True) for m in marks]
    top = jnp.maximum(chosen[0], chosen[1])
    exps = [jnp.exp(c - top) for c in chosen]
    gates = [e / (exps[0] + exps[1]) for e in exps]
    slot_ids = lax.broadcasted_iota(jnp.int32, (rows, experts * capacity), 1)
    grad_out = cot_ref[...].astype(F32)
    picks = []
    for k in range(2):
        slot = jnp.sum(marks[k] * ranks, axis=1, keepdims=True).astype(jnp.int32)
        place = routes[:, k : k + 1] * capacity + slot
        picks.append((place == slot_ids).astype(F32).astype(BF16))
        pick_ref[k] = picks[k]
    send_rows = dot(picks[0] + picks[1], second, TN).astype(BF16)
    send_grads = dot(picks[0], (gates[0] * grad_out).astype(BF16), TN) + dot(
        picks[1], (gates[1] * grad_out).astype(BF16), TN
    )
    send_grads = send_grads.astype(BF16)
    for e in range(experts):
        here = slice(capacity * e, capacity * e + capacity)
        send_ref[e, :capacity, :] = send_rows[here]
        send_ref[e, capacity:, :] = send_grads[here]
    lane = lax.broadcasted_iota(jnp.int32, (rows, 128), 1)
    gates_ref[...] = jnp.where(lane == 0, gates[0], gates[1])


def dispatch(tokens, cotangent, heads, w_out, gain_two, w_router, routes, experts):
    rows, width = tokens.shape
    capacity = 3 * rows // experts
    return pl.pallas_call(
        lambda *refs: dispatch_kernel(experts, capacity, *refs),
        name="dispatch",
        cost_estimate=pl.CostEstimate(flops=500000000, bytes_accessed=4000000, transcendentals=0),
        out_shape=(
            jax.ShapeDtypeStruct((experts, 2 * capacity, width), BF16),
            jax.ShapeDtypeStruct((rows, width), BF16),
            jax.ShapeDtypeStruct((rows, width), F32),
            jax.ShapeDtypeStruct((rows, width), BF16),
            jax.ShapeDtypeStruct((2, rows, experts * capacity), BF16),
            jax.ShapeDtypeStruct((rows, 128), F32),
        ),
        in_specs=[vspec()] * 7,
        out_specs=(vspec(),) * 6,
        compiler_params=whole(),
    )(tokens, cotangent, heads, w_out, gain_two, w_router, routes)


def expert_kernel(rows_ref, w_ref, back_ref, dw_ref, x_s, g_s, y_s, dx_s):
    step = pl.program_id(0)
    sources, both, width = rows_ref.shape
    capacity = both // 2

    @pl.when(step == 0)
    def _():
        for s in range(sources):
            x_s[capacity * s : capacity * s + capacity, :] = rows_ref[s, :capacity, :]
            g_s[capacity * s : capacity * s + capacity, :] = rows_ref[s, capacity:, :]
        y_s[...] = jnp.zeros_like(y_s)
        dx_s[...] = jnp.zeros_like(dx_s)

    each = w_ref.shape[1] // 2
    w_in = w_ref[:, :each, :].reshape(-1, width)
    w_back = w_ref[:, each:, :].reshape(-1, width)
    pre = dot(x_s[...], w_in, NT)
    square = pre * pre
    curve = jnp.tanh(0.7978845608 * (pre + 0.044715 * square * pre))
    act = (0.5 * pre * (1.0 + curve)).astype(BF16)
    slope = 0.5 * (1.0 + curve) + 0.5 * pre * (1.0 - curve * curve) * (
        0.7978845608 * (1.0 + 3.0 * 0.044715 * square)
    )
    grad_pre = (dot(g_s[...], w_back, NT) * slope).astype(BF16)
    y_s[...] += dot(act, w_back)
    dx_s[...] += dot(grad_pre, w_in)
    dw_ref[:, :each, :] = dot(grad_pre, x_s[...], TN).astype(BF16).reshape(-1, each, width)
    dw_ref[:, each:, :] = dot(act, g_s[...], TN).astype(BF16).reshape(-1, each, width)

    @pl.when(step == pl.num_programs(0) - 1)
    def _():
        for s in range(sources):
            here = slice(capacity * s, capacity * s + capacity)
            back_ref[s, :capacity, :] = y_s[here, :].astype(BF16)
            back_ref[s, capacity:, :] = dx_s[here, :].astype(BF16)


AT_ONCE = 4


def expert_both(rows, shared):
    sources, both, width = rows.shape
    count, given, unused = shared.shape
    held = sources * both // 2
    return pl.pallas_call(
        expert_kernel,
        name="expert_both",
        cost_estimate=pl.CostEstimate(flops=18000000000, bytes_accessed=22000000, transcendentals=5000000),
        grid=(count // AT_ONCE,),
        out_shape=(
            jax.ShapeDtypeStruct(rows.shape, BF16),
            jax.ShapeDtypeStruct(shared.shape, BF16),
        ),
        in_specs=[
            pl.BlockSpec(rows.shape, lambda i: (0, 0, 0)),
            pl.BlockSpec((AT_ONCE, given, width), lambda i: (i, 0, 0)),
        ],
        out_specs=(
            pl.BlockSpec(rows.shape, lambda i: (0, 0, 0)),
            pl.BlockSpec((AT_ONCE, given, width), lambda i: (i, 0, 0)),
        ),
        scratch_shapes=[
            pltpu.VMEM((held, width), BF16),
            pltpu.VMEM((held, width), BF16),
            pltpu.VMEM((held, width), F32),
            pltpu.VMEM((held, width), F32),
        ],
        compiler_params=whole(),
    )(rows, shared)


def combine_kernel(
    cot_ref,
    back_ref,
    pick_ref,
    gates_ref,
    mixed_ref,
    second_ref,
    routes_ref,
    gain_ref,
    wr_ref,
    wo_ref,
    out_ref,
    grad_mixed_ref,
    heads_ref,
    small_ref,
    y_s,
    dx_s,
):
    experts, both, width = back_ref.shape
    capacity = both // 2
    rows = cot_ref.shape[0]
    for s in range(experts):
        here = slice(capacity * s, capacity * s + capacity)
        y_s[here, :] = back_ref[s, :capacity, :]
        dx_s[here, :] = back_ref[s, capacity:, :]
    grad_out = cot_ref[...].astype(F32)
    mixed = mixed_ref[...]
    gates = [gates_ref[:, k : k + 1] for k in range(2)]
    picked = [dot(pick_ref[k], y_s[...]) for k in range(2)]
    out_ref[...] = (mixed + (gates[0] * picked[0] + gates[1] * picked[1])).astype(BF16)
    grad_gates = [jnp.sum(p * grad_out, axis=1, keepdims=True) for p in picked]
    mean = gates[0] * grad_gates[0] + gates[1] * grad_gates[1]
    grad_chosen = [gates[k] * (grad_gates[k] - mean) for k in range(2)]
    ids = lax.broadcasted_iota(jnp.int32, (rows, experts), 1)
    routes = routes_ref[...]
    grad_logits = jnp.where(routes[:, :1] == ids, grad_chosen[0], 0.0) + jnp.where(
        routes[:, 1:2] == ids, grad_chosen[1], 0.0
    )
    grad_second = dot(pick_ref[0], dx_s[...]) + dot(pick_ref[1], dx_s[...])
    grad_second = grad_second + dot(grad_logits, wr_ref[...].astype(F32), NT, HIGHEST)
    second = second_ref[...]
    grad_router = dot(grad_logits, second.astype(F32), TN, HIGHEST)
    scale = rms_scale(mixed)
    grad_gain = jnp.sum(grad_second * mixed * scale, axis=0, keepdims=True)
    grad_mixed = grad_out + norm_back(mixed, scale, gain_ref[...][None, :], grad_second)
    grad_mixed_ref[...] = grad_mixed
    grad_branch = grad_mixed.astype(BF16)
    grad_att = dot(grad_branch, wo_ref[...], NT).astype(BF16)
    heads = width // 64
    for h in range(heads):
        cols = slice(64 * h, 64 * h + 64)
        heads_ref[h] = jnp.concatenate([grad_att[:64, cols], grad_att[64:, cols]], axis=1)
    for h in range(heads, HEAD_SLOTS):
        heads_ref[h] = jnp.zeros_like(heads_ref[h])
    small_ref[...] = jnp.concatenate([grad_router, jnp.broadcast_to(grad_gain, (8, width))], axis=0)


def out_grad_kernel(place_ref, att_ref, grad_mixed_ref, small_ref, keep_ref, pass_ref, all_s):
    grad_wo = dot(att_ref[...], grad_mixed_ref[...].astype(BF16), TN).astype(BF16)
    slots, each, width = all_s.shape
    used = width // each
    for c in range(used):
        all_s[c] = grad_wo[each * c : each * c + each]
    for c in range(used, slots):
        all_s[c] = jnp.zeros_like(all_s[c])
    all_s[used, :16, :] = small_ref[...].astype(BF16)
    core = place_ref[3]
    for c in range(slots // 2):
        keep_ref[c] = all_s[2 * c + core]
        pass_ref[c] = all_s[2 * c + 1 - core]


def out_grad(place, attended, grad_mixed, small):
    width = attended.shape[1]
    return pl.pallas_call(
        out_grad_kernel,
        name="out_grad",
        cost_estimate=pl.CostEstimate(flops=500000000, bytes_accessed=4000000, transcendentals=0),
        out_shape=(jax.ShapeDtypeStruct((HEAD_SLOTS // 2, 64, width), BF16),) * 2,
        in_specs=[sspec()] + [vspec()] * 3,
        out_specs=(vspec(),) * 2,
        scratch_shapes=[pltpu.VMEM((HEAD_SLOTS, 64, width), BF16)],
        compiler_params=whole(),
    )(place, attended, grad_mixed, small)


def combine(cotangent, back, picks, gates, mixed, second, routes, gain_two, w_router, w_out):
    rows, width = cotangent.shape
    experts, both, unused = back.shape
    held = experts * both // 2
    return pl.pallas_call(
        combine_kernel,
        name="combine",
        cost_estimate=pl.CostEstimate(flops=1000000000, bytes_accessed=5000000, transcendentals=0),
        out_shape=(
            jax.ShapeDtypeStruct((rows, width), BF16),
            jax.ShapeDtypeStruct((rows, width), F32),
            jax.ShapeDtypeStruct((HEAD_SLOTS, rows // 2, 128), BF16),
            jax.ShapeDtypeStruct((16, width), F32),
        ),
        in_specs=[vspec()] * 10,
        out_specs=(vspec(),) * 4,
        scratch_shapes=[pltpu.VMEM((held, width), BF16), pltpu.VMEM((held, width), BF16)],
        compiler_params=whole(),
    )(
        cotangent,
        back,
        picks,
        gates,
        mixed,
        second,
        routes,
        gain_two,
        w_router,
        w_out,
    )


def input_grad_kernel(tok_ref, gain_ref, grads_ref, wq_ref, wk_ref, wv_ref, mixed_ref, out_ref, dq_s, dk_s, dv_s):
    for j in range(dq_s.shape[1] // 128):
        cols = slice(128 * j, 128 * j + 128)
        one, two = grads_ref[2 * j], grads_ref[2 * j + 1]
        dq_s[:, cols] = jnp.concatenate([one[:128, :64], two[:128, :64]], axis=1)
        dk_s[:, cols] = jnp.concatenate([one[:128, 64:], two[:128, 64:]], axis=1)
        dv_s[:64, cols] = jnp.concatenate([one[128:, :64], two[128:, :64]], axis=1)
        dv_s[64:, cols] = jnp.concatenate([one[128:, 64:], two[128:, 64:]], axis=1)
    grad_normed = dot(dq_s[...], wq_ref[...], NT)
    grad_normed = grad_normed + dot(dk_s[...], wk_ref[...], NT)
    grad_normed = grad_normed + dot(dv_s[...], wv_ref[...], NT)
    inputs = tok_ref[...].astype(F32)
    out_ref[...] = mixed_ref[...] + norm_back(inputs, rms_scale(inputs), gain_ref[...][None, :], grad_normed)


def input_grad(tokens, gain_one, grads, w_query, w_key, w_value, grad_mixed):
    rows, width = tokens.shape
    return pl.pallas_call(
        input_grad_kernel,
        name="input_grad",
        cost_estimate=pl.CostEstimate(flops=500000000, bytes_accessed=5000000, transcendentals=0),
        out_shape=jax.ShapeDtypeStruct((rows, width), F32),
        in_specs=[vspec()] * 7,
        out_specs=vspec(),
        scratch_shapes=[pltpu.VMEM((rows, width), BF16)] * 3,
        compiler_params=whole(),
    )(tokens, gain_one, grads, w_query, w_key, w_value, grad_mixed)


def coordinates(index):
    context, expert = index // 8, index % 8
    return (context // 8 * 2 + expert % 2, expert // 2, context // 2 % 4, context % 2)


def device_at(x, y, z, core):
    return ((x // 2 * 4 + z) * 2 + core) * 8 + y * 2 + x % 2


def shifted(dim, by):
    pairs = []
    for index in range(128):
        place = list(coordinates(index))
        place[dim] = (place[dim] + by) % (2 if dim == 3 else 4)
        pairs.append((index, device_at(*place)))
    return pairs


AXES = ("context", "expert")


def direct_gather(block, dim):
    return jnp.stack([block] + [lax.ppermute(block, AXES, shifted(dim, -by)) for by in (1, 2, 3)])


def around(block, dim):
    return lax.ppermute(block, AXES, shifted(dim, -1)), lax.ppermute(block, AXES, shifted(dim, 1))


def across(ahead, behind, dim):
    half = ahead.shape[0] // 2
    return (
        lax.ppermute(ahead[:half], AXES, shifted(dim, -1)),
        lax.ppermute(behind[half:], AXES, shifted(dim, 1)),
    )


def gather_first(piece, cut):
    both = jnp.concatenate([direct_gather(piece[:cut], 2), direct_gather(piece[cut:], 1)], axis=1)
    both = direct_gather(both, 0)
    return both[:, :, :cut], both[:, :, cut:]


def gather_last(first, second, beside):
    near_first, near_second = around(first, 1), around(second, 2)
    near_first, near_second, beside = lax.optimization_barrier((near_first, near_second, beside))
    mine = (first,) + near_first + across(*near_first, 1)
    mine = mine + (second,) + near_second + across(*near_second, 2)
    other = tuple(lax.ppermute(part, AXES, shifted(3, 1)) for part in mine)
    return mine + other, beside


def unpack_kernel(
    buckets,
    place_ref,
    wq_ref,
    wk_ref,
    wv_ref,
    *rest,
):
    parts, (dwq_ref, dwk_ref, dwv_ref, dwo_ref, bias_ref, small_ref, router_ref, gain_grad_ref) = rest[:20], rest[20:28]
    first_s, second_s, sems = rest[28:]
    expert = pl.program_id(0)

    @pl.when(expert == 0)
    def _():
        copies = []
        for core in range(2):
            for k, held in enumerate((first_s, second_s)):
                half = held.shape[2] // 2
                for i in range(5):
                    place = (
                        held.at[core, (0, 1, 3)[i]]
                        if i < 3
                        else held.at[core, 2, pl.ds(half * (i - 3), half)]
                    )
                    number = 10 * core + 5 * k + i
                    copies.append(pltpu.make_async_copy(parts[number], place, sems.at[number]))
        for copy in copies:
            copy.start()
        for copy in copies:
            copy.wait()

    my_x, my_y, my_z, my_core = (place_ref[i] for i in range(4))
    each = dwq_ref.shape[0]
    half = each // 2
    width = dwq_ref.shape[1]
    rel_y = lax.rem(expert // 2 - my_y + 4, 4)

    def block(context):
        core = jnp.where(my_core == context % 2, 0, 1)
        rel_x = lax.rem(context // 8 * 2 + lax.rem(expert, 2) - my_x + 4, 4)
        rel_z = lax.rem(context // 2 % 4 - my_z + 4, 4)
        return first_s[core, rel_y, rel_x, rel_z], second_s[core, rel_z, rel_x, rel_y]

    bias = []
    for j in range(width // 128):
        cols = slice(128 * j, 128 * j + 128)
        (one, one_more), (two, two_more) = block(2 * j), block(2 * j + 1)
        dwq_ref[:, cols] = jnp.concatenate([one[:, :64], two[:, :64]], axis=1).astype(F32)
        dwk_ref[:, cols] = jnp.concatenate([one[:, 64:], two[:, 64:]], axis=1).astype(F32)
        left = jnp.concatenate([one_more[:half, :64], two_more[:half, :64]], axis=1)
        right = jnp.concatenate([one_more[:half, 64:], two_more[:half, 64:]], axis=1)
        dwv_ref[:half, cols] = left.astype(F32)
        dwv_ref[half:, cols] = right.astype(F32)
        for i, more in enumerate((one_more, two_more)):
            more = more[half:].astype(F32)
            bias.append(more[:1])
            for k in range(width // 128):
                dwo_ref[2 * j + i, :, 128 * k : 128 * k + 128] = more[16 + 8 * k : 24 + 8 * k]
    bias_ref[...] = jnp.concatenate(bias, axis=0)[:, :buckets]
    more = block(width // 64)[1][half:].astype(F32)
    small = jnp.concatenate([more[16 + 8 * k : 24 + 8 * k] for k in range(width // 128)], axis=1)

    @pl.when(expert == 0)
    def _():
        router_ref[...] = small

    @pl.when(expert == 1)
    def _():
        small_ref[...] = small

    prod = (
        dwq_ref[...] * wq_ref[...].astype(F32)
        + dwk_ref[...] * wk_ref[...].astype(F32)
        + dwv_ref[...] * wv_ref[...].astype(F32)
    )
    lanes = prod[:, :128]
    for j in range(1, width // 128):
        lanes = lanes + prod[:, 128 * j : 128 * j + 128]
    gain_grad_ref[...] = jnp.broadcast_to(jnp.sum(lanes.T, axis=0, keepdims=True), (8, each))


def unpack(place, parts, w_query, w_key, w_value, heads, buckets, experts):
    width = w_query.shape[0]
    each = width // experts
    held = (parts[0].shape[2], parts[5].shape[2])
    rows = pl.BlockSpec((each, width), lambda i: (i, 0))
    return pl.pallas_call(
        lambda *refs: unpack_kernel(buckets, *refs),
        name="unpack",
        cost_estimate=pl.CostEstimate(flops=1000000000, bytes_accessed=24000000, transcendentals=0),
        grid=(experts,),
        out_shape=(
            jax.ShapeDtypeStruct((width, width), F32),
            jax.ShapeDtypeStruct((width, width), F32),
            jax.ShapeDtypeStruct((width, width), F32),
            jax.ShapeDtypeStruct((heads, experts, 8, width), F32),
            jax.ShapeDtypeStruct((heads, buckets), F32),
            jax.ShapeDtypeStruct((8, width), F32),
            jax.ShapeDtypeStruct((8, width), F32),
            jax.ShapeDtypeStruct((experts, 8, each), F32),
        ),
        in_specs=[sspec(), rows, rows, rows] + [pl.BlockSpec(memory_space=pl.ANY)] * 20,
        out_specs=(
            rows,
            rows,
            rows,
            pl.BlockSpec((heads, None, 8, width), lambda i: (0, i, 0, 0)),
            pl.BlockSpec((heads, buckets), lambda i: (0, 0)),
            pl.BlockSpec((8, width), lambda i: (0, 0)),
            pl.BlockSpec((8, width), lambda i: (0, 0)),
            pl.BlockSpec((None, 8, each), lambda i: (i, 0, 0)),
        ),
        scratch_shapes=[
            pltpu.VMEM((2, 4, 4, 4, held[0], 128), BF16),
            pltpu.VMEM((2, 4, 4, 4, held[1], 128), BF16),
            pltpu.SemaphoreType.DMA((20,)),
        ],
        compiler_params=whole(),
    )(place, w_query, w_key, w_value, *parts)


def add_kernel(in_ref, out_ref):
    total = in_ref[0].astype(F32)
    for i in range(1, in_ref.shape[0]):
        total = total + in_ref[i].astype(F32)
    out_ref[...] = total.astype(BF16)


def add_up(received):
    return pl.pallas_call(
        add_kernel,
        name="add_up",
        out_shape=jax.ShapeDtypeStruct(received.shape[1:], BF16),
        in_specs=[vspec()],
        out_specs=vspec(),
        compiler_params=whole(),
    )(received)


def shards(
    tokens,
    gain_one,
    w_query,
    w_key,
    w_value,
    w_out,
    rel_table,
    gain_two,
    w_router,
    expert_in,
    expert_out,
    routes,
    cotangent,
):
    width = tokens.shape[2]
    heads, buckets = rel_table.shape
    experts = lax.axis_size("expert")
    inputs, grad_out, routes_here = tokens[0], cotangent[0], routes[0]
    context = lax.axis_index("context")
    head = jnp.minimum(context, heads - 1).astype(jnp.int32).reshape(1)

    own_weights = jnp.concatenate([expert_in[0].T, expert_out[0].T], axis=0)
    shared = lax.all_gather(own_weights, "context", axis=0, tiled=False)
    normed, packed = project(inputs, gain_one, w_query, w_key, w_value)
    qkv = lax.all_to_all(packed, "context", split_axis=0, concat_axis=0, tiled=True)
    expert = lax.axis_index("expert")
    place = jnp.stack(coordinates(context * experts + expert)).astype(jnp.int32)
    normed, qkv = lax.optimization_barrier((normed, qkv))
    normed_two = jnp.stack([normed, lax.ppermute(normed, AXES, shifted(0, 2))])

    out_heads, keep, lse = attend(head, rel_table, qkv)
    out_rows = lax.all_to_all(out_heads, "context", split_axis=0, concat_axis=0, tiled=True)
    send, attended, mixed, second, picks, gates = dispatch(
        inputs, grad_out, out_rows, w_out, gain_two, w_router, routes_here, experts
    )
    received = lax.all_to_all(send, "expert", split_axis=0, concat_axis=0, tiled=True)
    normed_two, received, shared = lax.optimization_barrier((normed_two, received, shared))
    normed_mine = direct_gather(normed_two, 2)
    back, weight_grads = expert_both(received, shared)
    returned = lax.all_to_all(back, "expert", split_axis=0, concat_axis=0, tiled=True)
    normed_mine, returned = lax.optimization_barrier((normed_mine, returned))
    normed_other = lax.ppermute(normed_mine, AXES, shifted(3, 1))
    own_grads = lax.psum_scatter(weight_grads, "context", scatter_dimension=0, tiled=False)
    block_out, grad_mixed, grad_heads, small = combine(
        grad_out, returned, picks, gates, mixed, second, routes_here, gain_two, w_router, w_out
    )
    keep_sums, pass_sums = out_grad(place, attended, grad_mixed, small)
    other_sums = lax.ppermute(pass_sums, AXES, shifted(3, 1))
    sums = (keep_sums.astype(F32) + other_sums.astype(F32)).astype(BF16)
    grad_here = lax.all_to_all(grad_heads, "context", split_axis=0, concat_axis=0, tiled=True)
    same_core = [[2 * i + core for i in range(8)] for core in range(2)]
    sums, grad_here = lax.optimization_barrier((sums, grad_here))
    sums = lax.all_to_all(
        sums, "context", split_axis=0, concat_axis=0, axis_index_groups=same_core, tiled=True
    )

    dqkv, bias = attend_back(head, rel_table, qkv, grad_here, keep, lse)
    terms = head_grads(place, dqkv, normed_mine, normed_other, bias, sums, experts)
    terms = lax.all_to_all(terms, "expert", split_axis=0, concat_axis=0, tiled=True)
    first, second_part = gather_first(add_up(terms), inputs.shape[1] // experts)
    first, second_part, dqkv = lax.optimization_barrier((first, second_part, dqkv))
    grads = lax.all_to_all(dqkv, "context", split_axis=0, concat_axis=0, tiled=True)
    own_grads = own_grads.astype(F32)
    hidden = own_grads.shape[0] // 2
    parts, (grads, grad_in, grad_back) = gather_last(
        first, second_part, (grads, own_grads[:hidden], own_grads[hidden:])
    )
    grad_tokens = input_grad(inputs, gain_one, grads, w_query, w_key, w_value, grad_mixed)

    dwq, dwk, dwv, dwo, bias, small, router, gain_grad = unpack(
        place, parts, w_query, w_key, w_value, heads, buckets, experts
    )
    return (
        block_out[None],
        grad_tokens[None],
        gain_grad[:, 0, :].reshape(width) / gain_one,
        dwq,
        dwk,
        dwv,
        dwo.reshape(width, width),
        bias,
        small[0],
        router.T,
        grad_in.T[None],
        grad_back.T[None],
    )


def solution(mesh):
    return jax.shard_map(
        shards,
        mesh=mesh,
        in_specs=(
            P("expert", "context", None),
            P(),
            P(),
            P(),
            P(),
            P(),
            P(),
            P(),
            P(),
            P("expert", None, "context"),
            P("expert", None, "context"),
            P("expert", "context", None),
            P("expert", "context", None),
        ),
        out_specs=(
            P("expert", "context", None),
            P("expert", "context", None),
            P(),
            P(),
            P(),
            P(),
            P(),
            P(),
            P(),
            P(),
            P("expert", None, "context"),
            P("expert", None, "context"),
        ),
        check_vma=False,
    )
```

```python
import math

import jax
import jax.numpy as jnp
from jax import lax
from jax.experimental import pallas as pl
from jax.experimental.pallas import tpu as pltpu
from jax.sharding import PartitionSpec as P

MAX_DIST = 128
EPSILON = 1e-06
NEG_LARGE = -1e30
BLK = 256
HEAD_SLOTS = 16

F32 = jnp.float32
BF16 = jnp.bfloat16
HIGHEST = lax.Precision.HIGHEST

NN = (((1,), (0,)), ((), ()))
NT = (((1,), (1,)), ((), ()))
TN = (((0,), (0,)), ((), ()))


def dot(a, b, dims=NN, precision=None):
    return lax.dot_general(a, b, dims, precision=precision, preferred_element_type=F32)


def bucket_starts(buckets, far_reach):
    span = buckets // 2
    rest = [
        int(math.ceil(span * (far_reach / span) ** (step / (buckets - span))))
        for step in range(1, buckets - span)
    ]
    return list(range(span + 1)) + rest


def rms_scale(values):
    return lax.rsqrt(jnp.mean(values * values, axis=-1, keepdims=True) + EPSILON)


def norm_back(values, inv_root, gain_vec, grad_normed):
    weighted = grad_normed * gain_vec
    cubed = inv_root * inv_root * inv_root
    return inv_root * weighted - values * cubed * jnp.mean(
        weighted * values, axis=-1, keepdims=True
    )


def whole(vmem_mib=56):
    return pltpu.CompilerParams(vmem_limit_bytes=vmem_mib * 2**20)


def vspec():
    return pl.BlockSpec(memory_space=pltpu.VMEM)


def sspec():
    return pl.BlockSpec(memory_space=pltpu.SMEM)


def project_kernel(tok_ref, gain_ref, wq_ref, wk_ref, wv_ref, normed_ref, out_ref):
    inputs = tok_ref[...].astype(F32)
    normed = (inputs * rms_scale(inputs) * gain_ref[...][None, :]).astype(BF16)
    rows, width = normed.shape
    half = rows // 2
    normed_ref[...] = normed
    queries = (dot(normed, wq_ref[...]).astype(BF16).astype(F32) * 0.125).astype(BF16)
    keys = dot(normed, wk_ref[...]).astype(BF16)
    values = dot(normed, wv_ref[...]).astype(BF16)
    heads = width // 64
    for h in range(heads):
        cols = slice(64 * h, 64 * h + 64)
        out_ref[h, :rows, :] = jnp.concatenate([queries[:, cols], keys[:, cols]], axis=1)
        out_ref[h, rows:, :] = jnp.concatenate([values[:half, cols], values[half:, cols]], axis=1)
    for h in range(heads, HEAD_SLOTS):
        out_ref[h] = jnp.zeros_like(out_ref[h])


def project(tokens, gain_one, w_query, w_key, w_value):
    rows, width = tokens.shape
    return pl.pallas_call(
        project_kernel,
        name="project",
        cost_estimate=pl.CostEstimate(flops=500000000, bytes_accessed=6000000, transcendentals=0),
        out_shape=(
            jax.ShapeDtypeStruct((rows, width), BF16),
            jax.ShapeDtypeStruct((HEAD_SLOTS, rows + rows // 2, 128), BF16),
        ),
        in_specs=[vspec()] * 5,
        out_specs=(vspec(), vspec()),
        compiler_params=whole(),
    )(tokens, gain_one, w_query, w_key, w_value)


def bias_tile(table_ref, head, buckets, rows_first, shape, key_dim):
    sign = [1, -1] if key_dim == 1 else [-1, 1]
    dist = (
        rows_first
        + sign[0] * lax.broadcasted_iota(jnp.int32, shape, 0)
        + sign[1] * lax.broadcasted_iota(jnp.int32, shape, 1)
    )
    far = table_ref[head, buckets - 1]
    tile = jnp.full(shape, NEG_LARGE, F32)
    for b, start in enumerate(bucket_starts(buckets, MAX_DIST)):
        tile = jnp.where(dist >= start, table_ref[head, b] - far, tile)
    return tile


def unpack_qkv(qkv_ref, q_s, k_s, v_s, ones_lane):
    count = qkv_ref.shape[0]
    lane = lax.broadcasted_iota(jnp.int32, (64, 64), 1)
    one = jnp.where(lane == 0, 1.0, 0.0).astype(BF16)
    for c in range(count):
        pair = qkv_ref[c, :128, :]
        q_s[128 * c : 128 * c + 128, :] = pair[:, :64]
        k_s[128 * c : 128 * c + 128, :] = pair[:, 64:]
        two = qkv_ref[c, 128:192, :]
        top, bottom = two[:, :64], two[:, 64:]
        if ones_lane:
            top = jnp.concatenate([top, one], axis=1)
            bottom = jnp.concatenate([bottom, one], axis=1)
        v_s[128 * c : 128 * c + 64, :] = top
        v_s[128 * c + 64 : 128 * c + 128, :] = bottom


def attend_kernel(buckets, head_ref, table_ref, qkv_ref, out_ref, keep_ref, lse_ref, q_s, k_s, v_s, bias_s):
    head = head_ref[0]
    unpack_qkv(qkv_ref, q_s, k_s, v_s, True)
    bias_s[0] = bias_tile(table_ref, head, buckets, BLK, (BLK, BLK), 1)
    bias_s[1] = bias_tile(table_ref, head, buckets, 0, (BLK, BLK), 1)
    blocks = q_s.shape[0] // BLK

    for qb in range(blocks):
        query = q_s[BLK * qb : BLK * qb + BLK, :]
        near = max(qb - 1, 0) * BLK
        parts = []
        if near:
            parts.append((0, dot(query, k_s[:near, :], NT)))
        if qb:
            parts.append((near, dot(query, k_s[near : near + BLK, :], NT) + bias_s[0]))
        parts.append((BLK * qb, dot(query, k_s[BLK * qb : BLK * qb + BLK, :], NT) + bias_s[1]))
        top = parts[-1][1]
        top = jnp.maximum(top[:, :128], top[:, 128:])
        for unused, scores in parts[:-1]:
            for j in range(scores.shape[1] // 128):
                top = jnp.maximum(top, scores[:, 128 * j : 128 * j + 128])
        top = jnp.max(top, axis=1, keepdims=True)
        total = jnp.zeros((BLK, 128), F32)
        for first, scores in parts:
            weights = jnp.exp(scores - top).astype(BF16)
            total = total + dot(weights, v_s[first : first + scores.shape[1], :])
        norm = total[:, 64:65]
        out = total[:, :64] / norm
        log_total = top + jnp.log(norm)
        spread = jnp.broadcast_to(log_total, (BLK, 128)).T
        lse_ref[qb] = spread[:8, :]
        for part in range(BLK // 128):
            two = jnp.concatenate(
                [out[128 * part : 128 * part + 64], out[128 * part + 64 : 128 * part + 128]], axis=1
            )
            place = qb * (BLK // 128) + part
            out_ref[place] = two.astype(BF16)
            keep_ref[place] = two


def attend(head, rel_table, qkv):
    count = qkv.shape[0]
    length = 128 * count
    blocks = length // BLK
    return pl.pallas_call(
        lambda *refs: attend_kernel(rel_table.shape[1], *refs),
        name="attend",
        cost_estimate=pl.CostEstimate(flops=7000000000, bytes_accessed=3000000, transcendentals=3000000),
        out_shape=(
            jax.ShapeDtypeStruct((count, 64, 128), BF16),
            jax.ShapeDtypeStruct((count, 64, 128), F32),
            jax.ShapeDtypeStruct((blocks, 8, BLK), F32),
        ),
        in_specs=[sspec(), sspec(), vspec()],
        out_specs=(vspec(), vspec(), vspec()),
        scratch_shapes=[
            pltpu.VMEM((length, 64), BF16),
            pltpu.VMEM((length, 64), BF16),
            pltpu.VMEM((length, 128), BF16),
            pltpu.VMEM((2, BLK, BLK), F32),
        ],
        compiler_params=whole(),
    )(head, rel_table, qkv)


def attend_back_kernel(
    buckets,
    head_ref,
    table_ref,
    qkv_ref,
    go_ref,
    keep_ref,
    lse_ref,
    dqkv_ref,
    bias_ref,
    q_s,
    k_s,
    v_s,
    kt_s,
    go_s,
    delta_s,
    dq_s,
    dk_s,
    dv_s,
    bias_s,
    acc_s,
):
    head = head_ref[0]
    length = q_s.shape[0]
    count = qkv_ref.shape[0]
    blocks = length // BLK
    unpack_qkv(qkv_ref, q_s, k_s, v_s, False)
    for c in range(count):
        kt_s[:, 128 * c : 128 * c + 128] = k_s[128 * c : 128 * c + 128, :].T
        two, kept = go_ref[c], keep_ref[c]
        go_s[128 * c : 128 * c + 64, :] = two[:, :64]
        go_s[128 * c + 64 : 128 * c + 128, :] = two[:, 64:]
        both = two.astype(F32) * kept
        turned = both.T
        delta = jnp.concatenate(
            [
                jnp.sum(turned[:64], axis=0, keepdims=True),
                jnp.sum(turned[64:], axis=0, keepdims=True),
            ],
            axis=1,
        )
        delta_s[:, 128 * c : 128 * c + 128] = jnp.broadcast_to(delta, (8, 128))
    bias_s[0] = bias_tile(table_ref, head, buckets, BLK, (BLK, BLK), 0)
    bias_s[1] = bias_tile(table_ref, head, buckets, 0, (BLK, BLK), 0)
    acc_s[...] = jnp.zeros_like(acc_s)
    dk_s[...] = jnp.zeros_like(dk_s)
    dv_s[...] = jnp.zeros_like(dv_s)

    far_sum = jnp.zeros((8, BLK), F32)
    for qb in range(blocks):
        rows = slice(BLK * qb, BLK * qb + BLK)
        query, grad = q_s[rows, :], go_s[rows, :]
        lse = lse_ref[qb][:1, :]
        delta = delta_s[:1, rows]
        grad_query = jnp.zeros((64, BLK), F32)
        for kb in range(qb + 1):
            cols = slice(BLK * kb, BLK * kb + BLK)
            near = kb - qb + 1
            scores = dot(k_s[cols, :], query, NT)
            if near >= 0:
                scores = scores + bias_s[near]
            probs = jnp.exp(scores - lse)
            grad_probs = dot(v_s[cols, :], grad, NT)
            grad_scores = (probs * (grad_probs - delta)).astype(BF16)
            dv_s[cols, :] += dot(probs.astype(BF16), grad)
            dk_s[cols, :] += dot(grad_scores, query)
            grad_query = grad_query + dot(kt_s[:, cols], grad_scores)
            wide = grad_scores.astype(F32)
            if near < 0:
                far_sum = far_sum + jnp.sum(wide.reshape(BLK // 8, 8, BLK), axis=0)
            else:
                acc_s[near] += wide
        dq_s[:, rows] = grad_query

    for c in range(count):
        here = slice(128 * c, 128 * c + 128)
        dq_t = (dq_s[:, here] * 0.125).astype(BF16)
        dk = dk_s[here, :].astype(BF16)
        dv = dv_s[here, :].astype(BF16)
        dqkv_ref[c, :128, :] = jnp.concatenate([dq_t.T, dk], axis=1)
        dqkv_ref[c, 128:192, :] = jnp.concatenate([dv[:64], dv[64:]], axis=1)

    lane = lax.broadcasted_iota(jnp.int32, (16, 128), 1)
    dist0 = (
        BLK
        - lax.broadcasted_iota(jnp.int32, (BLK, BLK), 0)
        + lax.broadcasted_iota(jnp.int32, (BLK, BLK), 1)
    )
    dist1 = dist0 - BLK

    def total(values):
        return jnp.sum(jnp.sum(values, axis=1, keepdims=True), axis=0, keepdims=True)

    starts = bucket_starts(buckets, MAX_DIST)
    row = jnp.zeros((16, 128), F32)
    above = None
    for b in reversed(range(buckets)):
        reach = total(
            jnp.where(dist0 >= starts[b], acc_s[0], 0.0)
            + jnp.where(dist1 >= starts[b], acc_s[1], 0.0)
        )
        mine = reach + total(far_sum) if b == buckets - 1 else reach - above
        above = reach
        row = jnp.where(lane == b, mine, row)
    bias_ref[...] = row


def attend_back(head, rel_table, qkv, grad_heads, keep, lse):
    count = qkv.shape[0]
    length = 128 * count
    return pl.pallas_call(
        lambda *refs: attend_back_kernel(rel_table.shape[1], *refs),
        name="attend_back",
        cost_estimate=pl.CostEstimate(flops=14000000000, bytes_accessed=4000000, transcendentals=3000000),
        out_shape=(
            jax.ShapeDtypeStruct(qkv.shape, BF16),
            jax.ShapeDtypeStruct((16, 128), F32),
        ),
        in_specs=[sspec(), sspec()] + [vspec()] * 4,
        out_specs=(vspec(), vspec()),
        scratch_shapes=[
            pltpu.VMEM((length, 64), BF16),
            pltpu.VMEM((length, 64), BF16),
            pltpu.VMEM((length, 64), BF16),
            pltpu.VMEM((64, length), BF16),
            pltpu.VMEM((length, 64), BF16),
            pltpu.VMEM((8, length), F32),
            pltpu.VMEM((64, length), F32),
            pltpu.VMEM((length, 64), F32),
            pltpu.VMEM((length, 64), F32),
            pltpu.VMEM((2, BLK, BLK), F32),
            pltpu.VMEM((2, BLK, BLK), F32),
        ],
        compiler_params=whole(),
    )(head, rel_table, qkv, grad_heads, keep, lse)


def head_grads_kernel(place_ref, dqkv_ref, mine_ref, other_ref, bias_ref, sums_ref, out_ref, turned_s):
    count = dqkv_ref.shape[0]
    width = mine_ref.shape[-1]
    held = mine_ref.shape[0] * mine_ref.shape[1]
    my_x, my_z, my_core = place_ref[0] // 2, place_ref[2], place_ref[3]
    for i in range(count):
        core, z, x = i // 8, i % 8 // 2, i % 2
        there = (lax.rem(my_x + x, 2) * 4 + lax.rem(my_z + z, 4)) * 2 + lax.rem(my_core + core, 2)
        turned_s[i] = dqkv_ref[there]
    pairs, third = 0.0, 0.0
    for core, normed_ref in enumerate((mine_ref, other_ref)):
        normed = normed_ref[...].reshape(held, 128, width)
        here = slice(held * core, held * core + held)
        two = turned_s[here, 128:192, :].reshape(held * 64, 128)
        for half in range(2):
            rows = slice(64 * half, 64 * half + 64)
            part = normed[:, rows, :].reshape(held * 64, width)
            pairs = pairs + dot(turned_s[here, rows, :].reshape(held * 64, 128), part, TN)
            third = third + dot(two, part, TN)[rows]
    pairs, third = pairs.T, third.T
    total = sums_ref[0].astype(F32)
    for c in range(1, sums_ref.shape[0]):
        total = total + sums_ref[c].astype(F32)
    shares = out_ref.shape[0]
    each = width // shares
    row = bias_ref[...].astype(BF16)
    for s in range(shares):
        mine = slice(each * s, each * s + each)
        out_ref[s, :each, :] = pairs[mine].astype(BF16)
        last = third[mine].astype(BF16)
        out_ref[s, each : each + each // 2, :] = jnp.concatenate(
            [last[: each // 2], last[each // 2 :]], axis=1
        )
        at = each + each // 2
        out_ref[s, at : at + 16, :] = row
        part = total[8 * s : 8 * s + 8]
        out_ref[s, at + 16 :, :] = jnp.concatenate(
            [part[:, 128 * j : 128 * j + 128] for j in range(width // 128)], axis=0
        ).astype(BF16)


def head_grads(place, dqkv, mine, other, bias, sums, shares):
    width = mine.shape[-1]
    each = width // shares
    held = each + each // 2 + 16 + width // 16
    return pl.pallas_call(
        head_grads_kernel,
        name="head_grads",
        cost_estimate=pl.CostEstimate(flops=3000000000, bytes_accessed=8000000, transcendentals=0),
        out_shape=jax.ShapeDtypeStruct((shares, held, 128), BF16),
        in_specs=[sspec()] + [vspec()] * 5,
        out_specs=vspec(),
        scratch_shapes=[pltpu.VMEM(dqkv.shape, BF16)],
        compiler_params=whole(),
    )(place, dqkv, mine, other, bias, sums)


def heads_to_rows(ref, scratch):
    for j in range(scratch.shape[1] // 128):
        one, two = ref[2 * j], ref[2 * j + 1]
        scratch[:64, 128 * j : 128 * j + 128] = jnp.concatenate([one[:, :64], two[:, :64]], axis=1)
        scratch[64:, 128 * j : 128 * j + 128] = jnp.concatenate([one[:, 64:], two[:, 64:]], axis=1)


def dispatch_kernel(
    experts,
    capacity,
    tok_ref,
    cot_ref,
    heads_ref,
    wo_ref,
    gain_ref,
    wr_ref,
    routes_ref,
    send_ref,
    att_ref,
    mixed_ref,
    second_ref,
    pick_ref,
    gates_ref,
):
    rows = tok_ref.shape[0]
    heads_to_rows(heads_ref, att_ref)
    mixed = tok_ref[...].astype(F32) + dot(att_ref[...], wo_ref[...])
    mixed_ref[...] = mixed
    second = (mixed * rms_scale(mixed) * gain_ref[...][None, :]).astype(BF16)
    second_ref[...] = second
    logits = dot(second, wr_ref[...])
    ids = lax.broadcasted_iota(jnp.int32, (rows, experts), 1)
    routes = routes_ref[...]
    marks = [(routes[:, k : k + 1] == ids).astype(F32) for k in range(2)]
    earlier = (
        lax.broadcasted_iota(jnp.int32, (rows, rows), 0)
        > lax.broadcasted_iota(jnp.int32, (rows, rows), 1)
    ).astype(F32)
    ranks = dot(earlier.astype(BF16), (marks[0] + marks[1]).astype(BF16))
    chosen = [jnp.sum(m * logits, axis=1, keepdims=True) for m in marks]
    top = jnp.maximum(chosen[0], chosen[1])
    exps = [jnp.exp(c - top) for c in chosen]
    gates = [e / (exps[0] + exps[1]) for e in exps]
    slot_ids = lax.broadcasted_iota(jnp.int32, (rows, experts * capacity), 1)
    grad_out = cot_ref[...].astype(F32)
    picks = []
    for k in range(2):
        slot = jnp.sum(marks[k] * ranks, axis=1, keepdims=True).astype(jnp.int32)
        place = routes[:, k : k + 1] * capacity + slot
        picks.append((place == slot_ids).astype(F32).astype(BF16))
        pick_ref[k] = picks[k]
    send_rows = dot(picks[0] + picks[1], second, TN).astype(BF16)
    send_grads = dot(picks[0], (gates[0] * grad_out).astype(BF16), TN) + dot(
        picks[1], (gates[1] * grad_out).astype(BF16), TN
    )
    send_grads = send_grads.astype(BF16)
    for e in range(experts):
        here = slice(capacity * e, capacity * e + capacity)
        send_ref[e, :capacity, :] = send_rows[here]
        send_ref[e, capacity:, :] = send_grads[here]
    lane = lax.broadcasted_iota(jnp.int32, (rows, 128), 1)
    gates_ref[...] = jnp.where(lane == 0, gates[0], gates[1])


def dispatch(tokens, cotangent, heads, w_out, gain_two, w_router, routes, experts):
    rows, width = tokens.shape
    capacity = 3 * rows // experts
    return pl.pallas_call(
        lambda *refs: dispatch_kernel(experts, capacity, *refs),
        name="dispatch",
        cost_estimate=pl.CostEstimate(flops=500000000, bytes_accessed=4000000, transcendentals=0),
        out_shape=(
            jax.ShapeDtypeStruct((experts, 2 * capacity, width), BF16),
            jax.ShapeDtypeStruct((rows, width), BF16),
            jax.ShapeDtypeStruct((rows, width), F32),
            jax.ShapeDtypeStruct((rows, width), BF16),
            jax.ShapeDtypeStruct((2, rows, experts * capacity), BF16),
            jax.ShapeDtypeStruct((rows, 128), F32),
        ),
        in_specs=[vspec()] * 7,
        out_specs=(vspec(),) * 6,
        compiler_params=whole(),
    )(tokens, cotangent, heads, w_out, gain_two, w_router, routes)


def expert_kernel(rows_ref, w_ref, back_ref, dw_ref, x_s, g_s, y_s, dx_s):
    step = pl.program_id(0)
    sources, both, width = rows_ref.shape
    capacity = both // 2

    @pl.when(step == 0)
    def _():
        for s in range(sources):
            x_s[capacity * s : capacity * s + capacity, :] = rows_ref[s, :capacity, :]
            g_s[capacity * s : capacity * s + capacity, :] = rows_ref[s, capacity:, :]
        y_s[...] = jnp.zeros_like(y_s)
        dx_s[...] = jnp.zeros_like(dx_s)

    each = w_ref.shape[1] // 2
    w_in = w_ref[:, :each, :].reshape(-1, width)
    w_back = w_ref[:, each:, :].reshape(-1, width)
    pre = dot(x_s[...], w_in, NT)
    square = pre * pre
    curve = jnp.tanh(0.7978845608 * (pre + 0.044715 * square * pre))
    act = (0.5 * pre * (1.0 + curve)).astype(BF16)
    slope = 0.5 * (1.0 + curve) + 0.5 * pre * (1.0 - curve * curve) * (
        0.7978845608 * (1.0 + 3.0 * 0.044715 * square)
    )
    grad_pre = (dot(g_s[...], w_back, NT) * slope).astype(BF16)
    y_s[...] += dot(act, w_back)
    dx_s[...] += dot(grad_pre, w_in)
    dw_ref[:, :each, :] = dot(grad_pre, x_s[...], TN).astype(BF16).reshape(-1, each, width)
    dw_ref[:, each:, :] = dot(act, g_s[...], TN).astype(BF16).reshape(-1, each, width)

    @pl.when(step == pl.num_programs(0) - 1)
    def _():
        for s in range(sources):
            here = slice(capacity * s, capacity * s + capacity)
            back_ref[s, :capacity, :] = y_s[here, :].astype(BF16)
            back_ref[s, capacity:, :] = dx_s[here, :].astype(BF16)


AT_ONCE = 4


def expert_both(rows, shared):
    sources, both, width = rows.shape
    count, given, unused = shared.shape
    held = sources * both // 2
    return pl.pallas_call(
        expert_kernel,
        name="expert_both",
        cost_estimate=pl.CostEstimate(flops=18000000000, bytes_accessed=22000000, transcendentals=5000000),
        grid=(count // AT_ONCE,),
        out_shape=(
            jax.ShapeDtypeStruct(rows.shape, BF16),
            jax.ShapeDtypeStruct(shared.shape, BF16),
        ),
        in_specs=[
            pl.BlockSpec(rows.shape, lambda i: (0, 0, 0)),
            pl.BlockSpec((AT_ONCE, given, width), lambda i: (i, 0, 0)),
        ],
        out_specs=(
            pl.BlockSpec(rows.shape, lambda i: (0, 0, 0)),
            pl.BlockSpec((AT_ONCE, given, width), lambda i: (i, 0, 0)),
        ),
        scratch_shapes=[
            pltpu.VMEM((held, width), BF16),
            pltpu.VMEM((held, width), BF16),
            pltpu.VMEM((held, width), F32),
            pltpu.VMEM((held, width), F32),
        ],
        compiler_params=whole(),
    )(rows, shared)


def combine_kernel(
    place_ref,
    cot_ref,
    back_ref,
    pick_ref,
    gates_ref,
    mixed_ref,
    second_ref,
    att_ref,
    routes_ref,
    gain_ref,
    wr_ref,
    wo_ref,
    out_ref,
    grad_mixed_ref,
    heads_ref,
    keep_ref,
    pass_ref,
    y_s,
    dx_s,
    all_s,
):
    experts, both, width = back_ref.shape
    capacity = both // 2
    rows = cot_ref.shape[0]
    for s in range(experts):
        here = slice(capacity * s, capacity * s + capacity)
        y_s[here, :] = back_ref[s, :capacity, :]
        dx_s[here, :] = back_ref[s, capacity:, :]
    grad_out = cot_ref[...].astype(F32)
    mixed = mixed_ref[...]
    gates = [gates_ref[:, k : k + 1] for k in range(2)]
    picked = [dot(pick_ref[k], y_s[...]) for k in range(2)]
    out_ref[...] = (mixed + (gates[0] * picked[0] + gates[1] * picked[1])).astype(BF16)
    grad_gates = [jnp.sum(p * grad_out, axis=1, keepdims=True) for p in picked]
    mean = gates[0] * grad_gates[0] + gates[1] * grad_gates[1]
    grad_chosen = [gates[k] * (grad_gates[k] - mean) for k in range(2)]
    ids = lax.broadcasted_iota(jnp.int32, (rows, experts), 1)
    routes = routes_ref[...]
    grad_logits = jnp.where(routes[:, :1] == ids, grad_chosen[0], 0.0) + jnp.where(
        routes[:, 1:2] == ids, grad_chosen[1], 0.0
    )
    grad_second = dot(pick_ref[0], dx_s[...]) + dot(pick_ref[1], dx_s[...])
    grad_second = grad_second + dot(grad_logits, wr_ref[...].astype(F32), NT, HIGHEST)
    second = second_ref[...]
    grad_router = dot(grad_logits, second.astype(F32), TN, HIGHEST)
    scale = rms_scale(mixed)
    grad_gain = jnp.sum(grad_second * mixed * scale, axis=0, keepdims=True)
    grad_mixed = grad_out + norm_back(mixed, scale, gain_ref[...][None, :], grad_second)
    grad_mixed_ref[...] = grad_mixed
    grad_branch = grad_mixed.astype(BF16)
    grad_att = dot(grad_branch, wo_ref[...], NT).astype(BF16)
    heads = width // 64
    for h in range(heads):
        cols = slice(64 * h, 64 * h + 64)
        heads_ref[h] = jnp.concatenate([grad_att[:64, cols], grad_att[64:, cols]], axis=1)
    for h in range(heads, HEAD_SLOTS):
        heads_ref[h] = jnp.zeros_like(heads_ref[h])
    small = jnp.concatenate([grad_router, jnp.broadcast_to(grad_gain, (8, width))], axis=0)
    grad_wo = dot(att_ref[...], grad_branch, TN).astype(BF16)
    slots, each, unused = all_s.shape
    used = width // each
    for c in range(used):
        all_s[c] = grad_wo[each * c : each * c + each]
    for c in range(used, slots):
        all_s[c] = jnp.zeros_like(all_s[c])
    all_s[used, :16, :] = small.astype(BF16)
    core = place_ref[3]
    for c in range(slots // 2):
        keep_ref[c] = all_s[2 * c + core]
        pass_ref[c] = all_s[2 * c + 1 - core]


def combine(place, cotangent, back, picks, gates, mixed, second, attended, routes, gain_two, w_router, w_out):
    rows, width = cotangent.shape
    experts, both, unused = back.shape
    held = experts * both // 2
    return pl.pallas_call(
        combine_kernel,
        name="combine",
        cost_estimate=pl.CostEstimate(flops=1000000000, bytes_accessed=5000000, transcendentals=0),
        out_shape=(
            jax.ShapeDtypeStruct((rows, width), BF16),
            jax.ShapeDtypeStruct((rows, width), F32),
            jax.ShapeDtypeStruct((HEAD_SLOTS, rows // 2, 128), BF16),
            jax.ShapeDtypeStruct((HEAD_SLOTS // 2, 64, width), BF16),
            jax.ShapeDtypeStruct((HEAD_SLOTS // 2, 64, width), BF16),
        ),
        in_specs=[sspec()] + [vspec()] * 11,
        out_specs=(vspec(),) * 5,
        scratch_shapes=[
            pltpu.VMEM((held, width), BF16),
            pltpu.VMEM((held, width), BF16),
            pltpu.VMEM((HEAD_SLOTS, 64, width), BF16),
        ],
        compiler_params=whole(),
    )(
        place,
        cotangent,
        back,
        picks,
        gates,
        mixed,
        second,
        attended,
        routes,
        gain_two,
        w_router,
        w_out,
    )


def input_grad_kernel(tok_ref, gain_ref, grads_ref, wq_ref, wk_ref, wv_ref, mixed_ref, out_ref, dq_s, dk_s, dv_s):
    for j in range(dq_s.shape[1] // 128):
        cols = slice(128 * j, 128 * j + 128)
        one, two = grads_ref[2 * j], grads_ref[2 * j + 1]
        dq_s[:, cols] = jnp.concatenate([one[:128, :64], two[:128, :64]], axis=1)
        dk_s[:, cols] = jnp.concatenate([one[:128, 64:], two[:128, 64:]], axis=1)
        dv_s[:64, cols] = jnp.concatenate([one[128:, :64], two[128:, :64]], axis=1)
        dv_s[64:, cols] = jnp.concatenate([one[128:, 64:], two[128:, 64:]], axis=1)
    grad_normed = dot(dq_s[...], wq_ref[...], NT)
    grad_normed = grad_normed + dot(dk_s[...], wk_ref[...], NT)
    grad_normed = grad_normed + dot(dv_s[...], wv_ref[...], NT)
    inputs = tok_ref[...].astype(F32)
    out_ref[...] = mixed_ref[...] + norm_back(inputs, rms_scale(inputs), gain_ref[...][None, :], grad_normed)


def input_grad(tokens, gain_one, grads, w_query, w_key, w_value, grad_mixed):
    rows, width = tokens.shape
    return pl.pallas_call(
        input_grad_kernel,
        name="input_grad",
        cost_estimate=pl.CostEstimate(flops=500000000, bytes_accessed=5000000, transcendentals=0),
        out_shape=jax.ShapeDtypeStruct((rows, width), F32),
        in_specs=[vspec()] * 7,
        out_specs=vspec(),
        scratch_shapes=[pltpu.VMEM((rows, width), BF16)] * 3,
        compiler_params=whole(),
    )(tokens, gain_one, grads, w_query, w_key, w_value, grad_mixed)


def coordinates(index):
    context, expert = index // 8, index % 8
    return (context // 8 * 2 + expert % 2, expert // 2, context // 2 % 4, context % 2)


def device_at(x, y, z, core):
    return ((x // 2 * 4 + z) * 2 + core) * 8 + y * 2 + x % 2


def shifted(dim, by):
    pairs = []
    for index in range(128):
        place = list(coordinates(index))
        place[dim] = (place[dim] + by) % (2 if dim == 3 else 4)
        pairs.append((index, device_at(*place)))
    return pairs


AXES = ("context", "expert")


def direct_gather(block, dim):
    return jnp.stack([block] + [lax.ppermute(block, AXES, shifted(dim, -by)) for by in (1, 2, 3)])


def gather_last(filled, beside, work):
    half = filled.shape[0] // 2
    ahead = lax.ppermute(filled, AXES, shifted(1, -1))
    behind = lax.ppermute(filled, AXES, shifted(1, 1))
    ahead, behind, beside = lax.optimization_barrier((ahead, behind, beside))
    across = (
        lax.ppermute(ahead[:half], AXES, shifted(1, -1)),
        lax.ppermute(behind[half:], AXES, shifted(1, 1)),
    )
    across, done = lax.optimization_barrier((across, work(beside[0])))
    beside = (done,) + tuple(beside[1:])
    mine = (filled, ahead, behind) + across
    other = tuple(lax.ppermute(part, AXES, shifted(3, 1)) for part in mine)
    return mine + other, beside


def unpack_kernel(
    buckets,
    place_ref,
    wq_ref,
    wk_ref,
    wv_ref,
    *rest,
):
    parts, (dwq_ref, dwk_ref, dwv_ref, dwo_ref, bias_ref, small_ref, router_ref, gain_grad_ref) = rest[:10], rest[10:18]
    all_s, sems = rest[18:]
    expert = pl.program_id(0)

    @pl.when(expert == 0)
    def _():
        copies = []
        for core in range(2):
            for i in range(5):
                part = parts[5 * core + i]
                half = all_s.shape[2] // 2
                place = (
                    all_s.at[core, (0, 1, 3)[i]]
                    if i < 3
                    else all_s.at[core, 2, pl.ds(half * (i - 3), half)]
                )
                copies.append(pltpu.make_async_copy(part, place, sems.at[5 * core + i]))
        for copy in copies:
            copy.start()
        for copy in copies:
            copy.wait()

    my_x, my_y, my_z, my_core = (place_ref[i] for i in range(4))
    each = dwq_ref.shape[0]
    half = each // 2
    width = dwq_ref.shape[1]
    rel_y = lax.rem(expert // 2 - my_y + 4, 4)

    def rel(context):
        x = context // 8 * 2 + lax.rem(expert, 2)
        return (
            jnp.where(my_core == context % 2, 0, 1),
            rel_y,
            lax.rem(x - my_x + 4, 4),
            lax.rem(context // 2 % 4 - my_z + 4, 4),
        )

    at = each + half
    bias = []
    for j in range(width // 128):
        cols = slice(128 * j, 128 * j + 128)
        one, two = all_s[rel(2 * j)], all_s[rel(2 * j + 1)]
        left = jnp.concatenate([one[:at, :64], two[:at, :64]], axis=1).astype(F32)
        right = jnp.concatenate([one[:at, 64:], two[:at, 64:]], axis=1).astype(F32)
        dwq_ref[:, cols] = left[:each]
        dwk_ref[:, cols] = right[:each]
        dwv_ref[:half, cols] = left[each:]
        dwv_ref[half:, cols] = right[each:]
        one, two = one[at:].astype(F32), two[at:].astype(F32)
        bias += [one[:1], two[:1]]
        for i, block in enumerate((one, two)):
            for k in range(width // 128):
                dwo_ref[2 * j + i, :, 128 * k : 128 * k + 128] = block[16 + 8 * k : 24 + 8 * k]
    bias_ref[...] = jnp.concatenate(bias, axis=0)[:, :buckets]
    block = all_s[rel(width // 64)].astype(F32)
    small = jnp.concatenate(
        [block[at + 16 + 8 * k : at + 24 + 8 * k] for k in range(width // 128)], axis=1
    )

    @pl.when(expert == 0)
    def _():
        router_ref[...] = small

    @pl.when(expert == 1)
    def _():
        small_ref[...] = small

    prod = (
        dwq_ref[...] * wq_ref[...].astype(F32)
        + dwk_ref[...] * wk_ref[...].astype(F32)
        + dwv_ref[...] * wv_ref[...].astype(F32)
    )
    lanes = prod[:, :128]
    for j in range(1, width // 128):
        lanes = lanes + prod[:, 128 * j : 128 * j + 128]
    gain_grad_ref[...] = jnp.broadcast_to(jnp.sum(lanes.T, axis=0, keepdims=True), (8, each))


def unpack(place, parts, w_query, w_key, w_value, heads, buckets, experts):
    width = w_query.shape[0]
    each = width // experts
    held = parts[0].shape[2]
    rows = pl.BlockSpec((each, width), lambda i: (i, 0))
    return pl.pallas_call(
        lambda *refs: unpack_kernel(buckets, *refs),
        name="unpack",
        cost_estimate=pl.CostEstimate(flops=1000000000, bytes_accessed=24000000, transcendentals=0),
        grid=(experts,),
        out_shape=(
            jax.ShapeDtypeStruct((width, width), F32),
            jax.ShapeDtypeStruct((width, width), F32),
            jax.ShapeDtypeStruct((width, width), F32),
            jax.ShapeDtypeStruct((heads, experts, 8, width), F32),
            jax.ShapeDtypeStruct((heads, buckets), F32),
            jax.ShapeDtypeStruct((8, width), F32),
            jax.ShapeDtypeStruct((8, width), F32),
            jax.ShapeDtypeStruct((experts, 8, each), F32),
        ),
        in_specs=[sspec(), rows, rows, rows] + [pl.BlockSpec(memory_space=pl.ANY)] * 10,
        out_specs=(
            rows,
            rows,
            rows,
            pl.BlockSpec((heads, None, 8, width), lambda i: (0, i, 0, 0)),
            pl.BlockSpec((heads, buckets), lambda i: (0, 0)),
            pl.BlockSpec((8, width), lambda i: (0, 0)),
            pl.BlockSpec((8, width), lambda i: (0, 0)),
            pl.BlockSpec((None, 8, each), lambda i: (i, 0, 0)),
        ),
        scratch_shapes=[
            pltpu.VMEM((2, 4, 4, 4, held, 128), BF16),
            pltpu.SemaphoreType.DMA((10,)),
        ],
        compiler_params=whole(),
    )(place, w_query, w_key, w_value, *parts)


def add_kernel(in_ref, out_ref):
    total = in_ref[0].astype(F32)
    for i in range(1, in_ref.shape[0]):
        total = total + in_ref[i].astype(F32)
    out_ref[...] = total.astype(BF16)


def add_up(received):
    return pl.pallas_call(
        add_kernel,
        name="add_up",
        out_shape=jax.ShapeDtypeStruct(received.shape[1:], BF16),
        in_specs=[vspec()],
        out_specs=vspec(),
        compiler_params=whole(),
    )(received)


def shards(
    tokens,
    gain_one,
    w_query,
    w_key,
    w_value,
    w_out,
    rel_table,
    gain_two,
    w_router,
    expert_in,
    expert_out,
    routes,
    cotangent,
):
    width = tokens.shape[2]
    heads, buckets = rel_table.shape
    experts = lax.axis_size("expert")
    inputs, grad_out, routes_here = tokens[0], cotangent[0], routes[0]
    context = lax.axis_index("context")
    head = jnp.minimum(context, heads - 1).astype(jnp.int32).reshape(1)

    own_weights = jnp.concatenate([expert_in[0].T, expert_out[0].T], axis=0)
    shared = lax.all_gather(own_weights, "context", axis=0, tiled=False)
    normed, packed = project(inputs, gain_one, w_query, w_key, w_value)
    qkv = lax.all_to_all(packed, "context", split_axis=0, concat_axis=0, tiled=True)
    expert = lax.axis_index("expert")
    place = jnp.stack(coordinates(context * experts + expert)).astype(jnp.int32)
    normed, qkv = lax.optimization_barrier((normed, qkv))
    normed_two = jnp.stack([normed, lax.ppermute(normed, AXES, shifted(0, 2))])

    out_heads, keep, lse = attend(head, rel_table, qkv)
    out_rows = lax.all_to_all(out_heads, "context", split_axis=0, concat_axis=0, tiled=True)
    send, attended, mixed, second, picks, gates = dispatch(
        inputs, grad_out, out_rows, w_out, gain_two, w_router, routes_here, experts
    )
    received = lax.all_to_all(send, "expert", split_axis=0, concat_axis=0, tiled=True)
    normed_two, received, shared = lax.optimization_barrier((normed_two, received, shared))
    normed_mine = direct_gather(normed_two, 2)
    back, weight_grads = expert_both(received, shared)
    returned = lax.all_to_all(back, "expert", split_axis=0, concat_axis=0, tiled=True)
    normed_mine, returned = lax.optimization_barrier((normed_mine, returned))
    normed_other = lax.ppermute(normed_mine, AXES, shifted(3, 1))
    own_grads = lax.psum_scatter(weight_grads, "context", scatter_dimension=0, tiled=False)
    block_out, grad_mixed, grad_heads, keep_sums, pass_sums = combine(
        place, grad_out, returned, picks, gates, mixed, second, attended, routes_here, gain_two, w_router, w_out
    )
    other_sums = lax.ppermute(pass_sums, AXES, shifted(3, 1))
    sums = (keep_sums.astype(F32) + other_sums.astype(F32)).astype(BF16)
    grad_here = lax.all_to_all(grad_heads, "context", split_axis=0, concat_axis=0, tiled=True)
    same_core = [[2 * i + core for i in range(8)] for core in range(2)]
    sums, grad_here = lax.optimization_barrier((sums, grad_here))
    sums = lax.all_to_all(
        sums, "context", split_axis=0, concat_axis=0, axis_index_groups=same_core, tiled=True
    )

    dqkv, bias = attend_back(head, rel_table, qkv, grad_here, keep, lse)
    terms = head_grads(place, dqkv, normed_mine, normed_other, bias, sums, experts)
    terms = lax.all_to_all(terms, "expert", split_axis=0, concat_axis=0, tiled=True)
    filled, dqkv = lax.optimization_barrier((direct_gather(direct_gather(add_up(terms), 2), 0), dqkv))
    grads = lax.all_to_all(dqkv, "context", split_axis=0, concat_axis=0, tiled=True)
    own_grads = own_grads.astype(F32)
    hidden = own_grads.shape[0] // 2
    parts, (grad_tokens, grad_in, grad_back) = gather_last(
        filled,
        (grads, own_grads[:hidden], own_grads[hidden:]),
        lambda here: input_grad(inputs, gain_one, here, w_query, w_key, w_value, grad_mixed),
    )

    dwq, dwk, dwv, dwo, bias, small, router, gain_grad = unpack(
        place, parts, w_query, w_key, w_value, heads, buckets, experts
    )
    return (
        block_out[None],
        grad_tokens[None],
        gain_grad[:, 0, :].reshape(width) / gain_one,
        dwq,
        dwk,
        dwv,
        dwo.reshape(width, width),
        bias,
        small[0],
        router.T,
        grad_in.T[None],
        grad_back.T[None],
    )


def solution(mesh):
    return jax.shard_map(
        shards,
        mesh=mesh,
        in_specs=(
            P("expert", "context", None),
            P(),
            P(),
            P(),
            P(),
            P(),
            P(),
            P(),
            P(),
            P("expert", None, "context"),
            P("expert", None, "context"),
            P("expert", "context", None),
            P("expert", "context", None),
        ),
        out_specs=(
            P("expert", "context", None),
            P("expert", "context", None),
            P(),
            P(),
            P(),
            P(),
            P(),
            P(),
            P(),
            P(),
            P("expert", None, "context"),
            P("expert", None, "context"),
        ),
        check_vma=False,
    )
```
